32 devices in a mesh: grp: 2 (over x), tm: 16 (over z, y, core).
Axes of the slice: x: 2, y: 2, z: 4, core: 2. Of those that a mesh axis runs over, the one named last changes fastest.
Arguments:
- right_sides: float32 [64, 4, 128], P(('grp', 'tm')), parts along dimension 0, may hold values from -6 to 6
- obs_var: float32 [64, 128], P(('grp', 'tm')), parts along dimension 0, may hold values from 0.25 to 1
- footprint: bfloat16 [512, 8, 128, 128], P(('grp', 'tm')), parts along dimension 0, may hold values from -0.5 to 0.5
- tile_block: int32 [512, 8], P(('grp', 'tm')), parts along dimension 0, may hold values from 0 to 1
- tile_place: int32 [512, 8], P(('grp', 'tm')), parts along dimension 0, may hold values from 0 to 1023
- time_cov: float32 [128, 128], replicated, as said below
- lat_cov: float32 [128, 128], replicated
- lon_cov: float32 [128, 128], replicated
Outputs:
- solution: float32 [64, 4, 128], P(('grp', 'tm')), parts along dimension 0
- flux_update: float32 [256, 128, 4, 128], P(('grp', 'tm')), parts along dimension 0
The draws below stay inside these ranges and needn't reach their ends.
There are 2 independent parts, one for each index of `grp`. The reference program is written for one: setup_inputs(seed, part) draws one part's arguments, and reference() takes and returns one part's arrays. A program takes and returns all parts, laid end to end along the dimension named above; an argument that names none is the same for every part. Nothing has to cross between parts.
Inputs may be any that keep to these rules, and one draw needn't show every extreme that they name: time_cov, lat_cov and lon_cov are symmetric positive definite with positive entries.
All inputs are finite; a program needn't handle non-finite values.
Results may differ from the reference program's by a relative error of at most 0.0074.
Values may be sent and summed in bfloat16 or wider, within the bound.
No kernel may reach another device: no remote copies, remote signals or barrier semaphores. Data moves between devices by JAX's collectives and lax.ppermute only.
A program may use at most 64 MiB of HBM per device.

```python
import math
import jax
import jax.numpy as jnp
import numpy as np
from jax import lax

NT = 128
LAT = 128
LON = 128
BLOCK_OBS = 128
SAMPLES = 4
BLOCKS_DEV = 2
TILES_DEV = 128
ITERS = 2
STEPS_DEV = 8
SLOTS = 8
BLOCKS = 32
N_TM = 16


def covariance(key, extent, length, lowest, highest):
    scales = jax.random.uniform(key, (extent,), jnp.float32, lowest, highest)
    places = jnp.arange(extent, dtype=jnp.float32)
    kernel = jnp.exp(-jnp.abs(places[:, None] - places[None, :]) / length)
    return kernel * (scales[:, None] * scales[None, :]) / length


def draw_time_cov(key, part):
    key = jax.random.fold_in(key, 11)
    return covariance(key, NT, 16.0, 0.6, 1.4)


def draw_lat_cov(key, part):
    key = jax.random.fold_in(key, 23)
    return covariance(key, LAT, LAT / 16.0, 0.6, 1.4)


def draw_lon_cov(key, part):
    key = jax.random.fold_in(key, 37)
    return covariance(key, LON, LON / 16.0, 0.6, 1.4)


def touch_ends(array, stream_key, low, largest):
    shape = array.shape
    index_at = [jax.random.randint(jax.random.fold_in(stream_key, axis), (), 0, shape[axis]) for axis in range(len(shape))]
    array = array.at[tuple(index_at)].set(low)
    longest = shape.index(max(shape))
    index_at[longest] = (index_at[longest] + 1) % shape[longest]
    return array.at[tuple(index_at)].set(largest)


def block_levels(key, shape, pieces, least, high):
    loudness = 1.0
    for axis_at, shards_of in pieces:
        steps = jax.random.uniform(jax.random.fold_in(jax.random.fold_in(key, 6), axis_at), (shards_of,), jnp.float32, least / len(pieces), high / len(pieces))
        loudness = loudness * jnp.repeat(jnp.exp(steps), shape[axis_at] // shards_of).reshape((-1,) + (1,) * (len(shape) - 1 - axis_at))
    return loudness


def rank_bounds(number_of, lean):
    portions = [(1 << 20) // math.isqrt(rank ** lean) + 1 for rank in range(1, number_of + 1)]
    width = 1 + sum(portions) // (1 << 30)
    return np.cumsum(np.array([max(1, weight // width) for weight in portions]))


def ranked_ids(stream_key, shape, number_of, skew):
    table = rank_bounds(number_of, skew)
    ticket = jax.random.randint(jax.random.fold_in(stream_key, 1), shape, 0, int(table[number_of - 1]))
    rank = jnp.searchsorted(jnp.asarray(table, jnp.int32), ticket, side="right")
    return jax.random.permutation(jax.random.fold_in(stream_key, 2), number_of)[rank].astype(jnp.int32)


def normal_values(rng, dims, scale, limit, cuts=(), kind=jnp.bfloat16):
    result = jax.random.normal(rng, dims, jnp.float32) * scale
    if len(cuts) > 0:
        result = block_levels(rng, dims, cuts, -0.22, 0.18) * result
    return jnp.clip(result, min=-limit, max=limit).astype(kind)


def setup_inputs(seed: int = 0, part: int = 0) -> dict:
    key_of = jax.random.split(jax.random.key(seed), 9)
    part_keys = jax.random.split(jax.random.fold_in(key_of[8], part), 9)
    return {
        "right_sides": normal_values(part_keys[0], (BLOCKS, SAMPLES, BLOCK_OBS), 1.0, 6.0, ((0, 16),), jnp.float32),
        "obs_var": jnp.clip(jnp.exp(math.log(1.0) - 1.3862944 * jax.random.uniform(part_keys[1], (BLOCKS, BLOCK_OBS), jnp.float32) ** block_levels(part_keys[1], (BLOCKS, BLOCK_OBS), ((0, 16),), -0.2, 0.2)), 0.25, 1.0),
        "footprint": normal_values(part_keys[2], (N_TM * N_TM, SLOTS, BLOCK_OBS, LON), (LON * TILES_DEV // (64 * BLOCKS_DEV)) ** -0.5, 0.5, ((0, 16),)),
        "tile_block": touch_ends(ranked_ids(part_keys[3], (N_TM * N_TM, SLOTS), BLOCKS_DEV, 2), jax.random.fold_in(part_keys[3], 3), 0, BLOCKS_DEV - 1).astype(jnp.int32),
        "tile_place": touch_ends(jax.random.randint(part_keys[4], (N_TM * N_TM, SLOTS), 0, STEPS_DEV * LAT), jax.random.fold_in(part_keys[4], 1), 0, (STEPS_DEV * LAT) - 1).astype(jnp.int32),
        "time_cov": draw_time_cov(jax.random.fold_in(key_of[8], 71), part),
        "lat_cov": draw_lat_cov(jax.random.fold_in(key_of[8], 71), part),
        "lon_cov": draw_lon_cov(jax.random.fold_in(key_of[8], 71), part),
    }


precise = lax.Precision.HIGHEST

def spread(blocks_bf, footprint, tile_block, tile_place):
    owner_base = (jnp.arange(N_TM, dtype=jnp.int32) * BLOCKS_DEV)[:, None]
    tiles = footprint.reshape(N_TM, N_TM, SLOTS, BLOCK_OBS, LON)
    block_ids = tile_block.reshape(N_TM, N_TM, SLOTS)
    places = tile_place.reshape(N_TM, N_TM, SLOTS)

    def per_device(inputs):
        tile_set, block_set, place_set = inputs
        chosen = jnp.take(blocks_bf, (owner_base + block_set).astype(jnp.int32), axis=0).astype(jnp.float32)
        contrib = jnp.einsum('ocks,ocsl->ockl', chosen, tile_set.astype(jnp.float32), precision=precise)
        return jax.ops.segment_sum(contrib.reshape(N_TM * SLOTS, SAMPLES, LON), place_set.reshape(-1), num_segments=STEPS_DEV * LAT)
    spread_rows = lax.map(per_device, (tiles, block_ids, places))
    return spread_rows.reshape(NT, LAT, SAMPLES, LON)

def collect(field_bf, footprint, tile_block, tile_place):
    flat_rows = field_bf.reshape(N_TM, STEPS_DEV * LAT, SAMPLES, LON)
    tiles = footprint.reshape(N_TM, N_TM, SLOTS, BLOCK_OBS, LON)
    block_ids = tile_block.reshape(N_TM, N_TM, SLOTS)
    places = tile_place.reshape(N_TM, N_TM, SLOTS)
    block_range = jnp.arange(BLOCKS_DEV, dtype=jnp.int32)

    def per_device(running, inputs):
        row_set, tile_set, block_set, place_set = inputs
        picked = jnp.take(row_set, place_set, axis=0).astype(jnp.float32)
        partial_value = jnp.einsum('ockl,ocsl->ocks', picked, tile_set.astype(jnp.float32), precision=precise)
        selector = (block_set[:, :, None] == block_range).astype(jnp.float32)
        block_term = jnp.einsum('ocb,ocks->obks', selector, partial_value, precision=precise)
        return (running + block_term.reshape(BLOCKS, SAMPLES, BLOCK_OBS), None)
    start_sum = jnp.zeros((BLOCKS, SAMPLES, BLOCK_OBS), jnp.float32)
    running, _ = lax.scan(per_device, start_sum, (flat_rows, tiles, block_ids, places))
    return running

def apply_prior(flux_field, time_cov, lat_cov, lon_cov):
    flux_field = jnp.einsum('ab,tbkl->takl', lat_cov, flux_field, precision=precise)
    flux_field = jnp.einsum('tbkl,lm->tbkm', flux_field, lon_cov, precision=precise)
    return jnp.einsum('st,tbkl->sbkl', time_cov, flux_field, precision=precise)

def inner_gram(left, right):
    return jnp.einsum('nks,njs->kj', left, right, precision=precise)

def solve_spd(matrix, target):
    factor = jnp.linalg.cholesky(matrix)
    halfway = lax.linalg.triangular_solve(factor, target, left_side=True, lower=True)
    return lax.linalg.triangular_solve(factor, halfway, left_side=True, lower=True, transpose_a=True)

def combine(vectors, weights):
    return jnp.einsum('nks,kj->njs', vectors, weights, precision=precise)

def reference(right_sides, obs_var, footprint, tile_block, tile_place, time_cov, lat_cov, lon_cov):

    def operate(direction):
        flux_field = apply_prior(spread(direction.astype(jnp.bfloat16), footprint, tile_block, tile_place), time_cov, lat_cov, lon_cov)
        return collect(flux_field.astype(jnp.bfloat16), footprint, tile_block, tile_place) + obs_var[:, None, :] * direction
    solution = jnp.zeros_like(right_sides)
    residual = right_sides
    direction = right_sides
    norm_now = inner_gram(residual, residual)
    for step in range(ITERS):
        image = operate(direction)
        step_size = solve_spd(inner_gram(direction, image), norm_now)
        solution = solution + combine(direction, step_size)
        residual = residual - combine(image, step_size)
        norm_next = inner_gram(residual, residual)
        mix_ratio = solve_spd(norm_now, norm_next)
        direction = residual + combine(direction, mix_ratio)
        norm_now = norm_next
    flux_update = apply_prior(spread(solution.astype(jnp.bfloat16), footprint, tile_block, tile_place), time_cov, lat_cov, lon_cov)
    return (solution, flux_update)
```

```python
import jax
import jax.numpy as jnp
from jax import lax
from jax.sharding import PartitionSpec as P

LAT = 128
LON = 128
BLOCK_OBS = 128
SAMPLES = 4
ITERS = 2


precise = lax.Precision.HIGHEST
high = lax.Precision.HIGH


def solve_spd(matrix, target):
    factor = jnp.linalg.cholesky(matrix)
    halfway = lax.linalg.triangular_solve(factor, target, left_side=True, lower=True)
    return lax.linalg.triangular_solve(
        factor, halfway, left_side=True, lower=True, transpose_a=True
    )


def combine(vectors, weights):
    return jnp.einsum("nks,kj->njs", vectors, weights, precision=precise)


def gram(left, right):
    return jnp.einsum("nks,njs->kj", left, right, precision=precise)


def to_all(array):
    devices = lax.axis_size("tm")
    copies = jnp.broadcast_to(array[None], (devices,) + array.shape)
    return lax.all_to_all(copies, "tm", split_axis=0, concat_axis=0, tiled=True)


def local(right_sides, obs_var, footprint, tile_block, tile_place, time_cov, lat_cov, lon_cov):
    devices = lax.axis_size("tm")
    me = lax.axis_index("tm")
    owned = right_sides.shape[0]
    blocks = devices * owned
    steps_here = time_cov.shape[0] // devices
    slots = tile_block.shape[1]
    tiles = devices * slots
    rows_here = steps_here * LAT
    owner_base = (jnp.arange(devices, dtype=jnp.int32) * owned)[:, None]
    requests = owner_base + tile_block

    packed = jnp.concatenate(
        [
            right_sides.reshape(-1, 128),
            obs_var.reshape(-1, 128),
            tile_place.astype(jnp.float32).reshape(-1, 128),
        ]
    )
    everyone = to_all(packed)
    at = owned * SAMPLES
    rhs = everyone[:, :at].reshape(blocks, SAMPLES, BLOCK_OBS)
    variance = everyone[:, at : at + owned].reshape(blocks, BLOCK_OBS)
    places = everyone[:, at + owned :].reshape(devices, tiles).astype(jnp.int32)
    times = (places // LAT + steps_here * jnp.arange(devices, dtype=jnp.int32)[:, None]).reshape(-1)
    rows = (places % LAT).reshape(-1)
    time_hot = (jnp.arange(time_cov.shape[0])[:, None] == times[None, :]).astype(jnp.float32)
    row_hot = (jnp.arange(LAT)[:, None] == rows[None, :]).astype(jnp.float32)
    my_times = lax.dynamic_slice_in_dim(time_cov, me * steps_here, steps_here, 0)
    time_part = jnp.dot(my_times, time_hot, precision=precise)
    row_part = jnp.dot(lat_cov, row_hot, precision=precise)
    dense = (time_part[:, None, :] * row_part[None, :, :]).astype(jnp.bfloat16)
    dense = dense.reshape(rows_here, devices * tiles)
    mine = jnp.take(dense, tile_place.reshape(-1), axis=0)

    def spread(vectors):
        chosen = jnp.take(vectors.astype(jnp.bfloat16), requests, axis=0)
        contrib = jnp.einsum(
            "ocks,ocsl->ockl", chosen, footprint, preferred_element_type=jnp.float32
        )
        contrib = contrib.astype(jnp.bfloat16).reshape(tiles, SAMPLES * LON)
        return lax.all_gather(contrib, "tm", axis=0, tiled=True)

    def collect(gathered):
        field = jnp.dot(mine, gathered, preferred_element_type=jnp.float32)
        field = jnp.dot(field.reshape(-1, LON), lon_cov, precision=precise)
        picked = field.astype(jnp.bfloat16).reshape(devices, slots, SAMPLES, LON)
        partial = jnp.einsum(
            "ockl,ocsl->ocks", picked, footprint, preferred_element_type=jnp.float32
        )
        block_range = jnp.arange(owned, dtype=jnp.int32)
        selector = (tile_block[:, :, None] == block_range).astype(jnp.float32)
        summed = jnp.einsum("ocb,ocks->obks", selector, partial, precision=precise)
        terms = lax.all_to_all(
            summed.reshape(devices, owned * SAMPLES, BLOCK_OBS), "tm", 0, 0, tiled=True
        )
        return to_all(terms.sum(0)).reshape(blocks, SAMPLES, BLOCK_OBS)

    solution = jnp.zeros_like(rhs)
    residual = rhs
    direction = rhs
    norm_now = gram(rhs, rhs)
    gathers, sizes = [], []
    for step in range(ITERS):
        gathered = spread(direction)
        image = collect(gathered) + variance[:, None, :] * direction
        step_size = solve_spd(gram(direction, image), norm_now)
        gathers.append(gathered)
        sizes.append(step_size)
        solution = solution + combine(direction, step_size)
        if step + 1 == ITERS:
            break
        residual = residual - combine(image, step_size)
        norm_next = gram(residual, residual)
        mix_ratio = solve_spd(norm_now, norm_next)
        direction = residual + combine(direction, mix_ratio)
        norm_now = norm_next

    def mix(gathered, size):
        whole = gathered.astype(jnp.float32).reshape(-1, SAMPLES, LON)
        return jnp.einsum("tkl,kj->tjl", whole, size, precision=precise)

    def apply_dense(gathered):
        return jnp.dot(dense, gathered, preferred_element_type=jnp.float32)

    if rows_here < devices * tiles // 4:
        flux = sum(mix(apply_dense(g), size) for g, size in zip(gathers, sizes))
    else:
        total = sum(mix(g, size) for g, size in zip(gathers, sizes))
        flux = apply_dense(total.astype(jnp.bfloat16).reshape(-1, SAMPLES * LON))
    flux = jnp.dot(flux.reshape(-1, LON), lon_cov, precision=precise)
    mine_now = lax.dynamic_slice_in_dim(solution, me * owned, owned, 0)
    return (mine_now, flux.reshape(steps_here, LAT, SAMPLES, LON))


def solution(mesh):
    in_specs = (
        P(("grp", "tm"), None, None),
        P(("grp", "tm"), None),
        P(("grp", "tm"), None, None, None),
        P(("grp", "tm"), None),
        P(("grp", "tm"), None),
        P(),
        P(),
        P(),
    )
    out_specs = (P(("grp", "tm"), None, None), P(("grp", "tm"), None, None, None))
    return jax.shard_map(local, mesh=mesh, in_specs=in_specs, out_specs=out_specs, check_vma=False)
```

```python
import functools

import jax
import jax.numpy as jnp
from jax import lax
from jax.experimental import pallas as pl
from jax.experimental.pallas import tpu as pltpu
from jax.sharding import PartitionSpec as P

LAT = 128
LON = 128
BLOCK_OBS = 128
SAMPLES = 4
ITERS = 2


precise = lax.Precision.HIGHEST


def solve_spd(matrix, target):
    factor = jnp.linalg.cholesky(matrix)
    halfway = lax.linalg.triangular_solve(factor, target, left_side=True, lower=True)
    return lax.linalg.triangular_solve(
        factor, halfway, left_side=True, lower=True, transpose_a=True
    )


def combine(vectors, weights):
    return jnp.einsum("nks,kj->njs", vectors, weights, precision=precise)


def gram(left, right):
    return jnp.einsum("nks,njs->kj", left, right, precision=precise)


def to_all(array):
    devices = lax.axis_size("tm")
    copies = jnp.broadcast_to(array[None], (devices,) + array.shape)
    return lax.all_to_all(copies, "tm", split_axis=0, concat_axis=0, tiled=True)


def by_gather(
    right_sides, obs_var, footprint, tile_block, tile_place, time_cov, lat_cov, lon_cov
):
    devices = lax.axis_size("tm")
    me = lax.axis_index("tm")
    owned = right_sides.shape[0]
    blocks = devices * owned
    steps_here = time_cov.shape[0] // devices
    slots = tile_block.shape[1]
    tiles = devices * slots
    rows_here = steps_here * LAT
    owner_base = (jnp.arange(devices, dtype=jnp.int32) * owned)[:, None]
    requests = owner_base + tile_block

    packed = jnp.concatenate(
        [
            right_sides.reshape(-1, 128),
            obs_var.reshape(-1, 128),
            tile_place.astype(jnp.float32).reshape(-1, 128),
        ]
    )
    everyone = to_all(packed)
    at = owned * SAMPLES
    rhs = everyone[:, :at].reshape(blocks, SAMPLES, BLOCK_OBS)
    variance = everyone[:, at : at + owned].reshape(blocks, BLOCK_OBS)
    places = everyone[:, at + owned :].reshape(devices, tiles).astype(jnp.int32)
    times = (places // LAT + steps_here * jnp.arange(devices, dtype=jnp.int32)[:, None]).reshape(-1)
    rows = (places % LAT).reshape(-1)
    time_hot = (jnp.arange(time_cov.shape[0])[:, None] == times[None, :]).astype(jnp.float32)
    row_hot = (jnp.arange(LAT)[:, None] == rows[None, :]).astype(jnp.float32)
    my_times = lax.dynamic_slice_in_dim(time_cov, me * steps_here, steps_here, 0)
    time_part = jnp.dot(my_times, time_hot, precision=precise)
    row_part = jnp.dot(lat_cov, row_hot, precision=precise)
    dense = (time_part[:, None, :] * row_part[None, :, :]).astype(jnp.bfloat16)
    dense = dense.reshape(rows_here, devices * tiles)
    mine = jnp.take(dense, tile_place.reshape(-1), axis=0)

    def spread(vectors):
        chosen = jnp.take(vectors.astype(jnp.bfloat16), requests, axis=0)
        contrib = jnp.einsum(
            "ocks,ocsl->ockl", chosen, footprint, preferred_element_type=jnp.float32
        )
        contrib = contrib.astype(jnp.bfloat16).reshape(tiles, SAMPLES * LON)
        return lax.all_gather(contrib, "tm", axis=0, tiled=True)

    def collect(gathered):
        field = jnp.dot(mine, gathered, preferred_element_type=jnp.float32)
        field = jnp.dot(field.reshape(-1, LON), lon_cov, precision=precise)
        picked = field.astype(jnp.bfloat16).reshape(devices, slots, SAMPLES, LON)
        partial = jnp.einsum(
            "ockl,ocsl->ocks", picked, footprint, preferred_element_type=jnp.float32
        )
        block_range = jnp.arange(owned, dtype=jnp.int32)
        selector = (tile_block[:, :, None] == block_range).astype(jnp.float32)
        summed = jnp.einsum("ocb,ocks->obks", selector, partial, precision=precise)
        terms = lax.all_to_all(
            summed.reshape(devices, owned * SAMPLES, BLOCK_OBS), "tm", 0, 0, tiled=True
        )
        return to_all(terms.sum(0)).reshape(blocks, SAMPLES, BLOCK_OBS)

    solution = jnp.zeros_like(rhs)
    residual = rhs
    direction = rhs
    norm_now = gram(rhs, rhs)
    gathers, sizes = [], []
    for step in range(ITERS):
        gathered = spread(direction)
        image = collect(gathered) + variance[:, None, :] * direction
        step_size = solve_spd(gram(direction, image), norm_now)
        gathers.append(gathered)
        sizes.append(step_size)
        solution = solution + combine(direction, step_size)
        if step + 1 == ITERS:
            break
        residual = residual - combine(image, step_size)
        norm_next = gram(residual, residual)
        mix_ratio = solve_spd(norm_now, norm_next)
        direction = residual + combine(direction, mix_ratio)
        norm_now = norm_next

    def mix(gathered, size):
        whole = gathered.astype(jnp.float32).reshape(-1, SAMPLES, LON)
        return jnp.einsum("tkl,kj->tjl", whole, size, precision=precise)

    def apply_dense(gathered):
        return jnp.dot(dense, gathered, preferred_element_type=jnp.float32)

    if rows_here < devices * tiles // 4:
        flux = sum(mix(apply_dense(g), size) for g, size in zip(gathers, sizes))
    else:
        total = sum(mix(g, size) for g, size in zip(gathers, sizes))
        flux = apply_dense(total.astype(jnp.bfloat16).reshape(-1, SAMPLES * LON))
    flux = jnp.dot(flux.reshape(-1, LON), lon_cov, precision=precise)
    mine_now = lax.dynamic_slice_in_dim(solution, me * owned, owned, 0)
    return (mine_now, flux.reshape(steps_here, LAT, SAMPLES, LON))


def rolled(x, shift):
    return x if shift == 0 else pltpu.roll(x, 8 - 2 * shift, x.ndim - 2)


def row_gram(left, right):
    entry = [[None] * SAMPLES for _ in range(SAMPLES)]
    for shift in range(SAMPLES):
        product = jnp.sum(left * rolled(right, shift), axis=0)
        total = jnp.broadcast_to(jnp.sum(product, axis=1, keepdims=True), product.shape)
        for k in range(SAMPLES):
            pair = total[2 * k : 2 * k + 1] + total[2 * k + 1 : 2 * k + 2]
            entry[k][(k + shift) % SAMPLES] = pair
    return entry


def row_solve(matrix, target):
    size = range(SAMPLES)
    sym = [[0.5 * (matrix[i][j] + matrix[j][i]) for j in size] for i in size]
    low = [[None] * SAMPLES for _ in size]
    scaled = [[None] * SAMPLES for _ in size]
    inverse = []
    for j in size:
        pivot = sym[j][j]
        for p in range(j):
            pivot = pivot - low[j][p] * scaled[j][p]
        inverse.append(1.0 / pivot)
        for i in range(j + 1, SAMPLES):
            value = sym[i][j]
            for p in range(j):
                value = value - scaled[i][p] * low[j][p]
            scaled[i][j] = value
            low[i][j] = value * inverse[j]
    out = [[None] * SAMPLES for _ in size]
    for c in size:
        part = []
        for i in size:
            value = target[i][c]
            for p in range(i):
                value = value - low[i][p] * part[p]
            part.append(value)
        for i in reversed(size):
            value = part[i] * inverse[i]
            for p in range(i + 1, SAMPLES):
                value = value - low[p][i] * out[p][c]
            out[i][c] = value
    return out


def row_weights(weights):
    sample = lax.broadcasted_iota(jnp.int32, (8, 128), 0) // 2
    result = []
    for shift in range(SAMPLES):
        rows = jnp.broadcast_to(weights[shift][0], (8, 128))
        for j in range(1, SAMPLES):
            rows = jnp.where(sample == j, weights[(j + shift) % SAMPLES][j], rows)
        result.append(rows)
    return result


def row_combine(x, per_shift):
    total = 0.0
    for shift in range(SAMPLES):
        total = total + rolled(x, shift) * per_shift[shift]
    return total


def spread_tiles(step, owners, vectors, footprint, products, split):
    slots = footprint.shape[1]
    for q in range(owners):
        owner = step * owners + q
        rows = vectors[owner]
        lhs = rows.astype(jnp.bfloat16)
        if split:
            upper = lhs.astype(jnp.float32)
            lhs = jnp.concatenate([upper, rows - upper], axis=0).astype(jnp.bfloat16)
        for c in range(slots):
            r = jnp.dot(lhs, footprint[q, c], preferred_element_type=jnp.float32)
            products[owner * slots + c] = r[:8] + r[8:] if split else r


def spread_end(products, second, lon, by_column, by_tile):
    width = by_column.shape[1]
    chunks = LON // width
    for k in range(SAMPLES):
        chosen = jnp.where(second, products[:, 2 * k + 1, :], products[:, 2 * k, :])
        mixed = jnp.dot(
            chosen, lon[...], precision=precise, preferred_element_type=jnp.float32
        )
        by_tile[:, k * LON : (k + 1) * LON] = mixed.astype(jnp.bfloat16)
        turned = mixed.T.astype(jnp.bfloat16)
        by_column[k * chunks : (k + 1) * chunks] = turned.reshape(chunks, width, LON)


def first_body(owners, everyone, second, lon, footprint, by_column, by_tile, products):
    step = pl.program_id(0)
    vectors = everyone.at[:, 0:8, :]
    spread_tiles(step, owners, vectors, footprint, products, False)

    @pl.when(step == pl.num_programs(0) - 1)
    def _():
        spread_end(products, second[...] == 1, lon, by_column, by_tile)


def update_body(
    owners, everyone, image_in, second, lon, footprint,
    by_column, by_tile, direction, sizes, norm, products,
):
    step = pl.program_id(0)

    @pl.when(step == 0)
    def _():
        first = everyone[:, 0:8, :]
        block = lax.broadcasted_iota(jnp.int32, first.shape, 1) % 2
        variance = jnp.where(block == 0, everyone[:, 8:9, :], everyone[:, 9:10, :])
        image = image_in[...] + variance * first
        norm_now = row_gram(first, first)
        step_size = row_solve(row_gram(first, image), norm_now)
        residual = first - row_combine(image, row_weights(step_size))
        norm_next = row_gram(residual, residual)
        ratio = row_solve(norm_now, norm_next)
        direction[...] = residual + row_combine(first, row_weights(ratio))
        for k in range(SAMPLES):
            for j in range(SAMPLES):
                at = SAMPLES * k + j
                sizes[at : at + 1] = step_size[k][j]
                norm[at : at + 1] = norm_next[k][j]

    spread_tiles(step, owners, direction, footprint, products, True)

    @pl.when(step == pl.num_programs(0) - 1)
    def _():
        spread_end(products, second[...] == 1, lon, by_column, by_tile)


def build_body(everyone, time_cov, lat_cov, tile_prior, time_part, row_part, hot, cols):
    step = pl.program_id(0)
    devices, tiles = everyone.shape[0], everyone.shape[2]
    steps_here = time_part.shape[1]
    rows = tile_prior.shape[0]

    @pl.when(step == 0)
    def _():
        at = lax.broadcasted_iota(jnp.int32, (LAT, tiles), 0)
        for d in range(devices):
            place = everyone[d, 10:11, :].astype(jnp.int32)
            here = slice(d * tiles, (d + 1) * tiles)
            for kind, where, cov in (
                (0, place // LAT + steps_here * d, time_cov),
                (1, place % LAT, lat_cov),
            ):
                one = (at == where).astype(jnp.float32)
                picked = jnp.dot(
                    cov[...], one, precision=precise, preferred_element_type=jnp.float32
                )
                upper = picked.astype(jnp.bfloat16)
                lower = (picked - upper.astype(jnp.float32)).astype(jnp.bfloat16)
                cols[kind, 0:LAT, here] = upper
                cols[kind, LAT : 2 * LAT, here] = lower
                turned = one.T.astype(jnp.bfloat16)
                hot[kind, here, 0:LAT] = turned
                hot[kind, here, LAT : 2 * LAT] = turned
                if kind == 0:
                    for e in range(devices):
                        mine = picked[e * steps_here : (e + 1) * steps_here]
                        time_part[e, :, here] = mine
                else:
                    row_part[:, here] = picked

    block = pl.ds(pl.multiple_of(step * rows, rows), rows)
    by_time = jnp.dot(hot[0, block, :], cols[0], preferred_element_type=jnp.float32)
    by_row = jnp.dot(hot[1, block, :], cols[1], preferred_element_type=jnp.float32)
    tile_prior[...] = (by_time * by_row).astype(jnp.bfloat16)


def mix_body(columns, tile_prior, mixed, total):
    step = pl.program_id(0)
    devices, width, tiles = columns.shape
    part = tile_prior.shape[0] // tiles
    lhs = jnp.concatenate([columns[step * part + p] for p in range(part)], axis=1)
    product = jnp.dot(lhs, tile_prior[...], preferred_element_type=jnp.float32)

    @pl.when(step == 0)
    def _():
        total[...] = product

    @pl.when(step > 0)
    def _():
        total[...] += product

    @pl.when(step == pl.num_programs(0) - 1)
    def _():
        for d in range(devices):
            mixed[d] = total[:, d * tiles : (d + 1) * tiles].astype(jnp.bfloat16)


def collect_body(owners, values, second, footprint, sums, rows):
    step = pl.program_id(0)
    chunks, slots = values.shape[0] // SAMPLES, footprint.shape[1]

    @pl.when(step == 0)
    def _():
        is_second = second[...] == 1
        for k in range(SAMPLES):
            turned = values[k * chunks : (k + 1) * chunks].reshape(LON, -1)
            turned = turned.astype(jnp.float32).T
            rows[:, 2 * k, :] = jnp.where(is_second, 0.0, turned)
            rows[:, 2 * k + 1, :] = jnp.where(is_second, turned, 0.0)

    for q in range(owners):
        owner = step * owners + q
        total = 0.0
        for c in range(slots):
            total = total + lax.dot_general(
                rows[owner * slots + c].astype(jnp.bfloat16),
                footprint[q, c],
                (((1,), (1,)), ((), ())),
                preferred_element_type=jnp.float32,
            )
        sums[owner] = total


def flux_body(
    me, everyone, image_in, direction, sizes, norm, time_part, row_part,
    gathered_one, gathered_two, answer, flux, total,
):
    step = pl.program_id(0)
    steps = flux.shape[0]

    @pl.when(step == 0)
    def _():
        second = direction[...]
        block = lax.broadcasted_iota(jnp.int32, second.shape, 1) % 2
        variance = jnp.where(block == 0, everyone[:, 8:9, :], everyone[:, 9:10, :])
        image = image_in[...] + variance * second
        grid = range(SAMPLES)
        norm_now = [[norm[SAMPLES * k + j : SAMPLES * k + j + 1] for j in grid] for k in grid]
        size_one = [[sizes[SAMPLES * k + j : SAMPLES * k + j + 1] for j in grid] for k in grid]
        size_two = row_solve(row_gram(second, image), norm_now)
        own = row_combine(everyone[me[0], 0:8, :], row_weights(size_one))
        own = own + row_combine(direction[me[0]], row_weights(size_two))
        for k in range(SAMPLES):
            for b in range(2):
                answer[b, k : k + 1, :] = own[2 * k + b : 2 * k + b + 1]
        part = 256
        for r in range(total.shape[0] // part):
            at = slice(r * part, (r + 1) * part)
            for j in range(SAMPLES):
                value = 0.0
                for gathered, size in ((gathered_one, size_one), (gathered_two, size_two)):
                    for k in range(SAMPLES):
                        piece = gathered[at, k * LON : (k + 1) * LON]
                        value = value + piece.astype(jnp.float32) * size[k][j]
                total[at, j * LON : (j + 1) * LON] = value.astype(jnp.bfloat16)

    dense = []
    for t in range(steps):
        times = time_part[0, pl.ds(step * steps + t, 1), :]
        dense.append((times * row_part[...]).astype(jnp.bfloat16))
    result = jnp.dot(
        jnp.concatenate(dense, axis=0), total[...], preferred_element_type=jnp.float32
    )
    for t in range(steps):
        for k in range(SAMPLES):
            flux[t, :, k, :] = result[t * LAT : (t + 1) * LAT, k * LON : (k + 1) * LON]


def whole(shape):
    return pl.BlockSpec(shape, lambda i, *_: (0,) * len(shape))


def params():
    return pltpu.CompilerParams(
        dimension_semantics=("arbitrary",), vmem_limit_bytes=48 * 1024 * 1024
    )


def shape_of(shape, dtype):
    return jax.ShapeDtypeStruct(shape, dtype)


def cost(flops, moved):
    return pl.CostEstimate(flops=flops, bytes_accessed=moved, transcendentals=0)


def by_columns(
    right_sides, obs_var, footprint, tile_block, tile_place, time_cov, lat_cov, lon_cov
):
    devices = lax.axis_size("tm")
    me = lax.axis_index("tm")
    owned = right_sides.shape[0]
    steps_here = time_cov.shape[0] // devices
    slots = tile_block.shape[1]
    tiles = devices * slots
    every_tile = devices * tiles
    width = SAMPLES * LON // devices
    f32, bf16 = jnp.float32, jnp.bfloat16

    packed = jnp.concatenate(
        [
            right_sides.transpose(1, 0, 2).reshape(-1, 128),
            obs_var,
            tile_place.astype(f32).reshape(1, 128),
            jnp.zeros((5, 128), f32),
        ]
    )
    everyone = to_all(packed)
    second = tile_block.reshape(tiles, 1)

    stages = 4
    owners = devices // stages
    footprint_spec = pl.BlockSpec(
        (owners, slots, BLOCK_OBS, LON), lambda i, *_: (i, 0, 0, 0)
    )
    everyone_spec = whole(everyone.shape)
    vector_shape = (devices, 8, BLOCK_OBS)
    vector_spec = whole(vector_shape)
    second_spec, lon_spec = whole((tiles, 1)), whole((LON, LON))
    column_shape, tile_shape = (devices, width, tiles), (tiles, SAMPLES * LON)
    small_shape = (SAMPLES * SAMPLES, 128)
    products = pltpu.VMEM((tiles, 8, LON), f32)
    tile_flops = 2 * 8 * tiles * BLOCK_OBS * LON

    by_column, by_tile = pl.pallas_call(
        functools.partial(first_body, owners),
        grid=(stages,),
        in_specs=[everyone_spec, second_spec, lon_spec, footprint_spec],
        out_specs=[whole(column_shape), whole(tile_shape)],
        out_shape=[shape_of(column_shape, bf16), shape_of(tile_shape, bf16)],
        scratch_shapes=[products],
        compiler_params=params(),
        cost_estimate=cost(tile_flops, footprint.size * 2),
        name="spread_first",
    )(everyone, second, lon_cov, footprint)
    gathered_one = lax.all_gather(by_tile, "tm", axis=0, tiled=True)

    build_stages = 8
    build_rows = every_tile // build_stages
    time_shape = (devices, steps_here, every_tile)
    tile_prior, time_part, row_part = pl.pallas_call(
        build_body,
        grid=(build_stages,),
        in_specs=[everyone_spec, whole((128, 128)), whole((128, 128))],
        out_specs=[
            pl.BlockSpec((build_rows, every_tile), lambda i: (i, 0)),
            whole(time_shape),
            whole((LAT, every_tile)),
        ],
        out_shape=[
            shape_of((every_tile, every_tile), bf16),
            shape_of(time_shape, f32),
            shape_of((LAT, every_tile), f32),
        ],
        scratch_shapes=[
            pltpu.VMEM((2, every_tile, 2 * LAT), bf16),
            pltpu.VMEM((2, 2 * LAT, every_tile), bf16),
        ],
        compiler_params=params(),
        cost_estimate=cost(4 * every_tile * every_tile * 256, every_tile * every_tile * 2),
        name="build_prior",
    )(everyone, time_cov, lat_cov)

    def prior(columns):
        sent = lax.all_to_all(columns, "tm", split_axis=0, concat_axis=0, tiled=True)
        mix_stages = 4
        mixed = pl.pallas_call(
            mix_body,
            grid=(mix_stages,),
            in_specs=[
                whole(column_shape),
                pl.BlockSpec((every_tile // mix_stages, every_tile), lambda i: (i, 0)),
            ],
            out_specs=whole(column_shape),
            out_shape=shape_of(column_shape, bf16),
            scratch_shapes=[pltpu.VMEM((width, every_tile), f32)],
            compiler_params=params(),
            cost_estimate=cost(2 * width * every_tile**2, every_tile**2 * 2),
            name="mix_columns",
        )(sent, tile_prior)
        return lax.all_to_all(mixed, "tm", split_axis=0, concat_axis=0, tiled=True)

    def collect(values):
        sums = pl.pallas_call(
            functools.partial(collect_body, owners),
            grid=(stages,),
            in_specs=[whole(column_shape), second_spec, footprint_spec],
            out_specs=vector_spec,
            out_shape=shape_of(vector_shape, f32),
            scratch_shapes=[products],
            compiler_params=params(),
            cost_estimate=cost(tile_flops, footprint.size * 2),
            name="collect",
        )(values, second, footprint)
        terms = lax.all_to_all(sums, "tm", split_axis=0, concat_axis=0, tiled=True)
        return to_all(terms.sum(0))

    image = collect(prior(by_column))
    by_column, by_tile, direction, sizes, norm = pl.pallas_call(
        functools.partial(update_body, owners),
        grid=(stages,),
        in_specs=[everyone_spec, vector_spec, second_spec, lon_spec, footprint_spec],
        out_specs=[
            whole(column_shape),
            whole(tile_shape),
            vector_spec,
            whole(small_shape),
            whole(small_shape),
        ],
        out_shape=[
            shape_of(column_shape, bf16),
            shape_of(tile_shape, bf16),
            shape_of(vector_shape, f32),
            shape_of(small_shape, f32),
            shape_of(small_shape, f32),
        ],
        scratch_shapes=[products],
        compiler_params=params(),
        cost_estimate=cost(tile_flops, footprint.size * 2),
        name="update_spread",
    )(everyone, image, second, lon_cov, footprint)
    gathered_two = lax.all_gather(by_tile, "tm", axis=0, tiled=True)

    image = collect(prior(by_column))
    flux_stages = 4
    flux_steps = steps_here // flux_stages
    answer, flux = pl.pallas_call(
        flux_body,
        grid_spec=pltpu.PrefetchScalarGridSpec(
            num_scalar_prefetch=1,
            grid=(flux_stages,),
            in_specs=[
                everyone_spec,
                vector_spec,
                vector_spec,
                whole(small_shape),
                whole(small_shape),
                pl.BlockSpec((1, steps_here, every_tile), lambda i, me: (me[0], 0, 0)),
                whole((LAT, every_tile)),
                whole((every_tile, SAMPLES * LON)),
                whole((every_tile, SAMPLES * LON)),
            ],
            out_specs=[
                whole((owned, SAMPLES, BLOCK_OBS)),
                pl.BlockSpec((flux_steps, LAT, SAMPLES, LON), lambda i, me: (i, 0, 0, 0)),
            ],
            scratch_shapes=[pltpu.VMEM((every_tile, SAMPLES * LON), bf16)],
        ),
        out_shape=[
            shape_of((owned, SAMPLES, BLOCK_OBS), f32),
            shape_of((steps_here, LAT, SAMPLES, LON), f32),
        ],
        compiler_params=params(),
        cost_estimate=cost(2 * steps_here * LAT * every_tile * SAMPLES * LON, 8 << 20),
        name="update_flux",
    )(
        me.reshape(1).astype(jnp.int32), everyone, image, direction, sizes, norm,
        time_part, row_part, gathered_one, gathered_two,
    )
    return (answer, flux)


def local(right_sides, obs_var, footprint, tile_block, tile_place, *covariances):
    devices = lax.axis_size("tm")
    tiles = tile_block.size
    fits = devices * tiles <= 2048 and devices % 4 == 0 and tiles == 128
    fits = fits and right_sides.shape[0] == 2 and (SAMPLES * LON) % (32 * devices) == 0
    fits = fits and (covariances[0].shape[0] // devices) % 4 == 0
    plan = by_columns if fits else by_gather
    return plan(right_sides, obs_var, footprint, tile_block, tile_place, *covariances)


def solution(mesh):
    in_specs = (
        P(("grp", "tm"), None, None),
        P(("grp", "tm"), None),
        P(("grp", "tm"), None, None, None),
        P(("grp", "tm"), None),
        P(("grp", "tm"), None),
        P(),
        P(),
        P(),
    )
    out_specs = (P(("grp", "tm"), None, None), P(("grp", "tm"), None, None, None))
    return jax.shard_map(local, mesh=mesh, in_specs=in_specs, out_specs=out_specs, check_vma=False)
```

```python
import jax
import jax.numpy as jnp
from jax import lax
from jax.experimental import pallas as pl
from jax.experimental.pallas import tpu as pltpu
from jax.sharding import PartitionSpec as P

LAT = 128
LON = 128
BLOCK_OBS = 128
SAMPLES = 4
ITERS = 2


precise = lax.Precision.HIGHEST


def solve_spd(matrix, target):
    factor = jnp.linalg.cholesky(matrix)
    halfway = lax.linalg.triangular_solve(factor, target, left_side=True, lower=True)
    return lax.linalg.triangular_solve(
        factor, halfway, left_side=True, lower=True, transpose_a=True
    )


def combine(vectors, weights):
    return jnp.einsum("nks,kj->njs", vectors, weights, precision=precise)


def gram(left, right):
    return jnp.einsum("nks,njs->kj", left, right, precision=precise)


def to_all(array):
    devices = lax.axis_size("tm")
    copies = jnp.broadcast_to(array[None], (devices,) + array.shape)
    return lax.all_to_all(copies, "tm", split_axis=0, concat_axis=0, tiled=True)


def by_gather(
    right_sides, obs_var, footprint, tile_block, tile_place, time_cov, lat_cov, lon_cov
):
    devices = lax.axis_size("tm")
    me = lax.axis_index("tm")
    owned = right_sides.shape[0]
    blocks = devices * owned
    steps_here = time_cov.shape[0] // devices
    slots = tile_block.shape[1]
    tiles = devices * slots
    rows_here = steps_here * LAT
    owner_base = (jnp.arange(devices, dtype=jnp.int32) * owned)[:, None]
    requests = owner_base + tile_block

    packed = jnp.concatenate(
        [
            right_sides.reshape(-1, 128),
            obs_var.reshape(-1, 128),
            tile_place.astype(jnp.float32).reshape(-1, 128),
        ]
    )
    everyone = to_all(packed)
    at = owned * SAMPLES
    rhs = everyone[:, :at].reshape(blocks, SAMPLES, BLOCK_OBS)
    variance = everyone[:, at : at + owned].reshape(blocks, BLOCK_OBS)
    places = everyone[:, at + owned :].reshape(devices, tiles).astype(jnp.int32)
    times = (places // LAT + steps_here * jnp.arange(devices, dtype=jnp.int32)[:, None]).reshape(-1)
    rows = (places % LAT).reshape(-1)
    time_hot = (jnp.arange(time_cov.shape[0])[:, None] == times[None, :]).astype(jnp.float32)
    row_hot = (jnp.arange(LAT)[:, None] == rows[None, :]).astype(jnp.float32)
    my_times = lax.dynamic_slice_in_dim(time_cov, me * steps_here, steps_here, 0)
    time_part = jnp.dot(my_times, time_hot, precision=precise)
    row_part = jnp.dot(lat_cov, row_hot, precision=precise)
    dense = (time_part[:, None, :] * row_part[None, :, :]).astype(jnp.bfloat16)
    dense = dense.reshape(rows_here, devices * tiles)
    mine = jnp.take(dense, tile_place.reshape(-1), axis=0)

    def spread(vectors):
        chosen = jnp.take(vectors.astype(jnp.bfloat16), requests, axis=0)
        contrib = jnp.einsum(
            "ocks,ocsl->ockl", chosen, footprint, preferred_element_type=jnp.float32
        )
        contrib = contrib.astype(jnp.bfloat16).reshape(tiles, SAMPLES * LON)
        return lax.all_gather(contrib, "tm", axis=0, tiled=True)

    def collect(gathered):
        field = jnp.dot(mine, gathered, preferred_element_type=jnp.float32)
        field = jnp.dot(field.reshape(-1, LON), lon_cov, precision=precise)
        picked = field.astype(jnp.bfloat16).reshape(devices, slots, SAMPLES, LON)
        partial = jnp.einsum(
            "ockl,ocsl->ocks", picked, footprint, preferred_element_type=jnp.float32
        )
        block_range = jnp.arange(owned, dtype=jnp.int32)
        selector = (tile_block[:, :, None] == block_range).astype(jnp.float32)
        summed = jnp.einsum("ocb,ocks->obks", selector, partial, precision=precise)
        terms = lax.all_to_all(
            summed.reshape(devices, owned * SAMPLES, BLOCK_OBS), "tm", 0, 0, tiled=True
        )
        return to_all(terms.sum(0)).reshape(blocks, SAMPLES, BLOCK_OBS)

    solution = jnp.zeros_like(rhs)
    residual = rhs
    direction = rhs
    norm_now = gram(rhs, rhs)
    gathers, sizes = [], []
    for step in range(ITERS):
        gathered = spread(direction)
        image = collect(gathered) + variance[:, None, :] * direction
        step_size = solve_spd(gram(direction, image), norm_now)
        gathers.append(gathered)
        sizes.append(step_size)
        solution = solution + combine(direction, step_size)
        if step + 1 == ITERS:
            break
        residual = residual - combine(image, step_size)
        norm_next = gram(residual, residual)
        mix_ratio = solve_spd(norm_now, norm_next)
        direction = residual + combine(direction, mix_ratio)
        norm_now = norm_next

    def mix(gathered, size):
        whole = gathered.astype(jnp.float32).reshape(-1, SAMPLES, LON)
        return jnp.einsum("tkl,kj->tjl", whole, size, precision=precise)

    def apply_dense(gathered):
        return jnp.dot(dense, gathered, preferred_element_type=jnp.float32)

    if rows_here < devices * tiles // 4:
        flux = sum(mix(apply_dense(g), size) for g, size in zip(gathers, sizes))
    else:
        total = sum(mix(g, size) for g, size in zip(gathers, sizes))
        flux = apply_dense(total.astype(jnp.bfloat16).reshape(-1, SAMPLES * LON))
    flux = jnp.dot(flux.reshape(-1, LON), lon_cov, precision=precise)
    mine_now = lax.dynamic_slice_in_dim(solution, me * owned, owned, 0)
    return (mine_now, flux.reshape(steps_here, LAT, SAMPLES, LON))


def rolled(x, shift):
    return x if shift == 0 else pltpu.roll(x, 8 - 2 * shift, x.ndim - 2)


def row_gram(left, right):
    entry = [[None] * SAMPLES for _ in range(SAMPLES)]
    for shift in range(SAMPLES):
        product = jnp.sum(left * rolled(right, shift), axis=0)
        total = jnp.broadcast_to(jnp.sum(product, axis=1, keepdims=True), product.shape)
        for k in range(SAMPLES):
            pair = total[2 * k : 2 * k + 1] + total[2 * k + 1 : 2 * k + 2]
            entry[k][(k + shift) % SAMPLES] = pair
    return entry


def row_solve(matrix, target):
    size = range(SAMPLES)
    sym = [[0.5 * (matrix[i][j] + matrix[j][i]) for j in size] for i in size]
    low = [[None] * SAMPLES for _ in size]
    scaled = [[None] * SAMPLES for _ in size]
    inverse = []
    for j in size:
        pivot = sym[j][j]
        for p in range(j):
            pivot = pivot - low[j][p] * scaled[j][p]
        inverse.append(1.0 / pivot)
        for i in range(j + 1, SAMPLES):
            value = sym[i][j]
            for p in range(j):
                value = value - scaled[i][p] * low[j][p]
            scaled[i][j] = value
            low[i][j] = value * inverse[j]
    out = [[None] * SAMPLES for _ in size]
    for c in size:
        part = []
        for i in size:
            value = target[i][c]
            for p in range(i):
                value = value - low[i][p] * part[p]
            part.append(value)
        for i in reversed(size):
            value = part[i] * inverse[i]
            for p in range(i + 1, SAMPLES):
                value = value - low[p][i] * out[p][c]
            out[i][c] = value
    return out


def row_weights(weights):
    sample = lax.broadcasted_iota(jnp.int32, (8, 128), 0) // 2
    result = []
    for shift in range(SAMPLES):
        rows = jnp.broadcast_to(weights[shift][0], (8, 128))
        for j in range(1, SAMPLES):
            rows = jnp.where(sample == j, weights[(j + shift) % SAMPLES][j], rows)
        result.append(rows)
    return result


def row_combine(x, per_shift):
    total = 0.0
    for shift in range(SAMPLES):
        total = total + rolled(x, shift) * per_shift[shift]
    return total


PIECES = 8


def fetch(footprint, held, arrived):
    size = footprint.shape[0] // PIECES
    copies = []
    for p in range(PIECES):
        at = pl.ds(p * size, size)
        copies.append(
            pltpu.make_async_copy(footprint.at[at], held.at[at], arrived.at[p])
        )
    for copy in copies:
        copy.start()
    return copies


def second_of(tile_block):
    owners, slots = tile_block.shape
    tiles = owners * slots
    tile = lax.broadcasted_iota(jnp.int32, (tiles, owners), 0)
    owner = lax.broadcasted_iota(jnp.int32, (tiles, owners), 1)
    rows = jnp.dot(
        (tile // slots == owner).astype(jnp.float32),
        tile_block[...].astype(jnp.float32),
        preferred_element_type=jnp.float32,
    )
    tile = lax.broadcasted_iota(jnp.int32, (tiles, slots), 0)
    slot = lax.broadcasted_iota(jnp.int32, (tiles, slots), 1)
    return jnp.sum(jnp.where(tile % slots == slot, rows, 0.0), axis=1, keepdims=True) > 0.5


def pack_body(right_sides, obs_var, tile_place, copies):
    owners, slots = tile_place.shape
    tiles = owners * slots
    spot = lax.broadcasted_iota(jnp.int32, (slots, tiles), 0)
    lane = lax.broadcasted_iota(jnp.int32, (slots, tiles), 1)
    spread_out = jnp.dot(
        tile_place[...].astype(jnp.float32),
        (lane % slots == spot).astype(jnp.float32),
        precision=precise,
        preferred_element_type=jnp.float32,
    )
    owner = lax.broadcasted_iota(jnp.int32, (owners, tiles), 0)
    lane = lax.broadcasted_iota(jnp.int32, (owners, tiles), 1)
    place = jnp.sum(jnp.where(lane // slots == owner, spread_out, 0.0), axis=0, keepdims=True)
    for k in range(SAMPLES):
        for b in range(2):
            copies[0, 2 * k + b : 2 * k + b + 1] = right_sides[b, k : k + 1]
    copies[0, 8:10] = obs_var[...]
    copies[0, 10:11] = place
    copies[0, 11:16] = jnp.zeros((5, tiles), jnp.float32)
    for d in range(1, copies.shape[0]):
        copies[d] = copies[0]


def spread_tiles(vectors, held, copies, products, split):
    owners, slots = held.shape[:2]
    for owner in range(owners):
        if owner % (owners // PIECES) == 0:
            copies[owner // (owners // PIECES)].wait()
        rows = vectors[owner, 0:8]
        lhs = rows.astype(jnp.bfloat16)
        if split:
            upper = lhs.astype(jnp.float32)
            lhs = jnp.concatenate([upper, rows - upper], axis=0).astype(jnp.bfloat16)
        for c in range(slots):
            r = jnp.dot(lhs, held[owner, c], preferred_element_type=jnp.float32)
            products[owner * slots + c] = r[:8] + r[8:] if split else r


def spread_end(products, second, lon, by_column, by_tile):
    width = by_column.shape[1]
    chunks = LON // width
    for k in range(SAMPLES):
        chosen = jnp.where(second, products[:, 2 * k + 1, :], products[:, 2 * k, :])
        mixed = jnp.dot(
            chosen, lon[...], precision=precise, preferred_element_type=jnp.float32
        )
        by_tile[:, k * LON : (k + 1) * LON] = mixed.astype(jnp.bfloat16)
        turned = mixed.T.astype(jnp.bfloat16)
        by_column[k * chunks : (k + 1) * chunks] = turned.reshape(chunks, width, LON)


def first_body(
    everyone, tile_block, lon, footprint, by_column, by_tile, products, held, arrived
):
    copies = fetch(footprint, held, arrived)
    spread_tiles(everyone, held, copies, products, False)
    spread_end(products, second_of(tile_block), lon, by_column, by_tile)


def with_variance(image, everyone, vectors):
    block = lax.broadcasted_iota(jnp.int32, vectors.shape, 1) % 2
    variance = jnp.where(block == 0, everyone[:, 8:9, :], everyone[:, 9:10, :])
    return image + variance * vectors


def entries(ref):
    grid = range(SAMPLES)
    return [[ref[SAMPLES * k + j : SAMPLES * k + j + 1] for j in grid] for k in grid]


def keep(ref, matrix):
    for k in range(SAMPLES):
        for j in range(SAMPLES):
            ref[SAMPLES * k + j : SAMPLES * k + j + 1] = matrix[k][j]


def update_body(
    everyone, image_in, tile_block, lon, footprint,
    by_column, by_tile, direction, sizes, norm, products, held, arrived,
):
    copies = fetch(footprint, held, arrived)
    first = everyone[:, 0:8, :]
    image = with_variance(image_in[...], everyone, first)
    norm_now = row_gram(first, first)
    step_size = row_solve(row_gram(first, image), norm_now)
    residual = first - row_combine(image, row_weights(step_size))
    norm_next = row_gram(residual, residual)
    ratio = row_solve(norm_now, norm_next)
    direction[...] = residual + row_combine(first, row_weights(ratio))
    keep(sizes, step_size)
    keep(norm, norm_next)
    spread_tiles(direction, held, copies, products, True)
    spread_end(products, second_of(tile_block), lon, by_column, by_tile)


def build_body(everyone, time_cov, lat_cov, tile_prior, time_part, row_part, hot, cols):
    devices, tiles = everyone.shape[0], everyone.shape[2]
    steps_here = time_part.shape[1]
    at = lax.broadcasted_iota(jnp.int32, (LAT, tiles), 0)
    for kind, cov in ((0, time_cov), (1, lat_cov)):
        whole_cov = cov[...]
        upper = whole_cov.astype(jnp.bfloat16)
        lower = (whole_cov - upper.astype(jnp.float32)).astype(jnp.bfloat16)
        ones = []
        for d in range(devices):
            place = (everyone[d, 10:11, :] + 0.5).astype(jnp.int32)
            where = place // LAT + steps_here * d if kind == 0 else place % LAT
            one = (at == where).astype(jnp.float32)
            ones.append(one.astype(jnp.bfloat16))
            turned = one.T.astype(jnp.bfloat16)
            here = slice(d * tiles, (d + 1) * tiles)
            hot[kind, here, 0:LAT] = turned
            hot[kind, here, LAT : 2 * LAT] = turned
        picked = jnp.dot(
            jnp.concatenate([upper, lower], axis=0),
            jnp.concatenate(ones, axis=1),
            preferred_element_type=jnp.float32,
        )
        cols[kind] = picked.astype(jnp.bfloat16)
        both = picked[:LAT] + picked[LAT:]
        if kind == 0:
            time_part[...] = both.reshape(time_part.shape)
        else:
            row_part[...] = both

    rows = 256

    @pl.loop(0, tile_prior.shape[0] // rows)
    def _(step):
        block = pl.ds(pl.multiple_of(step * rows, rows), rows)
        by_time = jnp.dot(hot[0, block, :], cols[0], preferred_element_type=jnp.float32)
        by_row = jnp.dot(hot[1, block, :], cols[1], preferred_element_type=jnp.float32)
        tile_prior[block, :] = (by_time * by_row).astype(jnp.bfloat16)


def mix_body(columns, tile_prior, mixed):
    devices, width, tiles = columns.shape
    lhs = jnp.concatenate([columns[d] for d in range(devices)], axis=1)
    part = 512
    for p in range(devices * tiles // part):
        product = jnp.dot(
            lhs, tile_prior[:, p * part : (p + 1) * part], preferred_element_type=jnp.float32
        )
        for q in range(part // tiles):
            piece = product[:, q * tiles : (q + 1) * tiles]
            mixed[p * (part // tiles) + q] = piece.astype(jnp.bfloat16)


def collect_body(values, tile_block, footprint, sums, rows, held, arrived):
    copies = fetch(footprint, held, arrived)
    chunks = values.shape[0] // SAMPLES
    owners, slots = held.shape[:2]
    is_second = second_of(tile_block)
    for k in range(SAMPLES):
        turned = values[k * chunks : (k + 1) * chunks].reshape(LON, -1)
        turned = turned.astype(jnp.float32).T
        rows[:, 2 * k, :] = jnp.where(is_second, 0.0, turned)
        rows[:, 2 * k + 1, :] = jnp.where(is_second, turned, 0.0)
    for owner in range(owners):
        if owner % (owners // PIECES) == 0:
            copies[owner // (owners // PIECES)].wait()
        total = 0.0
        for c in range(slots):
            total = total + lax.dot_general(
                rows[owner * slots + c].astype(jnp.bfloat16),
                held[owner, c],
                (((1,), (1,)), ((), ())),
                preferred_element_type=jnp.float32,
            )
        sums[owner] = total


def apply_flux(me, time_part, row_part, source, out):
    steps = time_part.shape[1]
    pair = 2
    for step in range(0, steps, pair):
        dense = []
        for t in range(step, step + pair):
            times = time_part[me[0], t : t + 1, :]
            dense.append((times * row_part[...]).astype(jnp.bfloat16))
        out[step * LAT : (step + pair) * LAT] = jnp.dot(
            jnp.concatenate(dense, axis=0), source[...], preferred_element_type=jnp.float32
        )


def flux_first_body(me, sizes, time_part, row_part, gathered, out, total):
    size = entries(sizes)
    part = 256
    for r in range(total.shape[0] // part):
        at = slice(r * part, (r + 1) * part)
        for j in range(SAMPLES):
            value = 0.0
            for k in range(SAMPLES):
                piece = gathered[at, k * LON : (k + 1) * LON]
                value = value + piece.astype(jnp.float32) * size[k][j]
            total[at, j * LON : (j + 1) * LON] = value.astype(jnp.bfloat16)
    apply_flux(me, time_part, row_part, total, out)


def flux_second_body(me, after, time_part, row_part, gathered, out):
    del after
    apply_flux(me, time_part, row_part, gathered, out)


def last_body(
    me, everyone, image_in, direction, sizes, norm, flux_one, flux_two,
    answer, flux, last_size,
):
    @pl.when(pl.program_id(0) == 0)
    def _():
        second = direction[...]
        image = with_variance(image_in[...], everyone, second)
        size_two = row_solve(row_gram(second, image), entries(norm))
        keep(last_size, size_two)
        own = row_combine(everyone[me[0], 0:8, :], row_weights(entries(sizes)))
        own = own + row_combine(direction[me[0]], row_weights(size_two))
        for k in range(SAMPLES):
            for b in range(2):
                answer[b, k : k + 1, :] = own[2 * k + b : 2 * k + b + 1]

    size_two = entries(last_size)
    for t in range(flux.shape[0]):
        at = slice(t * LAT, (t + 1) * LAT)
        parts = [flux_two[at, k * LON : (k + 1) * LON] for k in range(SAMPLES)]
        for j in range(SAMPLES):
            value = flux_one[at, j * LON : (j + 1) * LON]
            for k in range(SAMPLES):
                value = value + parts[k] * size_two[k][j]
            flux[t, :, j, :] = value


def whole(shape):
    return pl.BlockSpec(shape, lambda i, *_: (0,) * len(shape))


def params():
    return pltpu.CompilerParams(vmem_limit_bytes=32 * 1024 * 1024)


def shape_of(shape, dtype):
    return jax.ShapeDtypeStruct(shape, dtype)


def cost(flops, moved):
    return pl.CostEstimate(flops=flops, bytes_accessed=moved, transcendentals=0)


def by_columns(
    right_sides, obs_var, footprint, tile_block, tile_place, time_cov, lat_cov, lon_cov
):
    devices = lax.axis_size("tm")
    me = lax.axis_index("tm").reshape(1).astype(jnp.int32)
    steps_here = time_cov.shape[0] // devices
    tiles = tile_block.size
    every_tile = devices * tiles
    columns = SAMPLES * LON
    width = columns // devices
    rows_here = steps_here * LAT
    f32, bf16 = jnp.float32, jnp.bfloat16

    vmem = pl.BlockSpec(memory_space=pltpu.VMEM)
    smem = pl.BlockSpec(memory_space=pltpu.SMEM)
    hbm = pl.BlockSpec(memory_space=pltpu.HBM)
    vector_shape = shape_of((devices, 8, BLOCK_OBS), f32)
    column_shape = shape_of((devices, width, tiles), bf16)
    tile_shape = shape_of((tiles, columns), bf16)
    small_shape = shape_of((SAMPLES * SAMPLES, 128), f32)
    field_shape = shape_of((rows_here, columns), f32)
    tile_scratch = [
        pltpu.VMEM((tiles, 8, LON), f32),
        pltpu.VMEM(footprint.shape, bf16),
        pltpu.SemaphoreType.DMA((PIECES,)),
    ]
    tile_cost = cost(2 * 8 * footprint.size, footprint.size * 2)
    flux_cost = cost(2 * rows_here * every_tile * columns, every_tile * columns * 2)

    def call(body, in_specs, out_shape, scratch, estimate, name):
        specs = [vmem] * len(out_shape) if isinstance(out_shape, list) else vmem
        return pl.pallas_call(
            body,
            in_specs=in_specs,
            out_specs=specs,
            out_shape=out_shape,
            scratch_shapes=scratch,
            compiler_params=params(),
            cost_estimate=estimate,
            name=name,
        )

    def exchange(array):
        return lax.all_to_all(array, "tm", split_axis=0, concat_axis=0, tiled=True)

    packed_shape = shape_of((devices, 16, 128), f32)
    everyone = exchange(
        call(pack_body, [vmem] * 3, packed_shape, [], cost(0, 1 << 17), "pack")(
            right_sides, obs_var, tile_place
        )
    )
    by_column, by_tile = call(
        first_body,
        [vmem, vmem, vmem, hbm],
        [column_shape, tile_shape],
        tile_scratch,
        tile_cost,
        "spread_first",
    )(everyone, tile_block, lon_cov, footprint)
    gathered_one = lax.all_gather(by_tile, "tm", axis=0, tiled=True)

    tile_prior, time_part, row_part = call(
        build_body,
        [vmem] * 3,
        [
            shape_of((every_tile, every_tile), bf16),
            shape_of((devices, steps_here, every_tile), f32),
            shape_of((LAT, every_tile), f32),
        ],
        [
            pltpu.VMEM((2, every_tile, 2 * LAT), bf16),
            pltpu.VMEM((2, 2 * LAT, every_tile), bf16),
        ],
        cost(4 * every_tile * every_tile * 256, every_tile * every_tile * 2),
        "build_prior",
    )(everyone, time_cov, lat_cov)

    def prior(by_column):
        mixed = call(
            mix_body,
            [vmem] * 2,
            column_shape,
            [],
            cost(2 * width * every_tile**2, every_tile**2 * 2),
            "mix_columns",
        )(exchange(by_column), tile_prior)
        return exchange(mixed)

    def collect(values):
        sums = call(
            collect_body, [vmem, vmem, hbm], vector_shape, tile_scratch, tile_cost, "collect"
        )(values, tile_block, footprint)
        return exchange(sums).sum(0)

    image = to_all(collect(prior(by_column)))
    by_column, by_tile, direction, sizes, norm = call(
        update_body,
        [vmem] * 4 + [hbm],
        [column_shape, tile_shape, vector_shape, small_shape, small_shape],
        tile_scratch,
        tile_cost,
        "update_spread",
    )(everyone, image, tile_block, lon_cov, footprint)
    gathered_two = lax.all_gather(by_tile, "tm", axis=0, tiled=True)
    flux_one = call(
        flux_first_body,
        [smem] + [vmem] * 4,
        field_shape,
        [pltpu.VMEM((every_tile, columns), bf16)],
        flux_cost,
        "flux_first",
    )(me, sizes, time_part, row_part, gathered_one)

    own_image = collect(prior(by_column))
    image = to_all(own_image)
    flux_two = call(
        flux_second_body,
        [smem] + [vmem] * 4,
        field_shape,
        [],
        flux_cost,
        "flux_second",
    )(me, own_image, time_part, row_part, gathered_two)

    stages = 4
    block = pl.BlockSpec((rows_here // stages, columns), lambda i: (i, 0))
    answer, flux = pl.pallas_call(
        last_body,
        grid=(stages,),
        in_specs=[
            smem,
            whole(everyone.shape),
            whole(image.shape),
            whole(direction.shape),
            whole(sizes.shape),
            whole(norm.shape),
            block,
            block,
        ],
        out_specs=[
            whole(right_sides.shape),
            pl.BlockSpec((steps_here // stages, LAT, SAMPLES, LON), lambda i: (i, 0, 0, 0)),
        ],
        out_shape=[
            shape_of(right_sides.shape, f32),
            shape_of((steps_here, LAT, SAMPLES, LON), f32),
        ],
        scratch_shapes=[pltpu.VMEM(small_shape.shape, f32)],
        compiler_params=params(),
        cost_estimate=cost(1 << 20, 6 << 20),
        name="last",
    )(me, everyone, image, direction, sizes, norm, flux_one, flux_two)
    return (answer, flux)


def local(right_sides, obs_var, footprint, tile_block, tile_place, *covariances):
    devices = lax.axis_size("tm")
    tiles = tile_block.size
    fits = devices * tiles <= 2048 and devices % 4 == 0 and tiles == 128
    fits = fits and right_sides.shape[0] == 2 and (SAMPLES * LON) % (32 * devices) == 0
    fits = fits and (covariances[0].shape[0] // devices) % 4 == 0
    plan = by_columns if fits else by_gather
    return plan(right_sides, obs_var, footprint, tile_block, tile_place, *covariances)


def solution(mesh):
    in_specs = (
        P(("grp", "tm"), None, None),
        P(("grp", "tm"), None),
        P(("grp", "tm"), None, None, None),
        P(("grp", "tm"), None),
        P(("grp", "tm"), None),
        P(),
        P(),
        P(),
    )
    out_specs = (P(("grp", "tm"), None, None), P(("grp", "tm"), None, None, None))
    return jax.shard_map(local, mesh=mesh, in_specs=in_specs, out_specs=out_specs, check_vma=False)
```

```python
import jax
import jax.numpy as jnp
from jax import lax
from jax.experimental import pallas as pl
from jax.experimental.pallas import tpu as pltpu
from jax.sharding import PartitionSpec as P

LAT = 128
LON = 128
BLOCK_OBS = 128
SAMPLES = 4
ITERS = 2


precise = lax.Precision.HIGHEST


def solve_spd(matrix, target):
    factor = jnp.linalg.cholesky(matrix)
    halfway = lax.linalg.triangular_solve(factor, target, left_side=True, lower=True)
    return lax.linalg.triangular_solve(
        factor, halfway, left_side=True, lower=True, transpose_a=True
    )


def combine(vectors, weights):
    return jnp.einsum("nks,kj->njs", vectors, weights, precision=precise)


def gram(left, right):
    return jnp.einsum("nks,njs->kj", left, right, precision=precise)


def to_all(array):
    devices = lax.axis_size("tm")
    copies = jnp.broadcast_to(array[None], (devices,) + array.shape)
    return lax.all_to_all(copies, "tm", split_axis=0, concat_axis=0, tiled=True)


def by_gather(
    right_sides, obs_var, footprint, tile_block, tile_place, time_cov, lat_cov, lon_cov
):
    devices = lax.axis_size("tm")
    me = lax.axis_index("tm")
    owned = right_sides.shape[0]
    blocks = devices * owned
    steps_here = time_cov.shape[0] // devices
    slots = tile_block.shape[1]
    tiles = devices * slots
    rows_here = steps_here * LAT
    owner_base = (jnp.arange(devices, dtype=jnp.int32) * owned)[:, None]
    requests = owner_base + tile_block

    packed = jnp.concatenate(
        [
            right_sides.reshape(-1, 128),
            obs_var.reshape(-1, 128),
            tile_place.astype(jnp.float32).reshape(-1, 128),
        ]
    )
    everyone = to_all(packed)
    at = owned * SAMPLES
    rhs = everyone[:, :at].reshape(blocks, SAMPLES, BLOCK_OBS)
    variance = everyone[:, at : at + owned].reshape(blocks, BLOCK_OBS)
    places = everyone[:, at + owned :].reshape(devices, tiles).astype(jnp.int32)
    times = (places // LAT + steps_here * jnp.arange(devices, dtype=jnp.int32)[:, None]).reshape(-1)
    rows = (places % LAT).reshape(-1)
    time_hot = (jnp.arange(time_cov.shape[0])[:, None] == times[None, :]).astype(jnp.float32)
    row_hot = (jnp.arange(LAT)[:, None] == rows[None, :]).astype(jnp.float32)
    my_times = lax.dynamic_slice_in_dim(time_cov, me * steps_here, steps_here, 0)
    time_part = jnp.dot(my_times, time_hot, precision=precise)
    row_part = jnp.dot(lat_cov, row_hot, precision=precise)
    dense = (time_part[:, None, :] * row_part[None, :, :]).astype(jnp.bfloat16)
    dense = dense.reshape(rows_here, devices * tiles)
    mine = jnp.take(dense, tile_place.reshape(-1), axis=0)

    def spread(vectors):
        chosen = jnp.take(vectors.astype(jnp.bfloat16), requests, axis=0)
        contrib = jnp.einsum(
            "ocks,ocsl->ockl", chosen, footprint, preferred_element_type=jnp.float32
        )
        contrib = contrib.astype(jnp.bfloat16).reshape(tiles, SAMPLES * LON)
        return lax.all_gather(contrib, "tm", axis=0, tiled=True)

    def collect(gathered):
        field = jnp.dot(mine, gathered, preferred_element_type=jnp.float32)
        field = jnp.dot(field.reshape(-1, LON), lon_cov, precision=precise)
        picked = field.astype(jnp.bfloat16).reshape(devices, slots, SAMPLES, LON)
        partial = jnp.einsum(
            "ockl,ocsl->ocks", picked, footprint, preferred_element_type=jnp.float32
        )
        block_range = jnp.arange(owned, dtype=jnp.int32)
        selector = (tile_block[:, :, None] == block_range).astype(jnp.float32)
        summed = jnp.einsum("ocb,ocks->obks", selector, partial, precision=precise)
        terms = lax.all_to_all(
            summed.reshape(devices, owned * SAMPLES, BLOCK_OBS), "tm", 0, 0, tiled=True
        )
        return to_all(terms.sum(0)).reshape(blocks, SAMPLES, BLOCK_OBS)

    solution = jnp.zeros_like(rhs)
    residual = rhs
    direction = rhs
    norm_now = gram(rhs, rhs)
    gathers, sizes = [], []
    for step in range(ITERS):
        gathered = spread(direction)
        image = collect(gathered) + variance[:, None, :] * direction
        step_size = solve_spd(gram(direction, image), norm_now)
        gathers.append(gathered)
        sizes.append(step_size)
        solution = solution + combine(direction, step_size)
        if step + 1 == ITERS:
            break
        residual = residual - combine(image, step_size)
        norm_next = gram(residual, residual)
        mix_ratio = solve_spd(norm_now, norm_next)
        direction = residual + combine(direction, mix_ratio)
        norm_now = norm_next

    def mix(gathered, size):
        whole = gathered.astype(jnp.float32).reshape(-1, SAMPLES, LON)
        return jnp.einsum("tkl,kj->tjl", whole, size, precision=precise)

    def apply_dense(gathered):
        return jnp.dot(dense, gathered, preferred_element_type=jnp.float32)

    if rows_here < devices * tiles // 4:
        flux = sum(mix(apply_dense(g), size) for g, size in zip(gathers, sizes))
    else:
        total = sum(mix(g, size) for g, size in zip(gathers, sizes))
        flux = apply_dense(total.astype(jnp.bfloat16).reshape(-1, SAMPLES * LON))
    flux = jnp.dot(flux.reshape(-1, LON), lon_cov, precision=precise)
    mine_now = lax.dynamic_slice_in_dim(solution, me * owned, owned, 0)
    return (mine_now, flux.reshape(steps_here, LAT, SAMPLES, LON))


def rolled(x, shift):
    return x if shift == 0 else pltpu.roll(x, 8 - 2 * shift, x.ndim - 2)


def row_gram(left, right):
    entry = [[None] * SAMPLES for _ in range(SAMPLES)]
    for shift in range(SAMPLES):
        product = jnp.sum(left * rolled(right, shift), axis=0)
        total = jnp.broadcast_to(jnp.sum(product, axis=1, keepdims=True), product.shape)
        for k in range(SAMPLES):
            pair = total[2 * k : 2 * k + 1] + total[2 * k + 1 : 2 * k + 2]
            entry[k][(k + shift) % SAMPLES] = pair
    return entry


def row_solve(matrix, target):
    size = range(SAMPLES)
    sym = [[0.5 * (matrix[i][j] + matrix[j][i]) for j in size] for i in size]
    low = [[None] * SAMPLES for _ in size]
    scaled = [[None] * SAMPLES for _ in size]
    inverse = []
    for j in size:
        pivot = sym[j][j]
        for p in range(j):
            pivot = pivot - low[j][p] * scaled[j][p]
        inverse.append(1.0 / pivot)
        for i in range(j + 1, SAMPLES):
            value = sym[i][j]
            for p in range(j):
                value = value - scaled[i][p] * low[j][p]
            scaled[i][j] = value
            low[i][j] = value * inverse[j]
    out = [[None] * SAMPLES for _ in size]
    for c in size:
        part = []
        for i in size:
            value = target[i][c]
            for p in range(i):
                value = value - low[i][p] * part[p]
            part.append(value)
        for i in reversed(size):
            value = part[i] * inverse[i]
            for p in range(i + 1, SAMPLES):
                value = value - low[p][i] * out[p][c]
            out[i][c] = value
    return out


def row_weights(weights):
    sample = lax.broadcasted_iota(jnp.int32, (8, 128), 0) // 2
    result = []
    for shift in range(SAMPLES):
        rows = jnp.broadcast_to(weights[shift][0], (8, 128))
        for j in range(1, SAMPLES):
            rows = jnp.where(sample == j, weights[(j + shift) % SAMPLES][j], rows)
        result.append(rows)
    return result


def row_combine(x, per_shift):
    total = 0.0
    for shift in range(SAMPLES):
        total = total + rolled(x, shift) * per_shift[shift]
    return total


PIECES = 8


def fetch(source, held, arrived):
    pieces = arrived.shape[0]
    size = source.shape[0] // pieces
    copies = []
    for p in range(pieces):
        at = pl.ds(p * size, size)
        copies.append(pltpu.make_async_copy(source.at[at], held.at[at], arrived.at[p]))
    for copy in copies:
        copy.start()
    return copies


def second_of(tile_block):
    slots, owners = tile_block.shape
    tiles = owners * slots
    tile = lax.broadcasted_iota(jnp.int32, (tiles, slots), 0)
    slot = lax.broadcasted_iota(jnp.int32, (tiles, slots), 1)
    rows = jnp.dot(
        (tile % slots == slot).astype(jnp.float32),
        tile_block[...].astype(jnp.float32),
        preferred_element_type=jnp.float32,
    )
    tile = lax.broadcasted_iota(jnp.int32, (tiles, owners), 0)
    owner = lax.broadcasted_iota(jnp.int32, (tiles, owners), 1)
    return jnp.sum(jnp.where(tile // slots == owner, rows, 0.0), axis=1, keepdims=True) > 0.5


def pack_body(right_sides, obs_var, tile_place, copies):
    slots, owners = tile_place.shape
    tiles = owners * slots
    owner = lax.broadcasted_iota(jnp.int32, (owners, tiles), 0)
    lane = lax.broadcasted_iota(jnp.int32, (owners, tiles), 1)
    spread_out = jnp.dot(
        tile_place[...].astype(jnp.float32),
        (lane // slots == owner).astype(jnp.float32),
        precision=precise,
        preferred_element_type=jnp.float32,
    )
    slot = lax.broadcasted_iota(jnp.int32, (slots, tiles), 0)
    lane = lax.broadcasted_iota(jnp.int32, (slots, tiles), 1)
    place = jnp.sum(jnp.where(lane % slots == slot, spread_out, 0.0), axis=0, keepdims=True)
    for k in range(SAMPLES):
        for b in range(2):
            copies[0, 2 * k + b : 2 * k + b + 1] = right_sides[b, k : k + 1]
    copies[0, 8:10] = obs_var[...]
    copies[0, 10:11] = place
    copies[0, 11:16] = jnp.zeros((5, tiles), jnp.float32)
    for d in range(1, copies.shape[0]):
        copies[d] = copies[0]


def spread_tiles(vectors, held, copies, products, split):
    owners, slots = held.shape[:2]
    for owner in range(owners):
        if owner % (owners // PIECES) == 0:
            copies[owner // (owners // PIECES)].wait()
        rows = vectors[owner, 0:8]
        lhs = rows.astype(jnp.bfloat16)
        if split:
            upper = lhs.astype(jnp.float32)
            lhs = jnp.concatenate([upper, rows - upper], axis=0).astype(jnp.bfloat16)
        for c in range(slots):
            r = jnp.dot(lhs, held[owner, c], preferred_element_type=jnp.float32)
            products[owner * slots + c] = r[:8] + r[8:] if split else r


def spread_end(products, second, lon, by_column, by_tile):
    width = by_column.shape[1]
    chunks = LON // width
    for k in range(SAMPLES):
        chosen = jnp.where(second, products[:, 2 * k + 1, :], products[:, 2 * k, :])
        mixed = jnp.dot(
            chosen, lon[...], precision=precise, preferred_element_type=jnp.float32
        )
        by_tile[:, k * LON : (k + 1) * LON] = mixed.astype(jnp.bfloat16)
        turned = mixed.T.astype(jnp.bfloat16)
        by_column[k * chunks : (k + 1) * chunks] = turned.reshape(chunks, width, LON)


def first_body(
    everyone, tile_block, lon, footprint, by_column, by_tile, products, held, arrived
):
    copies = fetch(footprint, held, arrived)
    spread_tiles(everyone, held, copies, products, False)
    spread_end(products, second_of(tile_block), lon, by_column, by_tile)


def with_variance(image, everyone, vectors):
    block = lax.broadcasted_iota(jnp.int32, vectors.shape, 1) % 2
    variance = jnp.where(block == 0, everyone[:, 8:9, :], everyone[:, 9:10, :])
    return image + variance * vectors


def entries(ref):
    grid = range(SAMPLES)
    return [[ref[SAMPLES * k + j : SAMPLES * k + j + 1] for j in grid] for k in grid]


def keep(ref, matrix):
    for k in range(SAMPLES):
        for j in range(SAMPLES):
            ref[SAMPLES * k + j : SAMPLES * k + j + 1] = matrix[k][j]


def update_body(
    everyone, image_in, tile_block, lon, footprint,
    by_column, by_tile, direction, sizes, norm, products, held, arrived,
):
    copies = fetch(footprint, held, arrived)
    first = everyone[:, 0:8, :]
    image = with_variance(image_in[...], everyone, first)
    norm_now = row_gram(first, first)
    step_size = row_solve(row_gram(first, image), norm_now)
    residual = first - row_combine(image, row_weights(step_size))
    norm_next = row_gram(residual, residual)
    ratio = row_solve(norm_now, norm_next)
    direction[...] = residual + row_combine(first, row_weights(ratio))
    keep(sizes, step_size)
    keep(norm, norm_next)
    spread_tiles(direction, held, copies, products, True)
    spread_end(products, second_of(tile_block), lon, by_column, by_tile)


def build_body(
    me, everyone, time_cov, lat_cov, tile_prior, time_part, row_part, hot, cols, times
):
    devices, tiles = everyone.shape[0], everyone.shape[2]
    steps_here = time_part.shape[0]
    rows = tile_prior.shape[0]
    step = pl.program_id(0)

    @pl.when(step == 0)
    def _():
        at = lax.broadcasted_iota(jnp.int32, (LAT, tiles), 0)
        for kind, cov in ((0, time_cov), (1, lat_cov)):
            whole_cov = cov[...]
            upper = whole_cov.astype(jnp.bfloat16)
            lower = (whole_cov - upper.astype(jnp.float32)).astype(jnp.bfloat16)
            ones = []
            for d in range(devices):
                place = (everyone[d, 10:11, :] + 0.5).astype(jnp.int32)
                where = place // LAT + steps_here * d if kind == 0 else place % LAT
                one = (at == where).astype(jnp.float32)
                ones.append(one.astype(jnp.bfloat16))
                turned = one.T.astype(jnp.bfloat16)
                here = slice(d * tiles, (d + 1) * tiles)
                hot[kind, here, 0:LAT] = turned
                hot[kind, here, LAT : 2 * LAT] = turned
            picked = jnp.dot(
                jnp.concatenate([upper, lower], axis=0),
                jnp.concatenate(ones, axis=1),
                preferred_element_type=jnp.float32,
            )
            cols[kind] = picked.astype(jnp.bfloat16)
            both = picked[:LAT] + picked[LAT:]
            if kind == 0:
                times[...] = both
                mine = pl.ds(pl.multiple_of(me[0] * steps_here, steps_here), steps_here)
                time_part[...] = times[mine, :]
            else:
                row_part[...] = both

    block = pl.ds(pl.multiple_of(step * rows, rows), rows)
    by_time = jnp.dot(hot[0, block, :], cols[0], preferred_element_type=jnp.float32)
    by_row = jnp.dot(hot[1, block, :], cols[1], preferred_element_type=jnp.float32)
    tile_prior[...] = (by_time * by_row).astype(jnp.bfloat16)


def mix_body(columns, tile_prior, mixed, total, held, arrived):
    copies = fetch(tile_prior, held, arrived)
    devices, width, tiles = columns.shape
    part = devices // len(copies)
    for p, copy in enumerate(copies):
        at = range(p * part, (p + 1) * part)
        lhs = jnp.concatenate([columns[d] for d in at], axis=1)
        copy.wait()
        product = jnp.dot(
            lhs,
            held[p * part * tiles : (p + 1) * part * tiles],
            preferred_element_type=jnp.float32,
        )
        total[...] = product if p == 0 else total[...] + product
    for d in range(devices):
        mixed[d] = total[:, d * tiles : (d + 1) * tiles].astype(jnp.bfloat16)


def collect_body(values, tile_block, footprint, *rest):
    sums, rows = rest[-2:]
    chunks = values.shape[0] // SAMPLES
    owners, slots = footprint.shape[:2]
    is_second = second_of(tile_block)
    for k in range(SAMPLES):
        turned = values[k * chunks : (k + 1) * chunks].reshape(LON, -1)
        turned = turned.astype(jnp.float32).T
        rows[:, 2 * k, :] = jnp.where(is_second, 0.0, turned)
        rows[:, 2 * k + 1, :] = jnp.where(is_second, turned, 0.0)
    for owner in range(owners):
        total = 0.0
        for c in range(slots):
            total = total + lax.dot_general(
                rows[owner * slots + c].astype(jnp.bfloat16),
                footprint[owner, c],
                (((1,), (1,)), ((), ())),
                preferred_element_type=jnp.float32,
            )
        sums[owner] = total


def apply_flux(time_part, row_part, source, out):
    steps = time_part.shape[0]
    pair = 2
    for step in range(0, steps, pair):
        dense = []
        for t in range(step, step + pair):
            dense.append((time_part[t : t + 1, :] * row_part[...]).astype(jnp.bfloat16))
        out[step * LAT : (step + pair) * LAT] = jnp.dot(
            jnp.concatenate(dense, axis=0), source[...], preferred_element_type=jnp.float32
        )


def flux_first_body(
    sizes, time_part, row_part, gathered,
    out, token, rows, held, total, row_arrived, arrived,
):
    copies = fetch(gathered, held, arrived)
    row_copies = fetch(row_part, rows, row_arrived)
    size = entries(sizes)
    part = total.shape[0] // len(copies)
    for r, copy in enumerate(copies):
        copy.wait()
        at = slice(r * part, (r + 1) * part)
        for j in range(SAMPLES):
            value = 0.0
            for k in range(SAMPLES):
                piece = held[at, k * LON : (k + 1) * LON]
                value = value + piece.astype(jnp.float32) * size[k][j]
            total[at, j * LON : (j + 1) * LON] = value.astype(jnp.bfloat16)
    for copy in row_copies:
        copy.wait()
    apply_flux(time_part, rows, total, out)
    token[...] = out[0:8, 0:128]


def flux_second_body(
    after, time_part, row_part, gathered, out, rows, held, row_arrived, arrived
):
    del after
    row_copies = fetch(row_part, rows, row_arrived)
    copies = fetch(gathered, held, arrived)
    for copy in row_copies + copies:
        copy.wait()
    apply_flux(time_part, rows, held, out)


def last_body(
    me, everyone, image_in, direction, sizes, norm, flux_one, flux_two,
    answer, flux, last_size,
):
    @pl.when(pl.program_id(0) == 0)
    def _():
        second = direction[...]
        image = with_variance(image_in[...], everyone, second)
        size_two = row_solve(row_gram(second, image), entries(norm))
        keep(last_size, size_two)
        own = row_combine(everyone[me[0], 0:8, :], row_weights(entries(sizes)))
        own = own + row_combine(direction[me[0]], row_weights(size_two))
        for k in range(SAMPLES):
            for b in range(2):
                answer[b, k : k + 1, :] = own[2 * k + b : 2 * k + b + 1]

    size_two = entries(last_size)
    for t in range(flux.shape[0]):
        at = slice(t * LAT, (t + 1) * LAT)
        parts = [flux_two[at, k * LON : (k + 1) * LON] for k in range(SAMPLES)]
        for j in range(SAMPLES):
            value = flux_one[at, j * LON : (j + 1) * LON]
            for k in range(SAMPLES):
                value = value + parts[k] * size_two[k][j]
            flux[t, :, j, :] = value


def whole(shape):
    return pl.BlockSpec(shape, lambda i, *_: (0,) * len(shape))


MIB = 1024 * 1024


def params(grant=59):
    return pltpu.CompilerParams(vmem_limit_bytes=grant * MIB)


def shape_of(shape, dtype):
    return jax.ShapeDtypeStruct(shape, dtype)


def cost(flops, moved):
    return pl.CostEstimate(flops=flops, bytes_accessed=moved, transcendentals=0)


def by_columns(
    right_sides, obs_var, footprint, tile_block, tile_place, time_cov, lat_cov, lon_cov
):
    devices = lax.axis_size("tm")
    me = lax.axis_index("tm").reshape(1).astype(jnp.int32)
    steps_here = time_cov.shape[0] // devices
    tiles = tile_block.size
    every_tile = devices * tiles
    columns = SAMPLES * LON
    width = columns // devices
    rows_here = steps_here * LAT
    f32, bf16 = jnp.float32, jnp.bfloat16

    vmem = pl.BlockSpec(memory_space=pltpu.VMEM)
    smem = pl.BlockSpec(memory_space=pltpu.SMEM)
    hbm = pl.BlockSpec(memory_space=pltpu.HBM)
    vector_shape = shape_of((devices, 8, BLOCK_OBS), f32)
    column_shape = shape_of((devices, width, tiles), bf16)
    tile_shape = shape_of((tiles, columns), bf16)
    small_shape = shape_of((SAMPLES * SAMPLES, 128), f32)
    field_shape = shape_of((rows_here, columns), f32)
    turned_block = tile_block.T
    row_shape = shape_of((LAT, every_tile), f32)
    row_scratch = [pltpu.VMEM(row_shape.shape, f32)]
    held_scratch = [pltpu.VMEM((every_tile, columns), bf16)]
    copied = [pltpu.SemaphoreType.DMA((1,)), pltpu.SemaphoreType.DMA((PIECES,))]
    tile_scratch = [
        pltpu.VMEM((tiles, 8, LON), f32),
        pltpu.VMEM(footprint.shape, bf16),
        pltpu.SemaphoreType.DMA((PIECES,)),
    ]
    tile_cost = cost(2 * 8 * footprint.size, footprint.size * 2)
    flux_cost = cost(2 * rows_here * every_tile * columns, every_tile * columns * 2)

    def call(body, in_specs, out_shape, scratch, estimate, name, grant=59):
        specs = [vmem] * len(out_shape) if isinstance(out_shape, list) else vmem
        return pl.pallas_call(
            body,
            in_specs=in_specs,
            out_specs=specs,
            out_shape=out_shape,
            scratch_shapes=scratch,
            compiler_params=params(grant),
            cost_estimate=estimate,
            name=name,
        )

    def exchange(array):
        return lax.all_to_all(array, "tm", split_axis=0, concat_axis=0, tiled=True)

    packed_shape = shape_of((devices, 16, 128), f32)
    everyone = exchange(
        call(pack_body, [vmem] * 3, packed_shape, [], cost(0, 1 << 17), "pack")(
            right_sides, obs_var, tile_place.T
        )
    )
    by_column, by_tile = call(
        first_body,
        [vmem, vmem, vmem, hbm],
        [column_shape, tile_shape],
        tile_scratch,
        tile_cost,
        "spread_first",
    )(everyone, turned_block, lon_cov, footprint)
    gathered_one = lax.all_gather(by_tile, "tm", axis=0, tiled=True)

    build_rows = every_tile // 8
    tile_prior, time_part, row_part = pl.pallas_call(
        build_body,
        grid=(8,),
        in_specs=[
            smem,
            whole(everyone.shape),
            whole(time_cov.shape),
            whole(lat_cov.shape),
        ],
        out_specs=[
            pl.BlockSpec((build_rows, every_tile), lambda i: (i, 0)),
            whole((steps_here, every_tile)),
            whole(row_shape.shape),
        ],
        out_shape=[
            shape_of((every_tile, every_tile), bf16),
            shape_of((steps_here, every_tile), f32),
            row_shape,
        ],
        scratch_shapes=[
            pltpu.VMEM((2, every_tile, 2 * LAT), bf16),
            pltpu.VMEM((2, 2 * LAT, every_tile), bf16),
            pltpu.VMEM((LAT, every_tile), f32),
        ],
        compiler_params=params(),
        cost_estimate=cost(4 * every_tile * every_tile * 256, every_tile * every_tile * 2),
        name="build_prior",
    )(me, everyone, time_cov, lat_cov)

    def prior(by_column):
        mixed = call(
            mix_body,
            [vmem, hbm],
            column_shape,
            [
                pltpu.VMEM((width, every_tile), f32),
                pltpu.VMEM((every_tile, every_tile), bf16),
                pltpu.SemaphoreType.DMA((PIECES,)),
            ],
            cost(2 * width * every_tile**2, every_tile**2 * 2),
            "mix_columns",
        )(exchange(by_column), tile_prior)
        return exchange(mixed)

    def collect(values, *after):
        sums = call(
            collect_body,
            [vmem] * 3 + [hbm] * len(after),
            vector_shape,
            tile_scratch[:1],
            tile_cost,
            "collect",
            48,
        )(values, turned_block, footprint, *after)
        return exchange(sums).sum(0)

    image = to_all(collect(prior(by_column)))
    by_column, by_tile, direction, sizes, norm = call(
        update_body,
        [vmem] * 4 + [hbm],
        [column_shape, tile_shape, vector_shape, small_shape, small_shape],
        tile_scratch,
        tile_cost,
        "update_spread",
    )(everyone, image, turned_block, lon_cov, footprint)
    gathered_two = lax.all_gather(by_tile, "tm", axis=0, tiled=True)
    flux_one, token = call(
        flux_first_body,
        [vmem, vmem, hbm, hbm],
        [field_shape, shape_of((8, 128), f32)],
        row_scratch + held_scratch * 2 + copied,
        flux_cost,
        "flux_first",
    )(sizes, time_part, row_part, gathered_one)

    own_image = collect(prior(by_column), token)
    image = to_all(own_image)
    flux_two = call(
        flux_second_body,
        [hbm, vmem, hbm, hbm],
        field_shape,
        row_scratch + held_scratch + copied,
        flux_cost,
        "flux_second",
    )(own_image, time_part, row_part, gathered_two)

    stages = 4
    block = pl.BlockSpec((rows_here // stages, columns), lambda i: (i, 0))
    answer, flux = pl.pallas_call(
        last_body,
        grid=(stages,),
        in_specs=[
            smem,
            whole(everyone.shape),
            whole(image.shape),
            whole(direction.shape),
            whole(sizes.shape),
            whole(norm.shape),
            block,
            block,
        ],
        out_specs=[
            whole(right_sides.shape),
            pl.BlockSpec((steps_here // stages, LAT, SAMPLES, LON), lambda i: (i, 0, 0, 0)),
        ],
        out_shape=[
            shape_of(right_sides.shape, f32),
            shape_of((steps_here, LAT, SAMPLES, LON), f32),
        ],
        scratch_shapes=[pltpu.VMEM(small_shape.shape, f32)],
        compiler_params=params(),
        cost_estimate=cost(1 << 20, 6 << 20),
        name="last",
    )(me, everyone, image, direction, sizes, norm, flux_one, flux_two)
    return (answer, flux)


def local(right_sides, obs_var, footprint, tile_block, tile_place, *covariances):
    devices = lax.axis_size("tm")
    tiles = tile_block.size
    fits = devices * tiles <= 2048 and devices % 4 == 0 and tiles == 128
    fits = fits and right_sides.shape[0] == 2 and (SAMPLES * LON) % (32 * devices) == 0
    fits = fits and (covariances[0].shape[0] // devices) % 4 == 0
    plan = by_columns if fits else by_gather
    return plan(right_sides, obs_var, footprint, tile_block, tile_place, *covariances)


def solution(mesh):
    in_specs = (
        P(("grp", "tm"), None, None),
        P(("grp", "tm"), None),
        P(("grp", "tm"), None, None, None),
        P(("grp", "tm"), None),
        P(("grp", "tm"), None),
        P(),
        P(),
        P(),
    )
    out_specs = (P(("grp", "tm"), None, None), P(("grp", "tm"), None, None, None))
    return jax.shard_map(local, mesh=mesh, in_specs=in_specs, out_specs=out_specs, check_vma=False)
```

```python
import jax
import jax.numpy as jnp
from jax import lax
from jax.experimental import pallas as pl
from jax.experimental.pallas import tpu as pltpu
from jax.sharding import PartitionSpec as P

LAT = 128
LON = 128
BLOCK_OBS = 128
SAMPLES = 4
ITERS = 2


precise = lax.Precision.HIGHEST


def solve_spd(matrix, target):
    factor = jnp.linalg.cholesky(matrix)
    halfway = lax.linalg.triangular_solve(factor, target, left_side=True, lower=True)
    return lax.linalg.triangular_solve(
        factor, halfway, left_side=True, lower=True, transpose_a=True
    )


def combine(vectors, weights):
    return jnp.einsum("nks,kj->njs", vectors, weights, precision=precise)


def gram(left, right):
    return jnp.einsum("nks,njs->kj", left, right, precision=precise)


def to_all(array):
    devices = lax.axis_size("tm")
    copies = jnp.broadcast_to(array[None], (devices,) + array.shape)
    return lax.all_to_all(copies, "tm", split_axis=0, concat_axis=0, tiled=True)


def by_gather(
    right_sides, obs_var, footprint, tile_block, tile_place, time_cov, lat_cov, lon_cov
):
    devices = lax.axis_size("tm")
    me = lax.axis_index("tm")
    owned = right_sides.shape[0]
    blocks = devices * owned
    steps_here = time_cov.shape[0] // devices
    slots = tile_block.shape[1]
    tiles = devices * slots
    rows_here = steps_here * LAT
    owner_base = (jnp.arange(devices, dtype=jnp.int32) * owned)[:, None]
    requests = owner_base + tile_block

    packed = jnp.concatenate(
        [
            right_sides.reshape(-1, 128),
            obs_var.reshape(-1, 128),
            tile_place.astype(jnp.float32).reshape(-1, 128),
        ]
    )
    everyone = to_all(packed)
    at = owned * SAMPLES
    rhs = everyone[:, :at].reshape(blocks, SAMPLES, BLOCK_OBS)
    variance = everyone[:, at : at + owned].reshape(blocks, BLOCK_OBS)
    places = everyone[:, at + owned :].reshape(devices, tiles).astype(jnp.int32)
    times = (places // LAT + steps_here * jnp.arange(devices, dtype=jnp.int32)[:, None]).reshape(-1)
    rows = (places % LAT).reshape(-1)
    time_hot = (jnp.arange(time_cov.shape[0])[:, None] == times[None, :]).astype(jnp.float32)
    row_hot = (jnp.arange(LAT)[:, None] == rows[None, :]).astype(jnp.float32)
    my_times = lax.dynamic_slice_in_dim(time_cov, me * steps_here, steps_here, 0)
    time_part = jnp.dot(my_times, time_hot, precision=precise)
    row_part = jnp.dot(lat_cov, row_hot, precision=precise)
    dense = (time_part[:, None, :] * row_part[None, :, :]).astype(jnp.bfloat16)
    dense = dense.reshape(rows_here, devices * tiles)
    mine = jnp.take(dense, tile_place.reshape(-1), axis=0)

    def spread(vectors):
        chosen = jnp.take(vectors.astype(jnp.bfloat16), requests, axis=0)
        contrib = jnp.einsum(
            "ocks,ocsl->ockl", chosen, footprint, preferred_element_type=jnp.float32
        )
        contrib = contrib.astype(jnp.bfloat16).reshape(tiles, SAMPLES * LON)
        return lax.all_gather(contrib, "tm", axis=0, tiled=True)

    def collect(gathered):
        field = jnp.dot(mine, gathered, preferred_element_type=jnp.float32)
        field = jnp.dot(field.reshape(-1, LON), lon_cov, precision=precise)
        picked = field.astype(jnp.bfloat16).reshape(devices, slots, SAMPLES, LON)
        partial = jnp.einsum(
            "ockl,ocsl->ocks", picked, footprint, preferred_element_type=jnp.float32
        )
        block_range = jnp.arange(owned, dtype=jnp.int32)
        selector = (tile_block[:, :, None] == block_range).astype(jnp.float32)
        summed = jnp.einsum("ocb,ocks->obks", selector, partial, precision=precise)
        terms = lax.all_to_all(
            summed.reshape(devices, owned * SAMPLES, BLOCK_OBS), "tm", 0, 0, tiled=True
        )
        return to_all(terms.sum(0)).reshape(blocks, SAMPLES, BLOCK_OBS)

    solution = jnp.zeros_like(rhs)
    residual = rhs
    direction = rhs
    norm_now = gram(rhs, rhs)
    gathers, sizes = [], []
    for step in range(ITERS):
        gathered = spread(direction)
        image = collect(gathered) + variance[:, None, :] * direction
        step_size = solve_spd(gram(direction, image), norm_now)
        gathers.append(gathered)
        sizes.append(step_size)
        solution = solution + combine(direction, step_size)
        if step + 1 == ITERS:
            break
        residual = residual - combine(image, step_size)
        norm_next = gram(residual, residual)
        mix_ratio = solve_spd(norm_now, norm_next)
        direction = residual + combine(direction, mix_ratio)
        norm_now = norm_next

    def mix(gathered, size):
        whole = gathered.astype(jnp.float32).reshape(-1, SAMPLES, LON)
        return jnp.einsum("tkl,kj->tjl", whole, size, precision=precise)

    def apply_dense(gathered):
        return jnp.dot(dense, gathered, preferred_element_type=jnp.float32)

    if rows_here < devices * tiles // 4:
        flux = sum(mix(apply_dense(g), size) for g, size in zip(gathers, sizes))
    else:
        total = sum(mix(g, size) for g, size in zip(gathers, sizes))
        flux = apply_dense(total.astype(jnp.bfloat16).reshape(-1, SAMPLES * LON))
    flux = jnp.dot(flux.reshape(-1, LON), lon_cov, precision=precise)
    mine_now = lax.dynamic_slice_in_dim(solution, me * owned, owned, 0)
    return (mine_now, flux.reshape(steps_here, LAT, SAMPLES, LON))


def rolled(x, shift):
    return x if shift == 0 else pltpu.roll(x, 8 - 2 * shift, x.ndim - 2)


def row_gram(left, right):
    entry = [[None] * SAMPLES for _ in range(SAMPLES)]
    for shift in range(SAMPLES):
        product = jnp.sum(left * rolled(right, shift), axis=0)
        total = jnp.broadcast_to(jnp.sum(product, axis=1, keepdims=True), product.shape)
        for k in range(SAMPLES):
            pair = total[2 * k : 2 * k + 1] + total[2 * k + 1 : 2 * k + 2]
            entry[k][(k + shift) % SAMPLES] = pair
    return entry


def row_solve(matrix, target):
    size = range(SAMPLES)
    sym = [[0.5 * (matrix[i][j] + matrix[j][i]) for j in size] for i in size]
    low = [[None] * SAMPLES for _ in size]
    scaled = [[None] * SAMPLES for _ in size]
    inverse = []
    for j in size:
        pivot = sym[j][j]
        for p in range(j):
            pivot = pivot - low[j][p] * scaled[j][p]
        inverse.append(1.0 / pivot)
        for i in range(j + 1, SAMPLES):
            value = sym[i][j]
            for p in range(j):
                value = value - scaled[i][p] * low[j][p]
            scaled[i][j] = value
            low[i][j] = value * inverse[j]
    out = [[None] * SAMPLES for _ in size]
    for c in size:
        part = []
        for i in size:
            value = target[i][c]
            for p in range(i):
                value = value - low[i][p] * part[p]
            part.append(value)
        for i in reversed(size):
            value = part[i] * inverse[i]
            for p in range(i + 1, SAMPLES):
                value = value - low[p][i] * out[p][c]
            out[i][c] = value
    return out


def row_weights(weights):
    sample = lax.broadcasted_iota(jnp.int32, (8, 128), 0) // 2
    result = []
    for shift in range(SAMPLES):
        rows = jnp.broadcast_to(weights[shift][0], (8, 128))
        for j in range(1, SAMPLES):
            rows = jnp.where(sample == j, weights[(j + shift) % SAMPLES][j], rows)
        result.append(rows)
    return result


def row_combine(x, per_shift):
    total = 0.0
    for shift in range(SAMPLES):
        total = total + rolled(x, shift) * per_shift[shift]
    return total


PIECES = 8


def fetch(source, held, arrived):
    pieces = arrived.shape[0]
    size = source.shape[0] // pieces
    copies = []
    for p in range(pieces):
        at = pl.ds(p * size, size)
        copies.append(pltpu.make_async_copy(source.at[at], held.at[at], arrived.at[p]))
    for copy in copies:
        copy.start()
    return copies


def second_of(tile_block):
    slots, owners = tile_block.shape
    tiles = owners * slots
    tile = lax.broadcasted_iota(jnp.int32, (tiles, slots), 0)
    slot = lax.broadcasted_iota(jnp.int32, (tiles, slots), 1)
    rows = jnp.dot(
        (tile % slots == slot).astype(jnp.float32),
        tile_block[...].astype(jnp.float32),
        preferred_element_type=jnp.float32,
    )
    tile = lax.broadcasted_iota(jnp.int32, (tiles, owners), 0)
    owner = lax.broadcasted_iota(jnp.int32, (tiles, owners), 1)
    return jnp.sum(jnp.where(tile // slots == owner, rows, 0.0), axis=1, keepdims=True) > 0.5


def pack_body(right_sides, obs_var, tile_place, copies):
    slots, owners = tile_place.shape
    tiles = owners * slots
    owner = lax.broadcasted_iota(jnp.int32, (owners, tiles), 0)
    lane = lax.broadcasted_iota(jnp.int32, (owners, tiles), 1)
    spread_out = jnp.dot(
        tile_place[...].astype(jnp.float32),
        (lane // slots == owner).astype(jnp.float32),
        precision=precise,
        preferred_element_type=jnp.float32,
    )
    slot = lax.broadcasted_iota(jnp.int32, (slots, tiles), 0)
    lane = lax.broadcasted_iota(jnp.int32, (slots, tiles), 1)
    place = jnp.sum(jnp.where(lane % slots == slot, spread_out, 0.0), axis=0, keepdims=True)
    for k in range(SAMPLES):
        for b in range(2):
            copies[0, 2 * k + b : 2 * k + b + 1] = right_sides[b, k : k + 1]
    copies[0, 8:10] = obs_var[...]
    copies[0, 10:11] = place
    copies[0, 11:16] = jnp.zeros((5, tiles), jnp.float32)
    for d in range(1, copies.shape[0]):
        copies[d] = copies[0]


def spread_tiles(vectors, footprint, products, split):
    owners, slots = footprint.shape[:2]
    for owner in range(owners):
        rows = vectors[owner, 0:8]
        lhs = rows.astype(jnp.bfloat16)
        if split:
            upper = lhs.astype(jnp.float32)
            lhs = jnp.concatenate([upper, rows - upper], axis=0).astype(jnp.bfloat16)
        for c in range(slots):
            r = jnp.dot(lhs, footprint[owner, c], preferred_element_type=jnp.float32)
            products[owner * slots + c] = r[:8] + r[8:] if split else r


def spread_end(products, second, lon, by_column, by_tile):
    width = by_column.shape[1]
    chunks = LON // width
    for k in range(SAMPLES):
        chosen = jnp.where(second, products[:, 2 * k + 1, :], products[:, 2 * k, :])
        mixed = jnp.dot(
            chosen, lon[...], precision=precise, preferred_element_type=jnp.float32
        )
        by_tile[:, k * LON : (k + 1) * LON] = mixed.astype(jnp.bfloat16)
        turned = mixed.T.astype(jnp.bfloat16)
        by_column[k * chunks : (k + 1) * chunks] = turned.reshape(chunks, width, LON)


def first_body(everyone, tile_block, lon, footprint, by_column, by_tile, products):
    spread_tiles(everyone, footprint, products, False)
    spread_end(products, second_of(tile_block), lon, by_column, by_tile)


def with_variance(image, everyone, vectors):
    block = lax.broadcasted_iota(jnp.int32, vectors.shape, 1) % 2
    variance = jnp.where(block == 0, everyone[:, 8:9, :], everyone[:, 9:10, :])
    return image + variance * vectors


def entries(ref):
    grid = range(SAMPLES)
    return [[ref[SAMPLES * k + j : SAMPLES * k + j + 1] for j in grid] for k in grid]


def keep(ref, matrix):
    for k in range(SAMPLES):
        for j in range(SAMPLES):
            ref[SAMPLES * k + j : SAMPLES * k + j + 1] = matrix[k][j]


def update_body(
    everyone, image_in, tile_block, lon, footprint,
    by_column, by_tile, direction, sizes, norm, products,
):
    first = everyone[:, 0:8, :]
    image = with_variance(image_in[...], everyone, first)
    norm_now = row_gram(first, first)
    step_size = row_solve(row_gram(first, image), norm_now)
    residual = first - row_combine(image, row_weights(step_size))
    norm_next = row_gram(residual, residual)
    ratio = row_solve(norm_now, norm_next)
    direction[...] = residual + row_combine(first, row_weights(ratio))
    keep(sizes, step_size)
    keep(norm, norm_next)
    spread_tiles(direction, footprint, products, True)
    spread_end(products, second_of(tile_block), lon, by_column, by_tile)


def build_body(
    me, everyone, time_cov, lat_cov,
    tile_prior, second_prior, time_part, row_part, hot, cols, times, sent,
):
    devices, tiles = everyone.shape[0], everyone.shape[2]
    steps_here = time_part.shape[0]
    at = lax.broadcasted_iota(jnp.int32, (LAT, tiles), 0)
    for kind, cov in ((0, time_cov), (1, lat_cov)):
        whole_cov = cov[...]
        upper = whole_cov.astype(jnp.bfloat16)
        lower = (whole_cov - upper.astype(jnp.float32)).astype(jnp.bfloat16)
        ones = []
        for d in range(devices):
            place = (everyone[d, 10:11, :] + 0.5).astype(jnp.int32)
            where = place // LAT + steps_here * d if kind == 0 else place % LAT
            one = (at == where).astype(jnp.float32)
            ones.append(one.astype(jnp.bfloat16))
            turned = one.T.astype(jnp.bfloat16)
            here = slice(d * tiles, (d + 1) * tiles)
            hot[kind, here, 0:LAT] = turned
            hot[kind, here, LAT : 2 * LAT] = turned
        picked = jnp.dot(
            jnp.concatenate([upper, lower], axis=0),
            jnp.concatenate(ones, axis=1),
            preferred_element_type=jnp.float32,
        )
        cols[kind] = picked.astype(jnp.bfloat16)
        both = picked[:LAT] + picked[LAT:]
        if kind == 0:
            times[...] = both
            mine = pl.ds(pl.multiple_of(me[0] * steps_here, steps_here), steps_here)
            time_part[...] = times[mine, :]
        else:
            row_part[...] = both

    rows = tile_prior.shape[0] // PIECES

    def sending(piece):
        block = pl.ds(pl.multiple_of(piece * rows, rows), rows)
        return pltpu.make_async_copy(
            tile_prior.at[block], second_prior.at[block], sent.at[piece]
        )

    @pl.loop(0, PIECES)
    def _(piece):
        block = pl.ds(pl.multiple_of(piece * rows, rows), rows)
        by_time = jnp.dot(hot[0, block, :], cols[0], preferred_element_type=jnp.float32)
        by_row = jnp.dot(hot[1, block, :], cols[1], preferred_element_type=jnp.float32)
        tile_prior[block, :] = (by_time * by_row).astype(jnp.bfloat16)
        sending(piece).start()

    for piece in range(PIECES):
        sending(piece).wait()


def mix_body(columns, tile_prior, mixed):
    devices, width, tiles = columns.shape
    lhs = jnp.concatenate([columns[d] for d in range(devices)], axis=1)
    part = 512
    for p in range(devices * tiles // part):
        product = jnp.dot(
            lhs, tile_prior[:, p * part : (p + 1) * part], preferred_element_type=jnp.float32
        )
        for q in range(part // tiles):
            piece = product[:, q * tiles : (q + 1) * tiles]
            mixed[p * (part // tiles) + q] = piece.astype(jnp.bfloat16)


def sum_body(terms, total, copies):
    value = jnp.sum(terms[...], axis=0)
    total[...] = value
    for d in range(copies.shape[0]):
        copies[d] = value


def collect_body(values, tile_block, footprint, *rest):
    sums, rows = rest[-2:]
    chunks = values.shape[0] // SAMPLES
    owners, slots = footprint.shape[:2]
    is_second = second_of(tile_block)
    for k in range(SAMPLES):
        turned = values[k * chunks : (k + 1) * chunks].reshape(LON, -1)
        turned = turned.astype(jnp.float32).T
        rows[:, 2 * k, :] = jnp.where(is_second, 0.0, turned)
        rows[:, 2 * k + 1, :] = jnp.where(is_second, turned, 0.0)
    for owner in range(owners):
        total = 0.0
        for c in range(slots):
            total = total + lax.dot_general(
                rows[owner * slots + c].astype(jnp.bfloat16),
                footprint[owner, c],
                (((1,), (1,)), ((), ())),
                preferred_element_type=jnp.float32,
            )
        sums[owner] = total


def apply_flux(time_part, row_part, source, out):
    steps = time_part.shape[0]
    pair = 2
    for step in range(0, steps, pair):
        dense = []
        for t in range(step, step + pair):
            dense.append((time_part[t : t + 1, :] * row_part[...]).astype(jnp.bfloat16))
        out[step * LAT : (step + pair) * LAT] = jnp.dot(
            jnp.concatenate(dense, axis=0), source[...], preferred_element_type=jnp.float32
        )


def flux_first_body(
    sizes, time_part, row_part, gathered,
    out, token, rows, held, total, row_arrived, arrived,
):
    copies = fetch(gathered, held, arrived)
    row_copies = fetch(row_part, rows, row_arrived)
    size = entries(sizes)
    part = total.shape[0] // len(copies)
    for r, copy in enumerate(copies):
        copy.wait()
        at = slice(r * part, (r + 1) * part)
        for j in range(SAMPLES):
            value = 0.0
            for k in range(SAMPLES):
                piece = held[at, k * LON : (k + 1) * LON]
                value = value + piece.astype(jnp.float32) * size[k][j]
            total[at, j * LON : (j + 1) * LON] = value.astype(jnp.bfloat16)
    for copy in row_copies:
        copy.wait()
    apply_flux(time_part, rows, total, out)
    token[...] = out[0:8, 0:128]


def flux_second_body(
    after, time_part, row_part, gathered, out, rows, held, row_arrived, arrived
):
    del after
    row_copies = fetch(row_part, rows, row_arrived)
    copies = fetch(gathered, held, arrived)
    for copy in row_copies + copies:
        copy.wait()
    apply_flux(time_part, rows, held, out)


def last_body(
    me, everyone, image_in, direction, sizes, norm, flux_one, flux_two,
    answer, flux, last_size,
):
    @pl.when(pl.program_id(0) == 0)
    def _():
        second = direction[...]
        image = with_variance(image_in[...], everyone, second)
        size_two = row_solve(row_gram(second, image), entries(norm))
        keep(last_size, size_two)
        own = row_combine(everyone[me[0], 0:8, :], row_weights(entries(sizes)))
        own = own + row_combine(direction[me[0]], row_weights(size_two))
        for k in range(SAMPLES):
            for b in range(2):
                answer[b, k : k + 1, :] = own[2 * k + b : 2 * k + b + 1]

    size_two = entries(last_size)
    for t in range(flux.shape[0]):
        at = slice(t * LAT, (t + 1) * LAT)
        parts = [flux_two[at, k * LON : (k + 1) * LON] for k in range(SAMPLES)]
        for j in range(SAMPLES):
            value = flux_one[at, j * LON : (j + 1) * LON]
            for k in range(SAMPLES):
                value = value + parts[k] * size_two[k][j]
            flux[t, :, j, :] = value


def whole(shape):
    return pl.BlockSpec(shape, lambda i, *_: (0,) * len(shape))


MIB = 1024 * 1024


def params(grant=32):
    return pltpu.CompilerParams(vmem_limit_bytes=grant * MIB)


def shape_of(shape, dtype):
    return jax.ShapeDtypeStruct(shape, dtype)


def cost(flops, moved):
    return pl.CostEstimate(flops=flops, bytes_accessed=moved, transcendentals=0)


def by_columns(
    right_sides, obs_var, footprint, tile_block, tile_place, time_cov, lat_cov, lon_cov
):
    devices = lax.axis_size("tm")
    me = lax.axis_index("tm").reshape(1).astype(jnp.int32)
    steps_here = time_cov.shape[0] // devices
    tiles = tile_block.size
    every_tile = devices * tiles
    columns = SAMPLES * LON
    width = columns // devices
    rows_here = steps_here * LAT
    f32, bf16 = jnp.float32, jnp.bfloat16

    vmem = pl.BlockSpec(memory_space=pltpu.VMEM)
    smem = pl.BlockSpec(memory_space=pltpu.SMEM)
    hbm = pl.BlockSpec(memory_space=pltpu.HBM)
    vector_shape = shape_of((devices, 8, BLOCK_OBS), f32)
    column_shape = shape_of((devices, width, tiles), bf16)
    tile_shape = shape_of((tiles, columns), bf16)
    small_shape = shape_of((SAMPLES * SAMPLES, 128), f32)
    field_shape = shape_of((rows_here, columns), f32)
    turned_block = tile_block.T
    row_shape = shape_of((LAT, every_tile), f32)
    row_scratch = [pltpu.VMEM(row_shape.shape, f32)]
    held_scratch = [pltpu.VMEM((every_tile, columns), bf16)]
    copied = [pltpu.SemaphoreType.DMA((1,)), pltpu.SemaphoreType.DMA((PIECES,))]
    tile_scratch = [pltpu.VMEM((tiles, 8, LON), f32)]
    tile_cost = cost(2 * 8 * footprint.size, footprint.size * 2)
    flux_cost = cost(2 * rows_here * every_tile * columns, every_tile * columns * 2)

    def call(body, in_specs, out_shape, scratch, estimate, name, grant=32):
        specs = [vmem] * len(out_shape) if isinstance(out_shape, list) else vmem
        return pl.pallas_call(
            body,
            in_specs=in_specs,
            out_specs=specs,
            out_shape=out_shape,
            scratch_shapes=scratch,
            compiler_params=params(grant),
            cost_estimate=estimate,
            name=name,
        )

    def exchange(array):
        return lax.all_to_all(array, "tm", split_axis=0, concat_axis=0, tiled=True)

    packed_shape = shape_of((devices, 16, 128), f32)
    everyone = exchange(
        call(pack_body, [vmem] * 3, packed_shape, [], cost(0, 12 * MIB), "pack")(
            right_sides, obs_var, tile_place.T
        )
    )
    by_column, by_tile = call(
        first_body,
        [vmem] * 4,
        [column_shape, tile_shape],
        tile_scratch,
        tile_cost,
        "spread_first",
    )(everyone, turned_block, lon_cov, footprint)
    gathered_one = lax.all_gather(by_tile, "tm", axis=0, tiled=True)

    prior_shape = shape_of((every_tile, every_tile), bf16)
    first_prior, second_prior, time_part, row_part = pl.pallas_call(
        build_body,
        in_specs=[smem] + [vmem] * 3,
        out_specs=[vmem, hbm, vmem, vmem],
        out_shape=[
            prior_shape,
            prior_shape,
            shape_of((steps_here, every_tile), f32),
            row_shape,
        ],
        scratch_shapes=[
            pltpu.VMEM((2, every_tile, 2 * LAT), bf16),
            pltpu.VMEM((2, 2 * LAT, every_tile), bf16),
            pltpu.VMEM((LAT, every_tile), f32),
            pltpu.SemaphoreType.DMA((PIECES,)),
        ],
        compiler_params=params(40),
        cost_estimate=cost(4 * every_tile * every_tile * 256, every_tile * every_tile * 2),
        name="build_prior",
    )(me, everyone, time_cov, lat_cov)

    def prior(by_column, tile_prior):
        mixed = call(
            mix_body,
            [vmem] * 2,
            column_shape,
            [],
            cost(2 * width * every_tile**2, every_tile**2 * 2),
            "mix_columns",
        )(exchange(by_column), tile_prior)
        return exchange(mixed)

    def collect(values, *after):
        sums = call(
            collect_body,
            [vmem] * 3 + [hbm] * len(after),
            vector_shape,
            tile_scratch,
            tile_cost,
            "collect",
        )(values, turned_block, footprint, *after)
        own, copies = call(
            sum_body,
            [vmem],
            [shape_of((8, BLOCK_OBS), f32), vector_shape],
            [],
            cost(0, 12 * MIB),
            "sum_terms",
        )(exchange(sums))
        return own, exchange(copies)


    _, image = collect(prior(by_column, first_prior))
    by_column, by_tile, direction, sizes, norm = call(
        update_body,
        [vmem] * 5,
        [column_shape, tile_shape, vector_shape, small_shape, small_shape],
        tile_scratch,
        cost(2 * 8 * footprint.size, 24 * MIB),
        "update_spread",
    )(everyone, image, turned_block, lon_cov, footprint)
    gathered_two = lax.all_gather(by_tile, "tm", axis=0, tiled=True)
    flux_one, token = call(
        flux_first_body,
        [vmem, vmem, hbm, hbm],
        [field_shape, shape_of((8, 128), f32)],
        row_scratch + held_scratch * 2 + copied,
        flux_cost,
        "flux_first",
    )(sizes, time_part, row_part, gathered_one)

    own_image, image = collect(prior(by_column, second_prior), token)
    flux_two = call(
        flux_second_body,
        [hbm, vmem, hbm, hbm],
        field_shape,
        row_scratch + held_scratch + copied,
        flux_cost,
        "flux_second",
    )(own_image, time_part, row_part, gathered_two)

    stages = 4
    block = pl.BlockSpec((rows_here // stages, columns), lambda i: (i, 0))
    answer, flux = pl.pallas_call(
        last_body,
        grid=(stages,),
        in_specs=[
            smem,
            whole(everyone.shape),
            whole(image.shape),
            whole(direction.shape),
            whole(sizes.shape),
            whole(norm.shape),
            block,
            block,
        ],
        out_specs=[
            whole(right_sides.shape),
            pl.BlockSpec((steps_here // stages, LAT, SAMPLES, LON), lambda i: (i, 0, 0, 0)),
        ],
        out_shape=[
            shape_of(right_sides.shape, f32),
            shape_of((steps_here, LAT, SAMPLES, LON), f32),
        ],
        scratch_shapes=[pltpu.VMEM(small_shape.shape, f32)],
        compiler_params=params(),
        cost_estimate=cost(1 << 20, 6 << 20),
        name="last",
    )(me, everyone, image, direction, sizes, norm, flux_one, flux_two)
    return (answer, flux)


def local(right_sides, obs_var, footprint, tile_block, tile_place, *covariances):
    devices = lax.axis_size("tm")
    tiles = tile_block.size
    fits = devices * tiles <= 2048 and devices % 4 == 0 and tiles == 128
    fits = fits and right_sides.shape[0] == 2 and (SAMPLES * LON) % (32 * devices) == 0
    fits = fits and (covariances[0].shape[0] // devices) % 4 == 0
    plan = by_columns if fits else by_gather
    return plan(right_sides, obs_var, footprint, tile_block, tile_place, *covariances)


def solution(mesh):
    in_specs = (
        P(("grp", "tm"), None, None),
        P(("grp", "tm"), None),
        P(("grp", "tm"), None, None, None),
        P(("grp", "tm"), None),
        P(("grp", "tm"), None),
        P(),
        P(),
        P(),
    )
    out_specs = (P(("grp", "tm"), None, None), P(("grp", "tm"), None, None, None))
    return jax.shard_map(local, mesh=mesh, in_specs=in_specs, out_specs=out_specs, check_vma=False)
```

```python
import jax
import jax.numpy as jnp
from jax import lax
from jax.experimental import pallas as pl
from jax.experimental.pallas import tpu as pltpu
from jax.sharding import PartitionSpec as P

LAT = 128
LON = 128
BLOCK_OBS = 128
SAMPLES = 4
ITERS = 2


precise = lax.Precision.HIGHEST


def solve_spd(matrix, target):
    factor = jnp.linalg.cholesky(matrix)
    halfway = lax.linalg.triangular_solve(factor, target, left_side=True, lower=True)
    return lax.linalg.triangular_solve(
        factor, halfway, left_side=True, lower=True, transpose_a=True
    )


def combine(vectors, weights):
    return jnp.einsum("nks,kj->njs", vectors, weights, precision=precise)


def gram(left, right):
    return jnp.einsum("nks,njs->kj", left, right, precision=precise)


def to_all(array):
    devices = lax.axis_size("tm")
    copies = jnp.broadcast_to(array[None], (devices,) + array.shape)
    return lax.all_to_all(copies, "tm", split_axis=0, concat_axis=0, tiled=True)


def by_gather(
    right_sides, obs_var, footprint, tile_block, tile_place, time_cov, lat_cov, lon_cov
):
    devices = lax.axis_size("tm")
    me = lax.axis_index("tm")
    owned = right_sides.shape[0]
    blocks = devices * owned
    steps_here = time_cov.shape[0] // devices
    slots = tile_block.shape[1]
    tiles = devices * slots
    rows_here = steps_here * LAT
    owner_base = (jnp.arange(devices, dtype=jnp.int32) * owned)[:, None]
    requests = owner_base + tile_block

    packed = jnp.concatenate(
        [
            right_sides.reshape(-1, 128),
            obs_var.reshape(-1, 128),
            tile_place.astype(jnp.float32).reshape(-1, 128),
        ]
    )
    everyone = to_all(packed)
    at = owned * SAMPLES
    rhs = everyone[:, :at].reshape(blocks, SAMPLES, BLOCK_OBS)
    variance = everyone[:, at : at + owned].reshape(blocks, BLOCK_OBS)
    places = everyone[:, at + owned :].reshape(devices, tiles).astype(jnp.int32)
    times = (places // LAT + steps_here * jnp.arange(devices, dtype=jnp.int32)[:, None]).reshape(-1)
    rows = (places % LAT).reshape(-1)
    time_hot = (jnp.arange(time_cov.shape[0])[:, None] == times[None, :]).astype(jnp.float32)
    row_hot = (jnp.arange(LAT)[:, None] == rows[None, :]).astype(jnp.float32)
    my_times = lax.dynamic_slice_in_dim(time_cov, me * steps_here, steps_here, 0)
    time_part = jnp.dot(my_times, time_hot, precision=precise)
    row_part = jnp.dot(lat_cov, row_hot, precision=precise)
    dense = (time_part[:, None, :] * row_part[None, :, :]).astype(jnp.bfloat16)
    dense = dense.reshape(rows_here, devices * tiles)
    mine = jnp.take(dense, tile_place.reshape(-1), axis=0)

    def spread(vectors):
        chosen = jnp.take(vectors.astype(jnp.bfloat16), requests, axis=0)
        contrib = jnp.einsum(
            "ocks,ocsl->ockl", chosen, footprint, preferred_element_type=jnp.float32
        )
        contrib = contrib.astype(jnp.bfloat16).reshape(tiles, SAMPLES * LON)
        return lax.all_gather(contrib, "tm", axis=0, tiled=True)

    def collect(gathered):
        field = jnp.dot(mine, gathered, preferred_element_type=jnp.float32)
        field = jnp.dot(field.reshape(-1, LON), lon_cov, precision=precise)
        picked = field.astype(jnp.bfloat16).reshape(devices, slots, SAMPLES, LON)
        partial = jnp.einsum(
            "ockl,ocsl->ocks", picked, footprint, preferred_element_type=jnp.float32
        )
        block_range = jnp.arange(owned, dtype=jnp.int32)
        selector = (tile_block[:, :, None] == block_range).astype(jnp.float32)
        summed = jnp.einsum("ocb,ocks->obks", selector, partial, precision=precise)
        terms = lax.all_to_all(
            summed.reshape(devices, owned * SAMPLES, BLOCK_OBS), "tm", 0, 0, tiled=True
        )
        return to_all(terms.sum(0)).reshape(blocks, SAMPLES, BLOCK_OBS)

    solution = jnp.zeros_like(rhs)
    residual = rhs
    direction = rhs
    norm_now = gram(rhs, rhs)
    gathers, sizes = [], []
    for step in range(ITERS):
        gathered = spread(direction)
        image = collect(gathered) + variance[:, None, :] * direction
        step_size = solve_spd(gram(direction, image), norm_now)
        gathers.append(gathered)
        sizes.append(step_size)
        solution = solution + combine(direction, step_size)
        if step + 1 == ITERS:
            break
        residual = residual - combine(image, step_size)
        norm_next = gram(residual, residual)
        mix_ratio = solve_spd(norm_now, norm_next)
        direction = residual + combine(direction, mix_ratio)
        norm_now = norm_next

    def mix(gathered, size):
        whole = gathered.astype(jnp.float32).reshape(-1, SAMPLES, LON)
        return jnp.einsum("tkl,kj->tjl", whole, size, precision=precise)

    def apply_dense(gathered):
        return jnp.dot(dense, gathered, preferred_element_type=jnp.float32)

    if rows_here < devices * tiles // 4:
        flux = sum(mix(apply_dense(g), size) for g, size in zip(gathers, sizes))
    else:
        total = sum(mix(g, size) for g, size in zip(gathers, sizes))
        flux = apply_dense(total.astype(jnp.bfloat16).reshape(-1, SAMPLES * LON))
    flux = jnp.dot(flux.reshape(-1, LON), lon_cov, precision=precise)
    mine_now = lax.dynamic_slice_in_dim(solution, me * owned, owned, 0)
    return (mine_now, flux.reshape(steps_here, LAT, SAMPLES, LON))


def rolled(x, shift):
    return x if shift == 0 else pltpu.roll(x, 8 - 2 * shift, x.ndim - 2)


def row_gram(left, right):
    entry = [[None] * SAMPLES for _ in range(SAMPLES)]
    for shift in range(SAMPLES):
        product = jnp.sum(left * rolled(right, shift), axis=0)
        total = jnp.broadcast_to(jnp.sum(product, axis=1, keepdims=True), product.shape)
        for k in range(SAMPLES):
            pair = total[2 * k : 2 * k + 1] + total[2 * k + 1 : 2 * k + 2]
            entry[k][(k + shift) % SAMPLES] = pair
    return entry


def row_solve(matrix, target):
    size = range(SAMPLES)
    sym = [[0.5 * (matrix[i][j] + matrix[j][i]) for j in size] for i in size]
    low = [[None] * SAMPLES for _ in size]
    scaled = [[None] * SAMPLES for _ in size]
    inverse = []
    for j in size:
        pivot = sym[j][j]
        for p in range(j):
            pivot = pivot - low[j][p] * scaled[j][p]
        inverse.append(1.0 / pivot)
        for i in range(j + 1, SAMPLES):
            value = sym[i][j]
            for p in range(j):
                value = value - scaled[i][p] * low[j][p]
            scaled[i][j] = value
            low[i][j] = value * inverse[j]
    out = [[None] * SAMPLES for _ in size]
    for c in size:
        part = []
        for i in size:
            value = target[i][c]
            for p in range(i):
                value = value - low[i][p] * part[p]
            part.append(value)
        for i in reversed(size):
            value = part[i] * inverse[i]
            for p in range(i + 1, SAMPLES):
                value = value - low[p][i] * out[p][c]
            out[i][c] = value
    return out


def row_weights(weights):
    sample = lax.broadcasted_iota(jnp.int32, (8, 128), 0) // 2
    result = []
    for shift in range(SAMPLES):
        rows = jnp.broadcast_to(weights[shift][0], (8, 128))
        for j in range(1, SAMPLES):
            rows = jnp.where(sample == j, weights[(j + shift) % SAMPLES][j], rows)
        result.append(rows)
    return result


def row_combine(x, per_shift):
    total = 0.0
    for shift in range(SAMPLES):
        total = total + rolled(x, shift) * per_shift[shift]
    return total


PIECES = 8


def fetch(source, held, arrived):
    pieces = arrived.shape[0]
    size = source.shape[0] // pieces
    copies = []
    for p in range(pieces):
        at = pl.ds(p * size, size)
        copies.append(pltpu.make_async_copy(source.at[at], held.at[at], arrived.at[p]))
    for copy in copies:
        copy.start()
    return copies


def second_of(tile_block):
    slots, owners = tile_block.shape
    tiles = owners * slots
    tile = lax.broadcasted_iota(jnp.int32, (tiles, slots), 0)
    slot = lax.broadcasted_iota(jnp.int32, (tiles, slots), 1)
    rows = jnp.dot(
        (tile % slots == slot).astype(jnp.float32),
        tile_block[...].astype(jnp.float32),
        preferred_element_type=jnp.float32,
    )
    tile = lax.broadcasted_iota(jnp.int32, (tiles, owners), 0)
    owner = lax.broadcasted_iota(jnp.int32, (tiles, owners), 1)
    return jnp.sum(jnp.where(tile // slots == owner, rows, 0.0), axis=1, keepdims=True)


def pack_body(right_sides, obs_var, tile_place, tile_block, lon, copies, mask_lon):
    slots, owners = tile_place.shape
    tiles = owners * slots
    owner = lax.broadcasted_iota(jnp.int32, (owners, tiles), 0)
    lane = lax.broadcasted_iota(jnp.int32, (owners, tiles), 1)
    spread_out = jnp.dot(
        tile_place[...].astype(jnp.float32),
        (lane // slots == owner).astype(jnp.float32),
        precision=precise,
        preferred_element_type=jnp.float32,
    )
    slot = lax.broadcasted_iota(jnp.int32, (slots, tiles), 0)
    lane = lax.broadcasted_iota(jnp.int32, (slots, tiles), 1)
    place = jnp.sum(jnp.where(lane % slots == slot, spread_out, 0.0), axis=0, keepdims=True)
    for k in range(SAMPLES):
        for b in range(2):
            copies[0, 2 * k + b : 2 * k + b + 1] = right_sides[b, k : k + 1]
    copies[0, 8:10] = obs_var[...]
    copies[0, 10:11] = place
    copies[0, 11:16] = jnp.zeros((5, tiles), jnp.float32)
    for d in range(1, copies.shape[0]):
        copies[d] = copies[0]
    mask_lon[0] = jnp.broadcast_to(second_of(tile_block), lon.shape)
    mask_lon[1] = lon[...]


def spread_tiles(vectors, held, copies, products, split):
    owners, slots = held.shape[:2]
    piece = owners // len(copies)
    for owner in range(owners):
        if owner % piece == 0:
            copies[owner // piece].wait()
        rows = vectors[owner, 0:8]
        lhs = rows.astype(jnp.bfloat16)
        if split:
            upper = lhs.astype(jnp.float32)
            lhs = jnp.concatenate([upper, rows - upper], axis=0).astype(jnp.bfloat16)
        for c in range(slots):
            r = jnp.dot(lhs, held[owner, c], preferred_element_type=jnp.float32)
            products[owner * slots + c] = r[:8] + r[8:] if split else r


def spread_end(products, mask_lon, by_column, by_tile):
    second = mask_lon[0] > 0.5
    width = by_column.shape[1]
    chunks = LON // width
    for k in range(SAMPLES):
        chosen = jnp.where(second, products[:, 2 * k + 1, :], products[:, 2 * k, :])
        mixed = jnp.dot(
            chosen, mask_lon[1], precision=precise, preferred_element_type=jnp.float32
        )
        by_tile[:, k * LON : (k + 1) * LON] = mixed.astype(jnp.bfloat16)
        turned = mixed.T.astype(jnp.bfloat16)
        by_column[k * chunks : (k + 1) * chunks] = turned.reshape(chunks, width, LON)


def first_body(
    everyone, mask_lon, footprint, by_column, by_tile, products, held, arrived
):
    copies = fetch(footprint, held, arrived)
    spread_tiles(everyone, held, copies, products, False)
    spread_end(products, mask_lon, by_column, by_tile)


def with_variance(image, everyone, vectors):
    block = lax.broadcasted_iota(jnp.int32, vectors.shape, 1) % 2
    variance = jnp.where(block == 0, everyone[:, 8:9, :], everyone[:, 9:10, :])
    return image + variance * vectors


def entries(ref):
    grid = range(SAMPLES)
    return [[ref[SAMPLES * k + j : SAMPLES * k + j + 1] for j in grid] for k in grid]


def keep(ref, matrix):
    for k in range(SAMPLES):
        for j in range(SAMPLES):
            ref[SAMPLES * k + j : SAMPLES * k + j + 1] = matrix[k][j]


def update_body(
    everyone, image_in, mask_lon, footprint,
    by_column, by_tile, direction, sizes, norm, products, held, arrived,
):
    copies = fetch(footprint, held, arrived)
    first = everyone[:, 0:8, :]
    image = with_variance(image_in[...], everyone, first)
    norm_now = row_gram(first, first)
    step_size = row_solve(row_gram(first, image), norm_now)
    residual = first - row_combine(image, row_weights(step_size))
    norm_next = row_gram(residual, residual)
    ratio = row_solve(norm_now, norm_next)
    direction[...] = residual + row_combine(first, row_weights(ratio))
    keep(sizes, step_size)
    keep(norm, norm_next)
    spread_tiles(direction, held, copies, products, True)
    spread_end(products, mask_lon, by_column, by_tile)


def build_body(
    me, everyone, time_cov, lat_cov,
    prior_out, time_part, row_part, tile_prior, hot, cols, times, sent,
):
    devices, tiles = everyone.shape[0], everyone.shape[2]
    steps_here = time_part.shape[0]
    at = lax.broadcasted_iota(jnp.int32, (LAT, tiles), 0)
    for kind, cov in ((0, time_cov), (1, lat_cov)):
        whole_cov = cov[...]
        upper = whole_cov.astype(jnp.bfloat16)
        lower = (whole_cov - upper.astype(jnp.float32)).astype(jnp.bfloat16)
        ones = []
        for d in range(devices):
            place = (everyone[d, 10:11, :] + 0.5).astype(jnp.int32)
            where = place // LAT + steps_here * d if kind == 0 else place % LAT
            one = (at == where).astype(jnp.float32)
            ones.append(one.astype(jnp.bfloat16))
            turned = one.T.astype(jnp.bfloat16)
            here = slice(d * tiles, (d + 1) * tiles)
            hot[kind, here, 0:LAT] = turned
            hot[kind, here, LAT : 2 * LAT] = turned
        picked = jnp.dot(
            jnp.concatenate([upper, lower], axis=0),
            jnp.concatenate(ones, axis=1),
            preferred_element_type=jnp.float32,
        )
        cols[kind] = picked.astype(jnp.bfloat16)
        both = picked[:LAT] + picked[LAT:]
        if kind == 0:
            times[...] = both
            mine = pl.ds(pl.multiple_of(me[0] * steps_here, steps_here), steps_here)
            time_part[...] = times[mine, :]
        else:
            row_part[...] = both

    rows = tile_prior.shape[0] // PIECES

    def sending(piece):
        block = pl.ds(pl.multiple_of(piece * rows, rows), rows)
        return pltpu.make_async_copy(
            tile_prior.at[block], prior_out.at[block], sent.at[piece]
        )

    @pl.loop(0, PIECES)
    def _(piece):
        block = pl.ds(pl.multiple_of(piece * rows, rows), rows)
        by_time = jnp.dot(hot[0, block, :], cols[0], preferred_element_type=jnp.float32)
        by_row = jnp.dot(hot[1, block, :], cols[1], preferred_element_type=jnp.float32)
        tile_prior[block, :] = (by_time * by_row).astype(jnp.bfloat16)
        sending(piece).start()

    for piece in range(PIECES):
        sending(piece).wait()


def mix_body(columns, tile_prior, *rest):
    mixed, total, held, arrived = rest[-4:]
    copies = fetch(tile_prior, held, arrived)
    devices, width, tiles = columns.shape
    part = devices // len(copies)
    for p, copy in enumerate(copies):
        at = range(p * part, (p + 1) * part)
        lhs = jnp.concatenate([columns[d] for d in at], axis=1)
        copy.wait()
        product = jnp.dot(
            lhs,
            held[p * part * tiles : (p + 1) * part * tiles],
            preferred_element_type=jnp.float32,
        )
        total[...] = product if p == 0 else total[...] + product
    for d in range(devices):
        mixed[d] = total[:, d * tiles : (d + 1) * tiles].astype(jnp.bfloat16)


def sum_body(terms, total, copies):
    value = jnp.sum(terms[...], axis=0)
    total[...] = value
    for d in range(copies.shape[0]):
        copies[d] = value


def collect_body(values, mask_lon, footprint, sums, rows):
    chunks = values.shape[0] // SAMPLES
    owners, slots = footprint.shape[:2]
    is_second = mask_lon[0] > 0.5
    for k in range(SAMPLES):
        turned = values[k * chunks : (k + 1) * chunks].reshape(LON, -1)
        turned = turned.astype(jnp.float32).T
        rows[:, 2 * k, :] = jnp.where(is_second, 0.0, turned)
        rows[:, 2 * k + 1, :] = jnp.where(is_second, turned, 0.0)
    for owner in range(owners):
        total = 0.0
        for c in range(slots):
            total = total + lax.dot_general(
                rows[owner * slots + c].astype(jnp.bfloat16),
                footprint[owner, c],
                (((1,), (1,)), ((), ())),
                preferred_element_type=jnp.float32,
            )
        sums[owner] = total


def apply_flux(time_part, row_part, source, out, ready, sent):
    steps = time_part.shape[0]
    pair = 2
    copies = []
    for step in range(0, steps, pair):
        dense = []
        for t in range(step, step + pair):
            dense.append((time_part[t : t + 1, :] * row_part[...]).astype(jnp.bfloat16))
        at = pl.ds(step * LAT, pair * LAT)
        ready[at] = jnp.dot(
            jnp.concatenate(dense, axis=0), source[...], preferred_element_type=jnp.float32
        )
        copy = pltpu.make_async_copy(ready.at[at], out.at[at], sent.at[step // pair])
        copy.start()
        copies.append(copy)
    for copy in copies:
        copy.wait()


def flux_first_body(
    sizes, time_part, row_part, gathered, out, token,
    ready, rows, held, row_arrived, arrived, sent, total,
):
    copies = fetch(gathered, held, arrived)
    row_copies = fetch(row_part, rows, row_arrived)
    size = entries(sizes)
    part = total.shape[0] // len(copies)
    for r, copy in enumerate(copies):
        copy.wait()
        at = slice(r * part, (r + 1) * part)
        for j in range(SAMPLES):
            value = 0.0
            for k in range(SAMPLES):
                piece = held[at, k * LON : (k + 1) * LON]
                value = value + piece.astype(jnp.float32) * size[k][j]
            total[at, j * LON : (j + 1) * LON] = value.astype(jnp.bfloat16)
    for copy in row_copies:
        copy.wait()
    apply_flux(time_part, rows, total, out, ready, sent)
    token[...] = ready[0:8, 0:128]


def flux_second_body(
    after, time_part, row_part, gathered, out,
    ready, rows, held, row_arrived, arrived, sent,
):
    del after
    row_copies = fetch(row_part, rows, row_arrived)
    copies = fetch(gathered, held, arrived)
    for copy in row_copies + copies:
        copy.wait()
    apply_flux(time_part, rows, held, out, ready, sent)


def last_body(
    me, everyone, image_in, direction, sizes, norm, flux_one, flux_two,
    answer, flux, one, two, ready, one_arrived, two_arrived, sent,
):
    two_copies = fetch(flux_two, two, two_arrived)
    one_copies = fetch(flux_one, one, one_arrived)
    second = direction[...]
    image = with_variance(image_in[...], everyone, second)
    size_two = row_solve(row_gram(second, image), entries(norm))
    own = row_combine(everyone[me[0], 0:8, :], row_weights(entries(sizes)))
    own = own + row_combine(direction[me[0]], row_weights(size_two))
    for k in range(SAMPLES):
        for b in range(2):
            answer[b, k : k + 1, :] = own[2 * k + b : 2 * k + b + 1]

    steps = ready.shape[0]
    piece = steps // len(one_copies)
    sending = []
    for t in range(steps):
        if t % piece == 0:
            two_copies[t // piece].wait()
            one_copies[t // piece].wait()
        at = slice(t * LAT, (t + 1) * LAT)
        parts = [two[at, k * LON : (k + 1) * LON] for k in range(SAMPLES)]
        for j in range(SAMPLES):
            value = one[at, j * LON : (j + 1) * LON]
            for k in range(SAMPLES):
                value = value + parts[k] * size_two[k][j]
            ready[t, :, j, :] = value
        copy = pltpu.make_async_copy(ready.at[t], flux.at[t], sent.at[t])
        copy.start()
        sending.append(copy)
    for copy in sending:
        copy.wait()


MIB = 1024 * 1024


def shape_of(shape, dtype):
    return jax.ShapeDtypeStruct(shape, dtype)


def cost(flops, moved):
    return pl.CostEstimate(flops=flops, bytes_accessed=moved, transcendentals=0)


def by_columns(
    right_sides, obs_var, footprint, tile_block, tile_place, time_cov, lat_cov, lon_cov
):
    devices = lax.axis_size("tm")
    me = lax.axis_index("tm").reshape(1).astype(jnp.int32)
    steps_here = time_cov.shape[0] // devices
    tiles = tile_block.size
    every_tile = devices * tiles
    columns = SAMPLES * LON
    width = columns // devices
    rows_here = steps_here * LAT
    f32, bf16 = jnp.float32, jnp.bfloat16

    vmem = pl.BlockSpec(memory_space=pltpu.VMEM)
    smem = pl.BlockSpec(memory_space=pltpu.SMEM)
    hbm = pl.BlockSpec(memory_space=pltpu.HBM)
    vector_shape = shape_of((devices, 8, BLOCK_OBS), f32)
    column_shape = shape_of((devices, width, tiles), bf16)
    tile_shape = shape_of((tiles, columns), bf16)
    small_shape = shape_of((SAMPLES * SAMPLES, 128), f32)
    field_shape = shape_of((rows_here, columns), f32)
    row_shape = shape_of((LAT, every_tile), f32)
    prior_shape = shape_of((every_tile, every_tile), bf16)
    flux_shape = shape_of((steps_here, LAT, SAMPLES, LON), f32)

    def flags(count):
        return pltpu.SemaphoreType.DMA((count,))

    products = pltpu.VMEM((tiles, 8, LON), f32)
    field = pltpu.VMEM(field_shape.shape, f32)
    gathered_held = pltpu.VMEM((every_tile, columns), bf16)
    prior_held = pltpu.VMEM(prior_shape.shape, bf16)
    spread_scratch = [products, pltpu.VMEM(footprint.shape, bf16), flags(PIECES)]
    flux_scratch = [field, pltpu.VMEM(row_shape.shape, f32), gathered_held]
    flux_scratch += [flags(1), flags(PIECES), flags(steps_here // 2)]
    tile_cost = cost(2 * 8 * footprint.size, footprint.size * 2)
    flux_cost = cost(2 * rows_here * every_tile * columns, every_tile * columns * 2)

    def call(body, in_specs, out_specs, out_shape, scratch, estimate, name, grant=53):
        return pl.pallas_call(
            body,
            in_specs=in_specs,
            out_specs=out_specs,
            out_shape=out_shape,
            scratch_shapes=scratch,
            compiler_params=pltpu.CompilerParams(vmem_limit_bytes=grant * MIB),
            cost_estimate=estimate,
            name=name,
        )

    def exchange(array):
        return lax.all_to_all(array, "tm", split_axis=0, concat_axis=0, tiled=True)

    packed, mask_lon = call(
        pack_body,
        [vmem] * 5,
        [vmem] * 2,
        [shape_of((devices, 16, 128), f32), shape_of((2, 128, 128), f32)],
        [],
        cost(0, 12 * MIB),
        "pack",
        59,
    )(right_sides, obs_var, tile_place.T, tile_block.T, lon_cov)
    everyone = exchange(packed)
    by_column, by_tile = call(
        first_body,
        [vmem, vmem, hbm],
        [vmem] * 2,
        [column_shape, tile_shape],
        spread_scratch,
        tile_cost,
        "spread_first",
    )(everyone, mask_lon, footprint)
    gathered_one = lax.all_gather(by_tile, "tm", axis=0, tiled=True)

    tile_prior, time_part, row_part = call(
        build_body,
        [smem] + [vmem] * 3,
        [hbm, vmem, vmem],
        [prior_shape, shape_of((steps_here, every_tile), f32), row_shape],
        [
            prior_held,
            pltpu.VMEM((2, every_tile, 2 * LAT), bf16),
            pltpu.VMEM((2, 2 * LAT, every_tile), bf16),
            pltpu.VMEM((LAT, every_tile), f32),
            flags(PIECES),
        ],
        cost(4 * every_tile * every_tile * 256, every_tile * every_tile * 2),
        "build_prior",
    )(me, everyone, time_cov, lat_cov)

    def prior(by_column, *after):
        mixed = call(
            mix_body,
            [vmem, hbm] + [hbm] * len(after),
            vmem,
            column_shape,
            [pltpu.VMEM((width, every_tile), f32), prior_held, flags(PIECES)],
            cost(2 * width * every_tile**2, every_tile**2 * 2),
            "mix_columns",
        )(exchange(by_column), tile_prior, *after)
        return exchange(mixed)

    def collect(values):
        sums = call(
            collect_body, [vmem] * 3, vmem, vector_shape, [products], tile_cost, "collect", 48
        )(values, mask_lon, footprint)
        own, copies = call(
            sum_body,
            [vmem],
            [vmem] * 2,
            [shape_of((8, BLOCK_OBS), f32), vector_shape],
            [],
            cost(0, 4 * MIB),
            "sum_terms",
        )(exchange(sums))
        return own, exchange(copies)

    _, image = collect(prior(by_column))
    by_column, by_tile, direction, sizes, norm = call(
        update_body,
        [vmem] * 3 + [hbm],
        [vmem] * 5,
        [column_shape, tile_shape, vector_shape, small_shape, small_shape],
        spread_scratch,
        tile_cost,
        "update_spread",
    )(everyone, image, mask_lon, footprint)
    gathered_two = lax.all_gather(by_tile, "tm", axis=0, tiled=True)
    flux_one, token = call(
        flux_first_body,
        [vmem, vmem, hbm, hbm],
        [hbm, vmem],
        [field_shape, shape_of((8, 128), f32)],
        flux_scratch + [gathered_held],
        flux_cost,
        "flux_first",
        59,
    )(sizes, time_part, row_part, gathered_one)

    own_image, image = collect(prior(by_column, token))
    flux_two = call(
        flux_second_body,
        [hbm, vmem, hbm, hbm],
        hbm,
        field_shape,
        flux_scratch,
        flux_cost,
        "flux_second",
        59,
    )(own_image, time_part, row_part, gathered_two)

    answer, flux = call(
        last_body,
        [smem] + [vmem] * 5 + [hbm] * 2,
        [vmem, hbm],
        [shape_of(right_sides.shape, f32), flux_shape],
        [field, field, pltpu.VMEM(flux_shape.shape, f32), flags(4), flags(4), flags(steps_here)],
        cost(1 << 20, 6 << 20),
        "last",
    )(me, everyone, image, direction, sizes, norm, flux_one, flux_two)
    return (answer, flux)


def local(right_sides, obs_var, footprint, tile_block, tile_place, *covariances):
    devices = lax.axis_size("tm")
    tiles = tile_block.size
    fits = devices * tiles <= 2048 and devices % 4 == 0 and tiles == 128
    fits = fits and right_sides.shape[0] == 2 and (SAMPLES * LON) % (32 * devices) == 0
    fits = fits and (covariances[0].shape[0] // devices) % 4 == 0
    plan = by_columns if fits else by_gather
    return plan(right_sides, obs_var, footprint, tile_block, tile_place, *covariances)


def solution(mesh):
    in_specs = (
        P(("grp", "tm"), None, None),
        P(("grp", "tm"), None),
        P(("grp", "tm"), None, None, None),
        P(("grp", "tm"), None),
        P(("grp", "tm"), None),
        P(),
        P(),
        P(),
    )
    out_specs = (P(("grp", "tm"), None, None), P(("grp", "tm"), None, None, None))
    return jax.shard_map(local, mesh=mesh, in_specs=in_specs, out_specs=out_specs, check_vma=False)
```

```python
import jax
import jax.numpy as jnp
from jax import lax
from jax.experimental import pallas as pl
from jax.experimental.pallas import tpu as pltpu
from jax.sharding import PartitionSpec as P

LAT = 128
LON = 128
BLOCK_OBS = 128
SAMPLES = 4
ITERS = 2


precise = lax.Precision.HIGHEST


def solve_spd(matrix, target):
    factor = jnp.linalg.cholesky(matrix)
    halfway = lax.linalg.triangular_solve(factor, target, left_side=True, lower=True)
    return lax.linalg.triangular_solve(
        factor, halfway, left_side=True, lower=True, transpose_a=True
    )


def combine(vectors, weights):
    return jnp.einsum("nks,kj->njs", vectors, weights, precision=precise)


def gram(left, right):
    return jnp.einsum("nks,njs->kj", left, right, precision=precise)


def to_all(array):
    devices = lax.axis_size("tm")
    copies = jnp.broadcast_to(array[None], (devices,) + array.shape)
    return lax.all_to_all(copies, "tm", split_axis=0, concat_axis=0, tiled=True)


def by_gather(
    right_sides, obs_var, footprint, tile_block, tile_place, time_cov, lat_cov, lon_cov
):
    devices = lax.axis_size("tm")
    me = lax.axis_index("tm")
    owned = right_sides.shape[0]
    blocks = devices * owned
    steps_here = time_cov.shape[0] // devices
    slots = tile_block.shape[1]
    tiles = devices * slots
    rows_here = steps_here * LAT
    owner_base = (jnp.arange(devices, dtype=jnp.int32) * owned)[:, None]
    requests = owner_base + tile_block

    packed = jnp.concatenate(
        [
            right_sides.reshape(-1, 128),
            obs_var.reshape(-1, 128),
            tile_place.astype(jnp.float32).reshape(-1, 128),
        ]
    )
    everyone = to_all(packed)
    at = owned * SAMPLES
    rhs = everyone[:, :at].reshape(blocks, SAMPLES, BLOCK_OBS)
    variance = everyone[:, at : at + owned].reshape(blocks, BLOCK_OBS)
    places = everyone[:, at + owned :].reshape(devices, tiles).astype(jnp.int32)
    times = (places // LAT + steps_here * jnp.arange(devices, dtype=jnp.int32)[:, None]).reshape(-1)
    rows = (places % LAT).reshape(-1)
    time_hot = (jnp.arange(time_cov.shape[0])[:, None] == times[None, :]).astype(jnp.float32)
    row_hot = (jnp.arange(LAT)[:, None] == rows[None, :]).astype(jnp.float32)
    my_times = lax.dynamic_slice_in_dim(time_cov, me * steps_here, steps_here, 0)
    time_part = jnp.dot(my_times, time_hot, precision=precise)
    row_part = jnp.dot(lat_cov, row_hot, precision=precise)
    dense = (time_part[:, None, :] * row_part[None, :, :]).astype(jnp.bfloat16)
    dense = dense.reshape(rows_here, devices * tiles)
    mine = jnp.take(dense, tile_place.reshape(-1), axis=0)

    def spread(vectors):
        chosen = jnp.take(vectors.astype(jnp.bfloat16), requests, axis=0)
        contrib = jnp.einsum(
            "ocks,ocsl->ockl", chosen, footprint, preferred_element_type=jnp.float32
        )
        contrib = contrib.astype(jnp.bfloat16).reshape(tiles, SAMPLES * LON)
        return lax.all_gather(contrib, "tm", axis=0, tiled=True)

    def collect(gathered):
        field = jnp.dot(mine, gathered, preferred_element_type=jnp.float32)
        field = jnp.dot(field.reshape(-1, LON), lon_cov, precision=precise)
        picked = field.astype(jnp.bfloat16).reshape(devices, slots, SAMPLES, LON)
        partial = jnp.einsum(
            "ockl,ocsl->ocks", picked, footprint, preferred_element_type=jnp.float32
        )
        block_range = jnp.arange(owned, dtype=jnp.int32)
        selector = (tile_block[:, :, None] == block_range).astype(jnp.float32)
        summed = jnp.einsum("ocb,ocks->obks", selector, partial, precision=precise)
        terms = lax.all_to_all(
            summed.reshape(devices, owned * SAMPLES, BLOCK_OBS), "tm", 0, 0, tiled=True
        )
        return to_all(terms.sum(0)).reshape(blocks, SAMPLES, BLOCK_OBS)

    solution = jnp.zeros_like(rhs)
    residual = rhs
    direction = rhs
    norm_now = gram(rhs, rhs)
    gathers, sizes = [], []
    for step in range(ITERS):
        gathered = spread(direction)
        image = collect(gathered) + variance[:, None, :] * direction
        step_size = solve_spd(gram(direction, image), norm_now)
        gathers.append(gathered)
        sizes.append(step_size)
        solution = solution + combine(direction, step_size)
        if step + 1 == ITERS:
            break
        residual = residual - combine(image, step_size)
        norm_next = gram(residual, residual)
        mix_ratio = solve_spd(norm_now, norm_next)
        direction = residual + combine(direction, mix_ratio)
        norm_now = norm_next

    def mix(gathered, size):
        whole = gathered.astype(jnp.float32).reshape(-1, SAMPLES, LON)
        return jnp.einsum("tkl,kj->tjl", whole, size, precision=precise)

    def apply_dense(gathered):
        return jnp.dot(dense, gathered, preferred_element_type=jnp.float32)

    if rows_here < devices * tiles // 4:
        flux = sum(mix(apply_dense(g), size) for g, size in zip(gathers, sizes))
    else:
        total = sum(mix(g, size) for g, size in zip(gathers, sizes))
        flux = apply_dense(total.astype(jnp.bfloat16).reshape(-1, SAMPLES * LON))
    flux = jnp.dot(flux.reshape(-1, LON), lon_cov, precision=precise)
    mine_now = lax.dynamic_slice_in_dim(solution, me * owned, owned, 0)
    return (mine_now, flux.reshape(steps_here, LAT, SAMPLES, LON))


def rolled(x, shift):
    return x if shift == 0 else pltpu.roll(x, 8 - 2 * shift, x.ndim - 2)


def row_gram(left, right):
    entry = [[None] * SAMPLES for _ in range(SAMPLES)]
    for shift in range(SAMPLES):
        product = jnp.sum(left * rolled(right, shift), axis=0)
        total = jnp.broadcast_to(jnp.sum(product, axis=1, keepdims=True), product.shape)
        for k in range(SAMPLES):
            pair = total[2 * k : 2 * k + 1] + total[2 * k + 1 : 2 * k + 2]
            entry[k][(k + shift) % SAMPLES] = pair
    return entry


def row_solve(matrix, target):
    size = range(SAMPLES)
    sym = [[0.5 * (matrix[i][j] + matrix[j][i]) for j in size] for i in size]
    low = [[None] * SAMPLES for _ in size]
    scaled = [[None] * SAMPLES for _ in size]
    inverse = []
    for j in size:
        pivot = sym[j][j]
        for p in range(j):
            pivot = pivot - low[j][p] * scaled[j][p]
        inverse.append(1.0 / pivot)
        for i in range(j + 1, SAMPLES):
            value = sym[i][j]
            for p in range(j):
                value = value - scaled[i][p] * low[j][p]
            scaled[i][j] = value
            low[i][j] = value * inverse[j]
    out = [[None] * SAMPLES for _ in size]
    for c in size:
        part = []
        for i in size:
            value = target[i][c]
            for p in range(i):
                value = value - low[i][p] * part[p]
            part.append(value)
        for i in reversed(size):
            value = part[i] * inverse[i]
            for p in range(i + 1, SAMPLES):
                value = value - low[p][i] * out[p][c]
            out[i][c] = value
    return out


def row_weights(weights):
    sample = lax.broadcasted_iota(jnp.int32, (8, 128), 0) // 2
    result = []
    for shift in range(SAMPLES):
        rows = jnp.broadcast_to(weights[shift][0], (8, 128))
        for j in range(1, SAMPLES):
            rows = jnp.where(sample == j, weights[(j + shift) % SAMPLES][j], rows)
        result.append(rows)
    return result


def row_combine(x, per_shift):
    total = 0.0
    for shift in range(SAMPLES):
        total = total + rolled(x, shift) * per_shift[shift]
    return total


PIECES = 8


def fetch(source, held, arrived):
    pieces = arrived.shape[0]
    size = source.shape[0] // pieces
    copies = []
    for p in range(pieces):
        at = pl.ds(p * size, size)
        copies.append(pltpu.make_async_copy(source.at[at], held.at[at], arrived.at[p]))
    for copy in copies:
        copy.start()
    return copies


def second_of(tile_block):
    slots, owners = tile_block.shape
    tiles = owners * slots
    tile = lax.broadcasted_iota(jnp.int32, (tiles, slots), 0)
    slot = lax.broadcasted_iota(jnp.int32, (tiles, slots), 1)
    rows = jnp.dot(
        (tile % slots == slot).astype(jnp.float32),
        tile_block[...].astype(jnp.float32),
        preferred_element_type=jnp.float32,
    )
    tile = lax.broadcasted_iota(jnp.int32, (tiles, owners), 0)
    owner = lax.broadcasted_iota(jnp.int32, (tiles, owners), 1)
    return jnp.sum(jnp.where(tile // slots == owner, rows, 0.0), axis=1, keepdims=True)


def pack_body(right_sides, obs_var, tile_place, tile_block, lon, copies, mask_lon):
    slots, owners = tile_place.shape
    tiles = owners * slots
    owner = lax.broadcasted_iota(jnp.int32, (owners, tiles), 0)
    lane = lax.broadcasted_iota(jnp.int32, (owners, tiles), 1)
    spread_out = jnp.dot(
        tile_place[...].astype(jnp.float32),
        (lane // slots == owner).astype(jnp.float32),
        precision=precise,
        preferred_element_type=jnp.float32,
    )
    slot = lax.broadcasted_iota(jnp.int32, (slots, tiles), 0)
    lane = lax.broadcasted_iota(jnp.int32, (slots, tiles), 1)
    place = jnp.sum(jnp.where(lane % slots == slot, spread_out, 0.0), axis=0, keepdims=True)
    for k in range(SAMPLES):
        for b in range(2):
            copies[0, 2 * k + b : 2 * k + b + 1] = right_sides[b, k : k + 1]
    copies[0, 8:10] = obs_var[...]
    copies[0, 10:11] = place
    copies[0, 11:16] = jnp.zeros((5, tiles), jnp.float32)
    for d in range(1, copies.shape[0]):
        copies[d] = copies[0]
    mask_lon[0] = jnp.broadcast_to(second_of(tile_block), lon.shape)
    mask_lon[1] = lon[...]


def spread_tiles(vectors, held, copies, products, split):
    owners, slots = held.shape[:2]
    piece = owners // len(copies)
    for owner in range(owners):
        if owner % piece == 0:
            copies[owner // piece].wait()
        rows = vectors[owner, 0:8]
        lhs = rows.astype(jnp.bfloat16)
        if split:
            upper = lhs.astype(jnp.float32)
            lhs = jnp.concatenate([upper, rows - upper], axis=0).astype(jnp.bfloat16)
        for c in range(slots):
            r = jnp.dot(lhs, held[owner, c], preferred_element_type=jnp.float32)
            products[owner * slots + c] = r[:8] + r[8:] if split else r


def spread_end(products, mask_lon, by_column, by_tile):
    second = mask_lon[0] > 0.5
    width = by_column.shape[1]
    chunks = LON // width
    for k in range(SAMPLES):
        chosen = jnp.where(second, products[:, 2 * k + 1, :], products[:, 2 * k, :])
        mixed = jnp.dot(
            chosen, mask_lon[1], precision=precise, preferred_element_type=jnp.float32
        )
        by_tile[:, k * LON : (k + 1) * LON] = mixed.astype(jnp.bfloat16)
        turned = mixed.T.astype(jnp.bfloat16)
        by_column[k * chunks : (k + 1) * chunks] = turned.reshape(chunks, width, LON)


def first_body(
    everyone, mask_lon, footprint, by_column, by_tile, products, held, arrived
):
    copies = fetch(footprint, held, arrived)
    spread_tiles(everyone, held, copies, products, False)
    spread_end(products, mask_lon, by_column, by_tile)


def with_variance(image, everyone, vectors):
    block = lax.broadcasted_iota(jnp.int32, vectors.shape, 1) % 2
    variance = jnp.where(block == 0, everyone[:, 8:9, :], everyone[:, 9:10, :])
    return image + variance * vectors


def entries(ref):
    grid = range(SAMPLES)
    return [[ref[SAMPLES * k + j : SAMPLES * k + j + 1] for j in grid] for k in grid]


def keep(ref, matrix):
    for k in range(SAMPLES):
        for j in range(SAMPLES):
            ref[SAMPLES * k + j : SAMPLES * k + j + 1] = matrix[k][j]


def update_body(
    everyone, image_in, mask_lon, footprint, after,
    by_column, by_tile, direction, sizes, norm, products, held, arrived,
):
    del after
    copies = fetch(footprint, held, arrived)
    first = everyone[:, 0:8, :]
    image = with_variance(image_in[...], everyone, first)
    norm_now = row_gram(first, first)
    step_size = row_solve(row_gram(first, image), norm_now)
    residual = first - row_combine(image, row_weights(step_size))
    norm_next = row_gram(residual, residual)
    ratio = row_solve(norm_now, norm_next)
    direction[...] = residual + row_combine(first, row_weights(ratio))
    keep(sizes, step_size)
    keep(norm, norm_next)
    spread_tiles(direction, held, copies, products, True)
    spread_end(products, mask_lon, by_column, by_tile)


def build_body(
    me, everyone, time_cov, lat_cov,
    prior_out, parts_out, tile_prior, hot, cols, times, parts, sent, parts_sent,
):
    devices, tiles = everyone.shape[0], everyone.shape[2]
    steps_here = parts.shape[0] - LAT
    at = lax.broadcasted_iota(jnp.int32, (LAT, tiles), 0)
    for kind, cov in ((0, time_cov), (1, lat_cov)):
        whole_cov = cov[...]
        upper = whole_cov.astype(jnp.bfloat16)
        lower = (whole_cov - upper.astype(jnp.float32)).astype(jnp.bfloat16)
        ones = []
        for d in range(devices):
            place = (everyone[d, 10:11, :] + 0.5).astype(jnp.int32)
            where = place // LAT + steps_here * d if kind == 0 else place % LAT
            one = (at == where).astype(jnp.float32)
            ones.append(one.astype(jnp.bfloat16))
            turned = one.T.astype(jnp.bfloat16)
            here = slice(d * tiles, (d + 1) * tiles)
            hot[kind, here, 0:LAT] = turned
            hot[kind, here, LAT : 2 * LAT] = turned
        picked = jnp.dot(
            jnp.concatenate([upper, lower], axis=0),
            jnp.concatenate(ones, axis=1),
            preferred_element_type=jnp.float32,
        )
        cols[kind] = picked.astype(jnp.bfloat16)
        both = picked[:LAT] + picked[LAT:]
        if kind == 0:
            times[...] = both
            mine = pl.ds(pl.multiple_of(me[0] * steps_here, steps_here), steps_here)
            parts[LAT:] = times[mine, :]
        else:
            parts[:LAT] = both

    parts_copy = pltpu.make_async_copy(parts, parts_out, parts_sent)
    parts_copy.start()
    rows = tile_prior.shape[0] // PIECES

    def sending(piece):
        block = pl.ds(pl.multiple_of(piece * rows, rows), rows)
        return pltpu.make_async_copy(
            tile_prior.at[block], prior_out.at[block], sent.at[piece]
        )

    @pl.loop(0, PIECES)
    def _(piece):
        block = pl.ds(pl.multiple_of(piece * rows, rows), rows)
        by_time = jnp.dot(hot[0, block, :], cols[0], preferred_element_type=jnp.float32)
        by_row = jnp.dot(hot[1, block, :], cols[1], preferred_element_type=jnp.float32)
        tile_prior[block, :] = (by_time * by_row).astype(jnp.bfloat16)
        sending(piece).start()

    parts_copy.wait()
    for piece in range(PIECES):
        sending(piece).wait()


def mix_body(columns, tile_prior, *rest):
    mixed, total, held, arrived = rest[-4:]
    copies = fetch(tile_prior, held, arrived)
    devices, width, tiles = columns.shape
    part = devices // len(copies)
    for p, copy in enumerate(copies):
        at = range(p * part, (p + 1) * part)
        lhs = jnp.concatenate([columns[d] for d in at], axis=1)
        copy.wait()
        product = jnp.dot(
            lhs,
            held[p * part * tiles : (p + 1) * part * tiles],
            preferred_element_type=jnp.float32,
        )
        total[...] = product if p == 0 else total[...] + product
    for d in range(devices):
        mixed[d] = total[:, d * tiles : (d + 1) * tiles].astype(jnp.bfloat16)


def sum_body(terms, total, copies):
    value = jnp.sum(terms[...], axis=0)
    total[...] = value
    for d in range(copies.shape[0]):
        copies[d] = value


def collect_body(values, mask_lon, footprint, sums, rows):
    chunks = values.shape[0] // SAMPLES
    owners, slots = footprint.shape[:2]
    is_second = mask_lon[0] > 0.5
    for k in range(SAMPLES):
        turned = values[k * chunks : (k + 1) * chunks].reshape(LON, -1)
        turned = turned.astype(jnp.float32).T
        rows[:, 2 * k, :] = jnp.where(is_second, 0.0, turned)
        rows[:, 2 * k + 1, :] = jnp.where(is_second, turned, 0.0)
    for owner in range(owners):
        total = 0.0
        for c in range(slots):
            total = total + lax.dot_general(
                rows[owner * slots + c].astype(jnp.bfloat16),
                footprint[owner, c],
                (((1,), (1,)), ((), ())),
                preferred_element_type=jnp.float32,
            )
        sums[owner] = total


def flux_product_body(
    after, parts, gathered, out, token,
    ready, parts_held, held, parts_arrived, arrived, sent,
):
    del after
    (parts_copy,) = fetch(parts, parts_held, parts_arrived)
    copies = fetch(gathered, held, arrived)
    steps = parts_held.shape[0] - LAT
    half = held.shape[0] // 2
    pair = 2
    parts_copy.wait()
    sending = []
    for step in range(0, steps, pair):
        dense = []
        for t in range(step, step + pair):
            times = parts_held[LAT + t : LAT + t + 1, :]
            dense.append((times * parts_held[:LAT]).astype(jnp.bfloat16))
        dense = jnp.concatenate(dense, axis=0)
        at = pl.ds(step * LAT, pair * LAT)
        if step == 0:
            total = 0.0
            for h in range(2):
                for copy in copies[h * PIECES // 2 : (h + 1) * PIECES // 2]:
                    copy.wait()
                total = total + jnp.dot(
                    dense[:, h * half : (h + 1) * half],
                    held[h * half : (h + 1) * half],
                    preferred_element_type=jnp.float32,
                )
            ready[at] = total
            token[...] = ready[0:8, 0:128]
        else:
            ready[at] = jnp.dot(dense, held[...], preferred_element_type=jnp.float32)
        copy = pltpu.make_async_copy(ready.at[at], out.at[at], sent.at[step // pair])
        copy.start()
        sending.append(copy)
    for copy in sending:
        copy.wait()


def flux_first_body(sizes, product, out, token, ready, held, arrived, sent):
    copies = fetch(product, held, arrived)
    size = entries(sizes)
    part = held.shape[0] // len(copies)
    sending = []
    for p, copy in enumerate(copies):
        copy.wait()
        at = pl.ds(p * part, part)
        pieces = [held[at, k * LON : (k + 1) * LON] for k in range(SAMPLES)]
        for j in range(SAMPLES):
            value = 0.0
            for k in range(SAMPLES):
                value = value + pieces[k] * size[k][j]
            ready[at, j * LON : (j + 1) * LON] = value
        copy = pltpu.make_async_copy(ready.at[at], out.at[at], sent.at[p])
        copy.start()
        sending.append(copy)
    token[...] = ready[0:8, 0:128]
    for copy in sending:
        copy.wait()


def last_body(
    me, everyone, image_in, direction, sizes, norm, flux_one, flux_two,
    answer, flux, one, two, ready, one_arrived, two_arrived, sent,
):
    two_copies = fetch(flux_two, two, two_arrived)
    one_copies = fetch(flux_one, one, one_arrived)
    second = direction[...]
    image = with_variance(image_in[...], everyone, second)
    size_two = row_solve(row_gram(second, image), entries(norm))
    own = row_combine(everyone[me[0], 0:8, :], row_weights(entries(sizes)))
    own = own + row_combine(direction[me[0]], row_weights(size_two))
    for k in range(SAMPLES):
        for b in range(2):
            answer[b, k : k + 1, :] = own[2 * k + b : 2 * k + b + 1]

    steps = ready.shape[0]
    piece = steps // len(one_copies)
    sending = []
    for t in range(steps):
        if t % piece == 0:
            two_copies[t // piece].wait()
            one_copies[t // piece].wait()
        at = slice(t * LAT, (t + 1) * LAT)
        parts = [two[at, k * LON : (k + 1) * LON] for k in range(SAMPLES)]
        for j in range(SAMPLES):
            value = one[at, j * LON : (j + 1) * LON]
            for k in range(SAMPLES):
                value = value + parts[k] * size_two[k][j]
            ready[t, :, j, :] = value
        copy = pltpu.make_async_copy(ready.at[t], flux.at[t], sent.at[t])
        copy.start()
        sending.append(copy)
    for copy in sending:
        copy.wait()


MIB = 1024 * 1024


def shape_of(shape, dtype):
    return jax.ShapeDtypeStruct(shape, dtype)


def cost(flops, moved):
    return pl.CostEstimate(flops=flops, bytes_accessed=moved, transcendentals=0)


def by_columns(
    right_sides, obs_var, footprint, tile_block, tile_place, time_cov, lat_cov, lon_cov
):
    devices = lax.axis_size("tm")
    me = lax.axis_index("tm").reshape(1).astype(jnp.int32)
    steps_here = time_cov.shape[0] // devices
    tiles = tile_block.size
    every_tile = devices * tiles
    columns = SAMPLES * LON
    width = columns // devices
    rows_here = steps_here * LAT
    f32, bf16 = jnp.float32, jnp.bfloat16

    vmem = pl.BlockSpec(memory_space=pltpu.VMEM)
    smem = pl.BlockSpec(memory_space=pltpu.SMEM)
    hbm = pl.BlockSpec(memory_space=pltpu.HBM)
    vector_shape = shape_of((devices, 8, BLOCK_OBS), f32)
    column_shape = shape_of((devices, width, tiles), bf16)
    tile_shape = shape_of((tiles, columns), bf16)
    small_shape = shape_of((SAMPLES * SAMPLES, 128), f32)
    field_shape = shape_of((rows_here, columns), f32)
    parts_shape = shape_of((LAT + steps_here, every_tile), f32)
    token_shape = shape_of((8, 128), f32)
    prior_shape = shape_of((every_tile, every_tile), bf16)
    flux_shape = shape_of((steps_here, LAT, SAMPLES, LON), f32)

    def flags(count):
        return pltpu.SemaphoreType.DMA((count,))

    products = pltpu.VMEM((tiles, 8, LON), f32)
    field = pltpu.VMEM(field_shape.shape, f32)
    gathered_held = pltpu.VMEM((every_tile, columns), bf16)
    prior_held = pltpu.VMEM(prior_shape.shape, bf16)
    spread_scratch = [products, pltpu.VMEM(footprint.shape, bf16), flags(PIECES)]
    flux_scratch = [field, pltpu.VMEM(parts_shape.shape, f32), gathered_held]
    flux_scratch += [flags(1), flags(PIECES), flags(steps_here // 2)]
    tile_cost = cost(2 * 8 * footprint.size, footprint.size * 2)
    flux_cost = cost(2 * rows_here * every_tile * columns, every_tile * columns * 2)

    def call(body, in_specs, out_specs, out_shape, scratch, estimate, name, grant=53):
        return pl.pallas_call(
            body,
            in_specs=in_specs,
            out_specs=out_specs,
            out_shape=out_shape,
            scratch_shapes=scratch,
            compiler_params=pltpu.CompilerParams(vmem_limit_bytes=grant * MIB),
            cost_estimate=estimate,
            name=name,
        )

    def exchange(array):
        return lax.all_to_all(array, "tm", split_axis=0, concat_axis=0, tiled=True)

    packed, mask_lon = call(
        pack_body,
        [vmem] * 5,
        [vmem] * 2,
        [shape_of((devices, 16, 128), f32), shape_of((2, 128, 128), f32)],
        [],
        cost(0, 12 * MIB),
        "pack",
        59,
    )(right_sides, obs_var, tile_place.T, tile_block.T, lon_cov)
    everyone = exchange(packed)
    by_column, by_tile = call(
        first_body,
        [vmem, vmem, hbm],
        [vmem] * 2,
        [column_shape, tile_shape],
        spread_scratch,
        tile_cost,
        "spread_first",
    )(everyone, mask_lon, footprint)
    gathered_one = lax.all_gather(by_tile, "tm", axis=0, tiled=True)

    tile_prior, parts = call(
        build_body,
        [smem] + [vmem] * 3,
        [hbm, hbm],
        [prior_shape, parts_shape],
        [
            prior_held,
            pltpu.VMEM((2, every_tile, 2 * LAT), bf16),
            pltpu.VMEM((2, 2 * LAT, every_tile), bf16),
            pltpu.VMEM((LAT, every_tile), f32),
            pltpu.VMEM(parts_shape.shape, f32),
            flags(PIECES),
            pltpu.SemaphoreType.DMA,
        ],
        cost(4 * every_tile * every_tile * 256, every_tile * every_tile * 2),
        "build_prior",
    )(me, everyone, time_cov, lat_cov)

    def flux_product(after, gathered):
        return call(
            flux_product_body,
            [hbm, hbm, hbm],
            [hbm, vmem],
            [field_shape, token_shape],
            flux_scratch,
            flux_cost,
            "flux_product",
        )(after, parts, gathered)

    def prior(by_column, *after):
        mixed = call(
            mix_body,
            [vmem, hbm] + [hbm] * len(after),
            vmem,
            column_shape,
            [pltpu.VMEM((width, every_tile), f32), prior_held, flags(PIECES)],
            cost(2 * width * every_tile**2, every_tile**2 * 2),
            "mix_columns",
        )(exchange(by_column), tile_prior, *after)
        return exchange(mixed)

    def collect(values):
        sums = call(
            collect_body, [vmem] * 3, vmem, vector_shape, [products], tile_cost, "collect", 48
        )(values, mask_lon, footprint)
        own, copies = call(
            sum_body,
            [vmem],
            [vmem] * 2,
            [shape_of((8, BLOCK_OBS), f32), vector_shape],
            [],
            cost(0, 4 * MIB),
            "sum_terms",
        )(exchange(sums))
        return own, exchange(copies)

    own_image, image = collect(prior(by_column))
    product_one, token = flux_product(own_image, gathered_one)
    by_column, by_tile, direction, sizes, norm = call(
        update_body,
        [vmem] * 3 + [hbm] * 2,
        [vmem] * 5,
        [column_shape, tile_shape, vector_shape, small_shape, small_shape],
        spread_scratch,
        tile_cost,
        "update_spread",
    )(everyone, image, mask_lon, footprint, token)
    gathered_two = lax.all_gather(by_tile, "tm", axis=0, tiled=True)
    flux_one, token = call(
        flux_first_body,
        [vmem, hbm],
        [hbm, vmem],
        [field_shape, token_shape],
        [field, field, flags(4), flags(4)],
        cost(1 << 24, 4 * MIB),
        "flux_first",
    )(sizes, product_one)

    own_image, image = collect(prior(by_column, token))
    flux_two, _ = flux_product(own_image, gathered_two)

    answer, flux = call(
        last_body,
        [smem] + [vmem] * 5 + [hbm] * 2,
        [vmem, hbm],
        [shape_of(right_sides.shape, f32), flux_shape],
        [field, field, pltpu.VMEM(flux_shape.shape, f32), flags(4), flags(4), flags(steps_here)],
        cost(1 << 20, 6 << 20),
        "last",
    )(me, everyone, image, direction, sizes, norm, flux_one, flux_two)
    return (answer, flux)


def local(right_sides, obs_var, footprint, tile_block, tile_place, *covariances):
    devices = lax.axis_size("tm")
    tiles = tile_block.size
    fits = devices * tiles <= 2048 and devices % 4 == 0 and tiles == 128
    fits = fits and right_sides.shape[0] == 2 and (SAMPLES * LON) % (32 * devices) == 0
    fits = fits and (covariances[0].shape[0] // devices) % 4 == 0
    plan = by_columns if fits else by_gather
    return plan(right_sides, obs_var, footprint, tile_block, tile_place, *covariances)


def solution(mesh):
    in_specs = (
        P(("grp", "tm"), None, None),
        P(("grp", "tm"), None),
        P(("grp", "tm"), None, None, None),
        P(("grp", "tm"), None),
        P(("grp", "tm"), None),
        P(),
        P(),
        P(),
    )
    out_specs = (P(("grp", "tm"), None, None), P(("grp", "tm"), None, None, None))
    return jax.shard_map(local, mesh=mesh, in_specs=in_specs, out_specs=out_specs, check_vma=False)
```

```python
import functools

import jax
import jax.numpy as jnp
from jax import lax
from jax.experimental import pallas as pl
from jax.experimental.pallas import tpu as pltpu
from jax.sharding import PartitionSpec as P

LAT = 128
LON = 128
BLOCK_OBS = 128
SAMPLES = 4
ITERS = 2


precise = lax.Precision.HIGHEST


def solve_spd(matrix, target):
    factor = jnp.linalg.cholesky(matrix)
    halfway = lax.linalg.triangular_solve(factor, target, left_side=True, lower=True)
    return lax.linalg.triangular_solve(
        factor, halfway, left_side=True, lower=True, transpose_a=True
    )


def combine(vectors, weights):
    return jnp.einsum("nks,kj->njs", vectors, weights, precision=precise)


def gram(left, right):
    return jnp.einsum("nks,njs->kj", left, right, precision=precise)


def to_all(array):
    devices = lax.axis_size("tm")
    copies = jnp.broadcast_to(array[None], (devices,) + array.shape)
    return lax.all_to_all(copies, "tm", split_axis=0, concat_axis=0, tiled=True)


def by_gather(
    right_sides, obs_var, footprint, tile_block, tile_place, time_cov, lat_cov, lon_cov
):
    devices = lax.axis_size("tm")
    me = lax.axis_index("tm")
    owned = right_sides.shape[0]
    blocks = devices * owned
    steps_here = time_cov.shape[0] // devices
    slots = tile_block.shape[1]
    tiles = devices * slots
    rows_here = steps_here * LAT
    owner_base = (jnp.arange(devices, dtype=jnp.int32) * owned)[:, None]
    requests = owner_base + tile_block

    packed = jnp.concatenate(
        [
            right_sides.reshape(-1, 128),
            obs_var.reshape(-1, 128),
            tile_place.astype(jnp.float32).reshape(-1, 128),
        ]
    )
    everyone = to_all(packed)
    at = owned * SAMPLES
    rhs = everyone[:, :at].reshape(blocks, SAMPLES, BLOCK_OBS)
    variance = everyone[:, at : at + owned].reshape(blocks, BLOCK_OBS)
    places = everyone[:, at + owned :].reshape(devices, tiles).astype(jnp.int32)
    times = (places // LAT + steps_here * jnp.arange(devices, dtype=jnp.int32)[:, None]).reshape(-1)
    rows = (places % LAT).reshape(-1)
    time_hot = (jnp.arange(time_cov.shape[0])[:, None] == times[None, :]).astype(jnp.float32)
    row_hot = (jnp.arange(LAT)[:, None] == rows[None, :]).astype(jnp.float32)
    my_times = lax.dynamic_slice_in_dim(time_cov, me * steps_here, steps_here, 0)
    time_part = jnp.dot(my_times, time_hot, precision=precise)
    row_part = jnp.dot(lat_cov, row_hot, precision=precise)
    dense = (time_part[:, None, :] * row_part[None, :, :]).astype(jnp.bfloat16)
    dense = dense.reshape(rows_here, devices * tiles)
    mine = jnp.take(dense, tile_place.reshape(-1), axis=0)

    def spread(vectors):
        chosen = jnp.take(vectors.astype(jnp.bfloat16), requests, axis=0)
        contrib = jnp.einsum(
            "ocks,ocsl->ockl", chosen, footprint, preferred_element_type=jnp.float32
        )
        contrib = contrib.astype(jnp.bfloat16).reshape(tiles, SAMPLES * LON)
        return lax.all_gather(contrib, "tm", axis=0, tiled=True)

    def collect(gathered):
        field = jnp.dot(mine, gathered, preferred_element_type=jnp.float32)
        field = jnp.dot(field.reshape(-1, LON), lon_cov, precision=precise)
        picked = field.astype(jnp.bfloat16).reshape(devices, slots, SAMPLES, LON)
        partial = jnp.einsum(
            "ockl,ocsl->ocks", picked, footprint, preferred_element_type=jnp.float32
        )
        block_range = jnp.arange(owned, dtype=jnp.int32)
        selector = (tile_block[:, :, None] == block_range).astype(jnp.float32)
        summed = jnp.einsum("ocb,ocks->obks", selector, partial, precision=precise)
        terms = lax.all_to_all(
            summed.reshape(devices, owned * SAMPLES, BLOCK_OBS), "tm", 0, 0, tiled=True
        )
        return to_all(terms.sum(0)).reshape(blocks, SAMPLES, BLOCK_OBS)

    solution = jnp.zeros_like(rhs)
    residual = rhs
    direction = rhs
    norm_now = gram(rhs, rhs)
    gathers, sizes = [], []
    for step in range(ITERS):
        gathered = spread(direction)
        image = collect(gathered) + variance[:, None, :] * direction
        step_size = solve_spd(gram(direction, image), norm_now)
        gathers.append(gathered)
        sizes.append(step_size)
        solution = solution + combine(direction, step_size)
        if step + 1 == ITERS:
            break
        residual = residual - combine(image, step_size)
        norm_next = gram(residual, residual)
        mix_ratio = solve_spd(norm_now, norm_next)
        direction = residual + combine(direction, mix_ratio)
        norm_now = norm_next

    def mix(gathered, size):
        whole = gathered.astype(jnp.float32).reshape(-1, SAMPLES, LON)
        return jnp.einsum("tkl,kj->tjl", whole, size, precision=precise)

    def apply_dense(gathered):
        return jnp.dot(dense, gathered, preferred_element_type=jnp.float32)

    if rows_here < devices * tiles // 4:
        flux = sum(mix(apply_dense(g), size) for g, size in zip(gathers, sizes))
    else:
        total = sum(mix(g, size) for g, size in zip(gathers, sizes))
        flux = apply_dense(total.astype(jnp.bfloat16).reshape(-1, SAMPLES * LON))
    flux = jnp.dot(flux.reshape(-1, LON), lon_cov, precision=precise)
    mine_now = lax.dynamic_slice_in_dim(solution, me * owned, owned, 0)
    return (mine_now, flux.reshape(steps_here, LAT, SAMPLES, LON))


def rolled(x, shift):
    return x if shift == 0 else pltpu.roll(x, 8 - 2 * shift, x.ndim - 2)


def row_gram(left, right):
    entry = [[None] * SAMPLES for _ in range(SAMPLES)]
    for shift in range(SAMPLES):
        product = jnp.sum(left * rolled(right, shift), axis=0)
        total = jnp.broadcast_to(jnp.sum(product, axis=1, keepdims=True), product.shape)
        for k in range(SAMPLES):
            pair = total[2 * k : 2 * k + 1] + total[2 * k + 1 : 2 * k + 2]
            entry[k][(k + shift) % SAMPLES] = pair
    return entry


def row_solve(matrix, target):
    size = range(SAMPLES)
    sym = [[0.5 * (matrix[i][j] + matrix[j][i]) for j in size] for i in size]
    low = [[None] * SAMPLES for _ in size]
    scaled = [[None] * SAMPLES for _ in size]
    inverse = []
    for j in size:
        pivot = sym[j][j]
        for p in range(j):
            pivot = pivot - low[j][p] * scaled[j][p]
        inverse.append(1.0 / pivot)
        for i in range(j + 1, SAMPLES):
            value = sym[i][j]
            for p in range(j):
                value = value - scaled[i][p] * low[j][p]
            scaled[i][j] = value
            low[i][j] = value * inverse[j]
    out = [[None] * SAMPLES for _ in size]
    for c in size:
        part = []
        for i in size:
            value = target[i][c]
            for p in range(i):
                value = value - low[i][p] * part[p]
            part.append(value)
        for i in reversed(size):
            value = part[i] * inverse[i]
            for p in range(i + 1, SAMPLES):
                value = value - low[p][i] * out[p][c]
            out[i][c] = value
    return out


def row_weights(weights):
    sample = lax.broadcasted_iota(jnp.int32, (8, 128), 0) // 2
    result = []
    for shift in range(SAMPLES):
        rows = jnp.broadcast_to(weights[shift][0], (8, 128))
        for j in range(1, SAMPLES):
            rows = jnp.where(sample == j, weights[(j + shift) % SAMPLES][j], rows)
        result.append(rows)
    return result


def row_combine(x, per_shift):
    total = 0.0
    for shift in range(SAMPLES):
        total = total + rolled(x, shift) * per_shift[shift]
    return total


PIECES = 8


def fetch(source, held, arrived):
    pieces = arrived.shape[0]
    size = source.shape[0] // pieces
    copies = []
    for p in range(pieces):
        at = pl.ds(p * size, size)
        copies.append(pltpu.make_async_copy(source.at[at], held.at[at], arrived.at[p]))
    for copy in copies:
        copy.start()
    return copies


def second_of(tile_block):
    slots, owners = tile_block.shape
    tiles = owners * slots
    tile = lax.broadcasted_iota(jnp.int32, (tiles, slots), 0)
    slot = lax.broadcasted_iota(jnp.int32, (tiles, slots), 1)
    rows = jnp.dot(
        (tile % slots == slot).astype(jnp.float32),
        tile_block[...].astype(jnp.float32),
        preferred_element_type=jnp.float32,
    )
    tile = lax.broadcasted_iota(jnp.int32, (tiles, owners), 0)
    owner = lax.broadcasted_iota(jnp.int32, (tiles, owners), 1)
    return jnp.sum(jnp.where(tile // slots == owner, rows, 0.0), axis=1, keepdims=True)


def pack_body(right_sides, obs_var, tile_place, tile_block, lon, copies, mask, shelf, pair, sent):
    slots, owners = tile_place.shape
    tiles = owners * slots
    owner = lax.broadcasted_iota(jnp.int32, (owners, tiles), 0)
    lane = lax.broadcasted_iota(jnp.int32, (owners, tiles), 1)
    spread_out = jnp.dot(
        tile_place[...].astype(jnp.float32),
        (lane // slots == owner).astype(jnp.float32),
        precision=precise,
        preferred_element_type=jnp.float32,
    )
    slot = lax.broadcasted_iota(jnp.int32, (slots, tiles), 0)
    lane = lax.broadcasted_iota(jnp.int32, (slots, tiles), 1)
    place = jnp.sum(jnp.where(lane % slots == slot, spread_out, 0.0), axis=0, keepdims=True)
    for k in range(SAMPLES):
        for b in range(2):
            copies[0, 2 * k + b : 2 * k + b + 1] = right_sides[b, k : k + 1]
    copies[0, 8:10] = obs_var[...]
    copies[0, 10:11] = place
    copies[0, 11:16] = jnp.zeros((5, tiles), jnp.float32)
    for d in range(1, copies.shape[0]):
        copies[d] = copies[0]
    second = jnp.broadcast_to(second_of(tile_block), lon.shape)
    mask[...] = second
    pair[0] = second
    pair[1] = lon[...]
    shelve = pltpu.make_async_copy(pair, shelf.at[0:2], sent)
    shelve.start()
    shelve.wait()


def spread_tiles(vectors, held, copies, products, split):
    owners, slots = held.shape[:2]
    piece = owners // len(copies)
    for owner in range(owners):
        if owner % piece == 0:
            copies[owner // piece].wait()
        rows = vectors[owner, 0:8]
        lhs = rows.astype(jnp.bfloat16)
        if split:
            upper = lhs.astype(jnp.float32)
            lhs = jnp.concatenate([upper, rows - upper], axis=0).astype(jnp.bfloat16)
        for c in range(slots):
            r = jnp.dot(lhs, held[owner, c], preferred_element_type=jnp.float32)
            products[owner * slots + c] = r[:8] + r[8:] if split else r


def spread_end(products, mask_lon, by_column, by_tile):
    second = mask_lon[0] > 0.5
    width = by_column.shape[1]
    chunks = LON // width
    for k in range(SAMPLES):
        chosen = jnp.where(second, products[:, 2 * k + 1, :], products[:, 2 * k, :])
        mixed = jnp.dot(
            chosen, mask_lon[1], precision=precise, preferred_element_type=jnp.float32
        )
        by_tile[:, k * LON : (k + 1) * LON] = mixed.astype(jnp.bfloat16)
        turned = mixed.T.astype(jnp.bfloat16)
        by_column[k * chunks : (k + 1) * chunks] = turned.reshape(chunks, width, LON)


def first_body(
    everyone, shelf, footprint,
    by_column, by_tile, products, held, arrived, mask_lon, shelf_arrived,
):
    copies = fetch(footprint, held, arrived)
    shelf_copy = pltpu.make_async_copy(shelf.at[0:2], mask_lon, shelf_arrived)
    shelf_copy.start()
    spread_tiles(everyone, held, copies, products, False)
    shelf_copy.wait()
    spread_end(products, mask_lon, by_column, by_tile)


def with_variance(image, everyone, vectors):
    block = lax.broadcasted_iota(jnp.int32, vectors.shape, 1) % 2
    variance = jnp.where(block == 0, everyone[:, 8:9, :], everyone[:, 9:10, :])
    return image + variance * vectors


def entries(ref):
    grid = range(SAMPLES)
    return [[ref[SAMPLES * k + j : SAMPLES * k + j + 1] for j in grid] for k in grid]


def keep(ref, matrix):
    for k in range(SAMPLES):
        for j in range(SAMPLES):
            ref[SAMPLES * k + j : SAMPLES * k + j + 1] = matrix[k][j]


def update_body(
    everyone, image_in, shelf, footprint, after,
    by_column, by_tile, direction, sizes, norm,
    products, held, arrived, mask_lon, shelf_arrived,
):
    del after
    copies = fetch(footprint, held, arrived)
    shelf_copy = pltpu.make_async_copy(shelf.at[0:2], mask_lon, shelf_arrived)
    shelf_copy.start()
    first = everyone[:, 0:8, :]
    image = with_variance(image_in[...], everyone, first)
    norm_now = row_gram(first, first)
    step_size = row_solve(row_gram(first, image), norm_now)
    residual = first - row_combine(image, row_weights(step_size))
    norm_next = row_gram(residual, residual)
    ratio = row_solve(norm_now, norm_next)
    direction[...] = residual + row_combine(first, row_weights(ratio))
    keep(sizes, step_size)
    keep(norm, norm_next)
    spread_tiles(direction, held, copies, products, True)
    shelf_copy.wait()
    spread_end(products, mask_lon, by_column, by_tile)


def build_body(
    me, everyone, time_cov, lat_cov,
    prior_out, parts_out, tile_prior, hot, cols, times, parts, sent, parts_sent,
):
    devices, tiles = everyone.shape[0], everyone.shape[2]
    steps_here = parts.shape[0] - LAT
    at = lax.broadcasted_iota(jnp.int32, (LAT, tiles), 0)
    for kind, cov in ((0, time_cov), (1, lat_cov)):
        whole_cov = cov[...]
        upper = whole_cov.astype(jnp.bfloat16)
        lower = (whole_cov - upper.astype(jnp.float32)).astype(jnp.bfloat16)
        ones = []
        for d in range(devices):
            place = (everyone[d, 10:11, :] + 0.5).astype(jnp.int32)
            where = place // LAT + steps_here * d if kind == 0 else place % LAT
            one = (at == where).astype(jnp.float32)
            ones.append(one.astype(jnp.bfloat16))
            turned = one.T.astype(jnp.bfloat16)
            here = slice(d * tiles, (d + 1) * tiles)
            hot[kind, here, 0:LAT] = turned
            hot[kind, here, LAT : 2 * LAT] = turned
        picked = jnp.dot(
            jnp.concatenate([upper, lower], axis=0),
            jnp.concatenate(ones, axis=1),
            preferred_element_type=jnp.float32,
        )
        cols[kind] = picked.astype(jnp.bfloat16)
        both = picked[:LAT] + picked[LAT:]
        if kind == 0:
            times[...] = both
            mine = pl.ds(pl.multiple_of(me[0] * steps_here, steps_here), steps_here)
            parts[LAT:] = times[mine, :]
        else:
            parts[:LAT] = both

    parts_copy = pltpu.make_async_copy(parts, parts_out, parts_sent)
    parts_copy.start()
    rows = tile_prior.shape[0] // PIECES

    def sending(piece):
        block = pl.ds(pl.multiple_of(piece * rows, rows), rows)
        return pltpu.make_async_copy(
            tile_prior.at[block], prior_out.at[block], sent.at[piece]
        )

    @pl.loop(0, PIECES)
    def _(piece):
        block = pl.ds(pl.multiple_of(piece * rows, rows), rows)
        by_time = jnp.dot(hot[0, block, :], cols[0], preferred_element_type=jnp.float32)
        by_row = jnp.dot(hot[1, block, :], cols[1], preferred_element_type=jnp.float32)
        tile_prior[block, :] = (by_time * by_row).astype(jnp.bfloat16)
        sending(piece).start()

    parts_copy.wait()
    for piece in range(PIECES):
        sending(piece).wait()


def mix_body(columns, tile_prior, *rest):
    mixed, total, held, arrived = rest[-4:]
    copies = fetch(tile_prior, held, arrived)
    devices, width, tiles = columns.shape
    part = devices // len(copies)
    for p, copy in enumerate(copies):
        at = range(p * part, (p + 1) * part)
        lhs = jnp.concatenate([columns[d] for d in at], axis=1)
        copy.wait()
        product = jnp.dot(
            lhs,
            held[p * part * tiles : (p + 1) * part * tiles],
            preferred_element_type=jnp.float32,
        )
        total[...] = product if p == 0 else total[...] + product
    for d in range(devices):
        mixed[d] = total[:, d * tiles : (d + 1) * tiles].astype(jnp.bfloat16)


def sum_body(terms, total, copies):
    value = jnp.sum(terms[...], axis=0)
    total[...] = value
    for d in range(copies.shape[0]):
        copies[d] = value


def collect_body(values, mask, footprint, sums, rows):
    chunks = values.shape[0] // SAMPLES
    owners, slots = footprint.shape[:2]
    is_second = mask[...] > 0.5
    for k in range(SAMPLES):
        turned = values[k * chunks : (k + 1) * chunks].reshape(LON, -1)
        turned = turned.astype(jnp.float32).T
        rows[:, 2 * k, :] = jnp.where(is_second, 0.0, turned)
        rows[:, 2 * k + 1, :] = jnp.where(is_second, turned, 0.0)
    for owner in range(owners):
        total = 0.0
        for c in range(slots):
            total = total + lax.dot_general(
                rows[owner * slots + c].astype(jnp.bfloat16),
                footprint[owner, c],
                (((1,), (1,)), ((), ())),
                preferred_element_type=jnp.float32,
            )
        sums[owner] = total


def dense_rows(parts, first):
    rows = []
    for t in range(first, first + 2):
        rows.append((parts[LAT + t : LAT + t + 1, :] * parts[:LAT]).astype(jnp.bfloat16))
    return jnp.concatenate(rows, axis=0)


def send_rows(ready, out, sent, step, value):
    at = pl.ds(step * LAT, 2 * LAT)
    ready[at] = value
    copy = pltpu.make_async_copy(ready.at[at], out.at[at], sent.at[step // 2])
    copy.start()
    return copy


def halved_product(dense, held, copies):
    half = held.shape[0] // 2
    total = 0.0
    for h in range(2):
        for copy in copies[h * PIECES // 2 : (h + 1) * PIECES // 2]:
            copy.wait()
        at = slice(h * half, (h + 1) * half)
        total = total + jnp.dot(dense[:, at], held[at], preferred_element_type=jnp.float32)
    return total


def mixed_samples(value, size):
    pieces = [value[:, k * LON : (k + 1) * LON] for k in range(SAMPLES)]
    mixed = []
    for j in range(SAMPLES):
        mixed.append(sum(pieces[k] * size[k][j] for k in range(SAMPLES)))
    return jnp.concatenate(mixed, axis=1)


def flux_product_body(
    rows, after, parts, gathered, out, token,
    ready, parts_held, held, parts_arrived, arrived, sent,
):
    del after
    (parts_copy,) = fetch(parts, parts_held, parts_arrived)
    copies = fetch(gathered, held, arrived)
    parts_copy.wait()
    sending = []
    for step in range(0, rows // LAT, 2):
        dense = dense_rows(parts_held, step)
        if step == 0:
            value = halved_product(dense, held, copies)
            token[...] = value[0:8, 0:128]
        else:
            value = jnp.dot(dense, held[...], preferred_element_type=jnp.float32)
        sending.append(send_rows(ready, out, sent, step, value))
    for copy in sending:
        copy.wait()


def flux_first_body(
    sizes, product, parts, gathered, out, token,
    ready, parts_held, held, parts_arrived, arrived, sent, product_held, product_arrived,
):
    done = product_held.shape[0] // LAT
    product_copies = fetch(product.at[: done * LAT], product_held, product_arrived)
    (parts_copy,) = fetch(parts, parts_held, parts_arrived)
    copies = fetch(gathered, held, arrived)
    size = entries(sizes)
    sending = []
    for copy in product_copies:
        copy.wait()
    for step in range(0, done, 2):
        value = product_held[step * LAT : (step + 2) * LAT]
        sending.append(send_rows(ready, out, sent, step, mixed_samples(value, size)))
    parts_copy.wait()
    for step in range(done, out.shape[0] // LAT, 2):
        dense = dense_rows(parts_held, step)
        if step == done:
            value = halved_product(dense, held, copies)
        else:
            value = jnp.dot(dense, held[...], preferred_element_type=jnp.float32)
        value = mixed_samples(value, size)
        sending.append(send_rows(ready, out, sent, step, value))
    token[...] = size[0][0] + jnp.zeros(token.shape, jnp.float32)
    for copy in sending:
        copy.wait()


def last_body(
    me, everyone, image_in, direction, sizes, norm, flux_one, flux_two,
    answer, flux, one, two, ready, one_arrived, two_arrived, sent,
):
    two_copies = fetch(flux_two, two, two_arrived)
    one_copies = fetch(flux_one, one, one_arrived)
    second = direction[...]
    image = with_variance(image_in[...], everyone, second)
    size_two = row_solve(row_gram(second, image), entries(norm))
    own = row_combine(everyone[me[0], 0:8, :], row_weights(entries(sizes)))
    own = own + row_combine(direction[me[0]], row_weights(size_two))
    for k in range(SAMPLES):
        for b in range(2):
            answer[b, k : k + 1, :] = own[2 * k + b : 2 * k + b + 1]

    steps = ready.shape[0]
    piece = steps // len(one_copies)
    sending = []
    for t in range(steps):
        if t % piece == 0:
            two_copies[t // piece].wait()
            one_copies[t // piece].wait()
        at = slice(t * LAT, (t + 1) * LAT)
        parts = [two[at, k * LON : (k + 1) * LON] for k in range(SAMPLES)]
        for j in range(SAMPLES):
            value = one[at, j * LON : (j + 1) * LON]
            for k in range(SAMPLES):
                value = value + parts[k] * size_two[k][j]
            ready[t, :, j, :] = value
        copy = pltpu.make_async_copy(ready.at[t], flux.at[t], sent.at[t])
        copy.start()
        sending.append(copy)
    for copy in sending:
        copy.wait()


MIB = 1024 * 1024


def shape_of(shape, dtype):
    return jax.ShapeDtypeStruct(shape, dtype)


def cost(flops, moved):
    return pl.CostEstimate(flops=flops, bytes_accessed=moved, transcendentals=0)


def by_columns(
    right_sides, obs_var, footprint, tile_block, tile_place, time_cov, lat_cov, lon_cov
):
    devices = lax.axis_size("tm")
    me = lax.axis_index("tm").reshape(1).astype(jnp.int32)
    steps_here = time_cov.shape[0] // devices
    tiles = tile_block.size
    every_tile = devices * tiles
    columns = SAMPLES * LON
    width = columns // devices
    rows_here = steps_here * LAT
    f32, bf16 = jnp.float32, jnp.bfloat16

    vmem = pl.BlockSpec(memory_space=pltpu.VMEM)
    smem = pl.BlockSpec(memory_space=pltpu.SMEM)
    hbm = pl.BlockSpec(memory_space=pltpu.HBM)
    vector_shape = shape_of((devices, 8, BLOCK_OBS), f32)
    column_shape = shape_of((devices, width, tiles), bf16)
    tile_shape = shape_of((tiles, columns), bf16)
    small_shape = shape_of((SAMPLES * SAMPLES, 128), f32)
    field_shape = shape_of((rows_here, columns), f32)
    parts_shape = shape_of((LAT + steps_here, every_tile), f32)
    token_shape = shape_of((8, 128), f32)
    prior_shape = shape_of((every_tile, every_tile), bf16)
    flux_shape = shape_of((steps_here, LAT, SAMPLES, LON), f32)

    def flags(count):
        return pltpu.SemaphoreType.DMA((count,))

    products = pltpu.VMEM((tiles, 8, LON), f32)
    field = pltpu.VMEM(field_shape.shape, f32)
    gathered_held = pltpu.VMEM((every_tile, columns), bf16)
    prior_held = pltpu.VMEM(prior_shape.shape, bf16)
    spread_scratch = [products, pltpu.VMEM(footprint.shape, bf16), flags(2 * PIECES)]
    spread_scratch += [pltpu.VMEM((2, 128, 128), f32), pltpu.SemaphoreType.DMA]
    flux_scratch = [field, pltpu.VMEM(parts_shape.shape, f32), gathered_held]
    flux_scratch += [flags(1), flags(PIECES), flags(steps_here // 2)]
    tile_cost = cost(2 * 8 * footprint.size, footprint.size * 2)
    flux_cost = cost(2 * rows_here * every_tile * columns, every_tile * columns * 2)

    def call(body, in_specs, out_specs, out_shape, scratch, estimate, name, grant=53):
        return pl.pallas_call(
            body,
            in_specs=in_specs,
            out_specs=out_specs,
            out_shape=out_shape,
            scratch_shapes=scratch,
            compiler_params=pltpu.CompilerParams(vmem_limit_bytes=grant * MIB),
            cost_estimate=estimate,
            name=name,
        )

    def exchange(array):
        return lax.all_to_all(array, "tm", split_axis=0, concat_axis=0, tiled=True)

    pair_scratch = [pltpu.VMEM((2, 128, 128), f32), pltpu.SemaphoreType.DMA]
    packed, mask, shelf = call(
        pack_body,
        [vmem] * 5,
        [vmem, vmem, hbm],
        [
            shape_of((devices, 16, 128), f32),
            shape_of((128, 128), f32),
            shape_of((64, 128, 128), f32),
        ],
        pair_scratch,
        cost(0, 12 * MIB),
        "pack",
        59,
    )(right_sides, obs_var, tile_place.T, tile_block.T, lon_cov)
    everyone = exchange(packed)
    by_column, by_tile = call(
        first_body,
        [vmem, hbm, hbm],
        [vmem] * 2,
        [column_shape, tile_shape],
        spread_scratch,
        tile_cost,
        "spread_first",
    )(everyone, shelf, footprint)
    gathered_one = lax.all_gather(by_tile, "tm", axis=0, tiled=True)

    tile_prior, parts = call(
        build_body,
        [smem] + [vmem] * 3,
        [hbm, hbm],
        [prior_shape, parts_shape],
        [
            prior_held,
            pltpu.VMEM((2, every_tile, 2 * LAT), bf16),
            pltpu.VMEM((2, 2 * LAT, every_tile), bf16),
            pltpu.VMEM((LAT, every_tile), f32),
            pltpu.VMEM(parts_shape.shape, f32),
            flags(PIECES),
            pltpu.SemaphoreType.DMA,
        ],
        cost(4 * every_tile * every_tile * 256, every_tile * every_tile * 2),
        "build_prior",
    )(me, everyone, time_cov, lat_cov)

    def flux_product(after, gathered, rows):
        return call(
            functools.partial(flux_product_body, rows),
            [hbm, hbm, hbm],
            [hbm, vmem],
            [field_shape, token_shape],
            flux_scratch,
            flux_cost,
            "flux_product",
        )(after, parts, gathered)

    def prior(by_column, *after):
        mixed = call(
            mix_body,
            [vmem, hbm] + [hbm] * len(after),
            vmem,
            column_shape,
            [pltpu.VMEM((width, every_tile), f32), prior_held, flags(PIECES)],
            cost(2 * width * every_tile**2, every_tile**2 * 2),
            "mix_columns",
        )(exchange(by_column), tile_prior, *after)
        return exchange(mixed)

    def collect(values):
        sums = call(
            collect_body, [vmem] * 3, vmem, vector_shape, [products], tile_cost, "collect", 48
        )(values, mask, footprint)
        own, copies = call(
            sum_body,
            [vmem],
            [vmem] * 2,
            [shape_of((8, BLOCK_OBS), f32), vector_shape],
            [],
            cost(0, 4 * MIB),
            "sum_terms",
        )(exchange(sums))
        return own, exchange(copies)

    own_image, image = collect(prior(by_column))
    product_one, token = flux_product(own_image, gathered_one, rows_here // 2)
    by_column, by_tile, direction, sizes, norm = call(
        update_body,
        [vmem] * 2 + [hbm] * 3,
        [vmem] * 5,
        [column_shape, tile_shape, vector_shape, small_shape, small_shape],
        spread_scratch,
        tile_cost,
        "update_spread",
    )(everyone, image, shelf, footprint, token)
    gathered_two = lax.all_gather(by_tile, "tm", axis=0, tiled=True)
    flux_one, token = call(
        flux_first_body,
        [vmem, hbm, hbm, hbm],
        [hbm, vmem],
        [field_shape, token_shape],
        flux_scratch + [pltpu.VMEM((rows_here // 2, columns), f32), flags(2)],
        flux_cost,
        "flux_first",
    )(sizes, product_one, parts, gathered_one)

    own_image, image = collect(prior(by_column, token))
    flux_two, _ = flux_product(own_image, gathered_two, rows_here)

    answer, flux = call(
        last_body,
        [smem] + [vmem] * 5 + [hbm] * 2,
        [vmem, hbm],
        [shape_of(right_sides.shape, f32), flux_shape],
        [field, field, pltpu.VMEM(flux_shape.shape, f32), flags(4), flags(4), flags(steps_here)],
        cost(1 << 20, 6 << 20),
        "last",
    )(me, everyone, image, direction, sizes, norm, flux_one, flux_two)
    return (answer, flux)


def local(right_sides, obs_var, footprint, tile_block, tile_place, *covariances):
    devices = lax.axis_size("tm")
    tiles = tile_block.size
    fits = devices * tiles <= 2048 and devices % 4 == 0 and tiles == 128
    fits = fits and right_sides.shape[0] == 2 and (SAMPLES * LON) % (32 * devices) == 0
    fits = fits and (covariances[0].shape[0] // devices) % 4 == 0
    plan = by_columns if fits else by_gather
    return plan(right_sides, obs_var, footprint, tile_block, tile_place, *covariances)


def solution(mesh):
    in_specs = (
        P(("grp", "tm"), None, None),
        P(("grp", "tm"), None),
        P(("grp", "tm"), None, None, None),
        P(("grp", "tm"), None),
        P(("grp", "tm"), None),
        P(),
        P(),
        P(),
    )
    out_specs = (P(("grp", "tm"), None, None), P(("grp", "tm"), None, None, None))
    return jax.shard_map(local, mesh=mesh, in_specs=in_specs, out_specs=out_specs, check_vma=False)
```

```python
import functools

import jax
import jax.numpy as jnp
from jax import lax
from jax.experimental import pallas as pl
from jax.experimental.pallas import tpu as pltpu
from jax.sharding import PartitionSpec as P

LAT = 128
LON = 128
BLOCK_OBS = 128
SAMPLES = 4
ITERS = 2


precise = lax.Precision.HIGHEST


def solve_spd(matrix, target):
    factor = jnp.linalg.cholesky(matrix)
    halfway = lax.linalg.triangular_solve(factor, target, left_side=True, lower=True)
    return lax.linalg.triangular_solve(
        factor, halfway, left_side=True, lower=True, transpose_a=True
    )


def combine(vectors, weights):
    return jnp.einsum("nks,kj->njs", vectors, weights, precision=precise)


def gram(left, right):
    return jnp.einsum("nks,njs->kj", left, right, precision=precise)


def to_all(array):
    devices = lax.axis_size("tm")
    copies = jnp.broadcast_to(array[None], (devices,) + array.shape)
    return lax.all_to_all(copies, "tm", split_axis=0, concat_axis=0, tiled=True)


def by_gather(
    right_sides, obs_var, footprint, tile_block, tile_place, time_cov, lat_cov, lon_cov
):
    devices = lax.axis_size("tm")
    me = lax.axis_index("tm")
    owned = right_sides.shape[0]
    blocks = devices * owned
    steps_here = time_cov.shape[0] // devices
    slots = tile_block.shape[1]
    tiles = devices * slots
    rows_here = steps_here * LAT
    owner_base = (jnp.arange(devices, dtype=jnp.int32) * owned)[:, None]
    requests = owner_base + tile_block

    packed = jnp.concatenate(
        [
            right_sides.reshape(-1, 128),
            obs_var.reshape(-1, 128),
            tile_place.astype(jnp.float32).reshape(-1, 128),
        ]
    )
    everyone = to_all(packed)
    at = owned * SAMPLES
    rhs = everyone[:, :at].reshape(blocks, SAMPLES, BLOCK_OBS)
    variance = everyone[:, at : at + owned].reshape(blocks, BLOCK_OBS)
    places = everyone[:, at + owned :].reshape(devices, tiles).astype(jnp.int32)
    times = (places // LAT + steps_here * jnp.arange(devices, dtype=jnp.int32)[:, None]).reshape(-1)
    rows = (places % LAT).reshape(-1)
    time_hot = (jnp.arange(time_cov.shape[0])[:, None] == times[None, :]).astype(jnp.float32)
    row_hot = (jnp.arange(LAT)[:, None] == rows[None, :]).astype(jnp.float32)
    my_times = lax.dynamic_slice_in_dim(time_cov, me * steps_here, steps_here, 0)
    time_part = jnp.dot(my_times, time_hot, precision=precise)
    row_part = jnp.dot(lat_cov, row_hot, precision=precise)
    dense = (time_part[:, None, :] * row_part[None, :, :]).astype(jnp.bfloat16)
    dense = dense.reshape(rows_here, devices * tiles)
    mine = jnp.take(dense, tile_place.reshape(-1), axis=0)

    def spread(vectors):
        chosen = jnp.take(vectors.astype(jnp.bfloat16), requests, axis=0)
        contrib = jnp.einsum(
            "ocks,ocsl->ockl", chosen, footprint, preferred_element_type=jnp.float32
        )
        contrib = contrib.astype(jnp.bfloat16).reshape(tiles, SAMPLES * LON)
        return lax.all_gather(contrib, "tm", axis=0, tiled=True)

    def collect(gathered):
        field = jnp.dot(mine, gathered, preferred_element_type=jnp.float32)
        field = jnp.dot(field.reshape(-1, LON), lon_cov, precision=precise)
        picked = field.astype(jnp.bfloat16).reshape(devices, slots, SAMPLES, LON)
        partial = jnp.einsum(
            "ockl,ocsl->ocks", picked, footprint, preferred_element_type=jnp.float32
        )
        block_range = jnp.arange(owned, dtype=jnp.int32)
        selector = (tile_block[:, :, None] == block_range).astype(jnp.float32)
        summed = jnp.einsum("ocb,ocks->obks", selector, partial, precision=precise)
        terms = lax.all_to_all(
            summed.reshape(devices, owned * SAMPLES, BLOCK_OBS), "tm", 0, 0, tiled=True
        )
        return to_all(terms.sum(0)).reshape(blocks, SAMPLES, BLOCK_OBS)

    solution = jnp.zeros_like(rhs)
    residual = rhs
    direction = rhs
    norm_now = gram(rhs, rhs)
    gathers, sizes = [], []
    for step in range(ITERS):
        gathered = spread(direction)
        image = collect(gathered) + variance[:, None, :] * direction
        step_size = solve_spd(gram(direction, image), norm_now)
        gathers.append(gathered)
        sizes.append(step_size)
        solution = solution + combine(direction, step_size)
        if step + 1 == ITERS:
            break
        residual = residual - combine(image, step_size)
        norm_next = gram(residual, residual)
        mix_ratio = solve_spd(norm_now, norm_next)
        direction = residual + combine(direction, mix_ratio)
        norm_now = norm_next

    def mix(gathered, size):
        whole = gathered.astype(jnp.float32).reshape(-1, SAMPLES, LON)
        return jnp.einsum("tkl,kj->tjl", whole, size, precision=precise)

    def apply_dense(gathered):
        return jnp.dot(dense, gathered, preferred_element_type=jnp.float32)

    if rows_here < devices * tiles // 4:
        flux = sum(mix(apply_dense(g), size) for g, size in zip(gathers, sizes))
    else:
        total = sum(mix(g, size) for g, size in zip(gathers, sizes))
        flux = apply_dense(total.astype(jnp.bfloat16).reshape(-1, SAMPLES * LON))
    flux = jnp.dot(flux.reshape(-1, LON), lon_cov, precision=precise)
    mine_now = lax.dynamic_slice_in_dim(solution, me * owned, owned, 0)
    return (mine_now, flux.reshape(steps_here, LAT, SAMPLES, LON))


def rolled(x, shift):
    return x if shift == 0 else pltpu.roll(x, 8 - 2 * shift, x.ndim - 2)


def row_gram(left, right):
    entry = [[None] * SAMPLES for _ in range(SAMPLES)]
    for shift in range(SAMPLES):
        product = jnp.sum(left * rolled(right, shift), axis=0)
        total = jnp.broadcast_to(jnp.sum(product, axis=1, keepdims=True), product.shape)
        for k in range(SAMPLES):
            pair = total[2 * k : 2 * k + 1] + total[2 * k + 1 : 2 * k + 2]
            entry[k][(k + shift) % SAMPLES] = pair
    return entry


def row_solve(matrix, target):
    size = range(SAMPLES)
    sym = [[0.5 * (matrix[i][j] + matrix[j][i]) for j in size] for i in size]
    low = [[None] * SAMPLES for _ in size]
    scaled = [[None] * SAMPLES for _ in size]
    inverse = []
    for j in size:
        pivot = sym[j][j]
        for p in range(j):
            pivot = pivot - low[j][p] * scaled[j][p]
        inverse.append(1.0 / pivot)
        for i in range(j + 1, SAMPLES):
            value = sym[i][j]
            for p in range(j):
                value = value - scaled[i][p] * low[j][p]
            scaled[i][j] = value
            low[i][j] = value * inverse[j]
    out = [[None] * SAMPLES for _ in size]
    for c in size:
        part = []
        for i in size:
            value = target[i][c]
            for p in range(i):
                value = value - low[i][p] * part[p]
            part.append(value)
        for i in reversed(size):
            value = part[i] * inverse[i]
            for p in range(i + 1, SAMPLES):
                value = value - low[p][i] * out[p][c]
            out[i][c] = value
    return out


def row_weights(weights):
    sample = lax.broadcasted_iota(jnp.int32, (8, 128), 0) // 2
    result = []
    for shift in range(SAMPLES):
        rows = jnp.broadcast_to(weights[shift][0], (8, 128))
        for j in range(1, SAMPLES):
            rows = jnp.where(sample == j, weights[(j + shift) % SAMPLES][j], rows)
        result.append(rows)
    return result


def row_combine(x, per_shift):
    total = 0.0
    for shift in range(SAMPLES):
        total = total + rolled(x, shift) * per_shift[shift]
    return total


PIECES = 8


def fetch(source, held, arrived):
    pieces = arrived.shape[0]
    size = source.shape[0] // pieces
    copies = []
    for p in range(pieces):
        at = pl.ds(p * size, size)
        copies.append(pltpu.make_async_copy(source.at[at], held.at[at], arrived.at[p]))
    for copy in copies:
        copy.start()
    return copies


def second_of(tile_block):
    slots, owners = tile_block.shape
    tiles = owners * slots
    tile = lax.broadcasted_iota(jnp.int32, (tiles, slots), 0)
    slot = lax.broadcasted_iota(jnp.int32, (tiles, slots), 1)
    rows = jnp.dot(
        (tile % slots == slot).astype(jnp.float32),
        tile_block[...].astype(jnp.float32),
        preferred_element_type=jnp.float32,
    )
    tile = lax.broadcasted_iota(jnp.int32, (tiles, owners), 0)
    owner = lax.broadcasted_iota(jnp.int32, (tiles, owners), 1)
    return jnp.sum(jnp.where(tile // slots == owner, rows, 0.0), axis=1, keepdims=True)


def pack_body(right_sides, obs_var, tile_place, tile_block, lon, copies, mask, shelf, pair, sent):
    slots, owners = tile_place.shape
    tiles = owners * slots
    owner = lax.broadcasted_iota(jnp.int32, (owners, tiles), 0)
    lane = lax.broadcasted_iota(jnp.int32, (owners, tiles), 1)
    spread_out = jnp.dot(
        tile_place[...].astype(jnp.float32),
        (lane // slots == owner).astype(jnp.float32),
        precision=precise,
        preferred_element_type=jnp.float32,
    )
    slot = lax.broadcasted_iota(jnp.int32, (slots, tiles), 0)
    lane = lax.broadcasted_iota(jnp.int32, (slots, tiles), 1)
    place = jnp.sum(jnp.where(lane % slots == slot, spread_out, 0.0), axis=0, keepdims=True)
    for k in range(SAMPLES):
        for b in range(2):
            copies[0, 2 * k + b : 2 * k + b + 1] = right_sides[b, k : k + 1]
    copies[0, 8:10] = obs_var[...]
    copies[0, 10:11] = place
    copies[0, 11:16] = jnp.zeros((5, tiles), jnp.float32)
    for d in range(1, copies.shape[0]):
        copies[d] = copies[0]
    second = jnp.broadcast_to(second_of(tile_block), lon.shape)
    mask[...] = second
    pair[0] = second
    pair[1] = lon[...]
    shelve = pltpu.make_async_copy(pair, shelf.at[0:2], sent)
    shelve.start()
    shelve.wait()


def spread_tiles(vectors, held, copies, products, split):
    owners, slots = held.shape[:2]
    piece = owners // len(copies)
    for owner in range(owners):
        if owner % piece == 0:
            copies[owner // piece].wait()
        rows = vectors[owner, 0:8]
        lhs = rows.astype(jnp.bfloat16)
        if split:
            upper = lhs.astype(jnp.float32)
            lhs = jnp.concatenate([upper, rows - upper], axis=0).astype(jnp.bfloat16)
        for c in range(slots):
            r = jnp.dot(lhs, held[owner, c], preferred_element_type=jnp.float32)
            products[owner * slots + c] = r[:8] + r[8:] if split else r


def spread_end(products, mask_lon, by_column, by_tile):
    second = mask_lon[0] > 0.5
    width = by_column.shape[1]
    chunks = LON // width
    for k in range(SAMPLES):
        chosen = jnp.where(second, products[:, 2 * k + 1, :], products[:, 2 * k, :])
        mixed = jnp.dot(
            chosen, mask_lon[1], precision=precise, preferred_element_type=jnp.float32
        )
        by_tile[:, k * LON : (k + 1) * LON] = mixed.astype(jnp.bfloat16)
        turned = mixed.T.astype(jnp.bfloat16)
        by_column[k * chunks : (k + 1) * chunks] = turned.reshape(chunks, width, LON)


def first_body(
    everyone, shelf, footprint,
    by_column, by_tile, products, held, arrived, mask_lon, shelf_arrived,
):
    shelf_copy = pltpu.make_async_copy(shelf.at[0:2], mask_lon, shelf_arrived)
    shelf_copy.start()
    copies = fetch(footprint, held, arrived)
    spread_tiles(everyone, held, copies, products, False)
    shelf_copy.wait()
    spread_end(products, mask_lon, by_column, by_tile)


def with_variance(image, everyone, vectors):
    block = lax.broadcasted_iota(jnp.int32, vectors.shape, 1) % 2
    variance = jnp.where(block == 0, everyone[:, 8:9, :], everyone[:, 9:10, :])
    return image + variance * vectors


def entries(ref):
    grid = range(SAMPLES)
    return [[ref[SAMPLES * k + j : SAMPLES * k + j + 1] for j in grid] for k in grid]


def keep(ref, matrix):
    for k in range(SAMPLES):
        for j in range(SAMPLES):
            ref[SAMPLES * k + j : SAMPLES * k + j + 1] = matrix[k][j]


def update_body(
    everyone, image_in, shelf, footprint, after,
    by_column, by_tile, direction, sizes, norm,
    products, held, arrived, mask_lon, shelf_arrived,
):
    del after
    shelf_copy = pltpu.make_async_copy(shelf.at[0:2], mask_lon, shelf_arrived)
    shelf_copy.start()
    copies = fetch(footprint, held, arrived)
    first = everyone[:, 0:8, :]
    image = with_variance(image_in[...], everyone, first)
    norm_now = row_gram(first, first)
    step_size = row_solve(row_gram(first, image), norm_now)
    residual = first - row_combine(image, row_weights(step_size))
    norm_next = row_gram(residual, residual)
    ratio = row_solve(norm_now, norm_next)
    direction[...] = residual + row_combine(first, row_weights(ratio))
    keep(sizes, step_size)
    keep(norm, norm_next)
    spread_tiles(direction, held, copies, products, True)
    shelf_copy.wait()
    spread_end(products, mask_lon, by_column, by_tile)


def prior_rows(hot, cols, block):
    by_time = jnp.dot(hot[0, block, :], cols[0], preferred_element_type=jnp.float32)
    by_row = jnp.dot(hot[1, block, :], cols[1], preferred_element_type=jnp.float32)
    return (by_time * by_row).astype(jnp.bfloat16)


def build_body(
    me, everyone, time_cov, lat_cov,
    prior_out, parts_out, hot_out, cols_out,
    tile_prior, hot, cols, times, parts, sent, rest_sent,
):
    devices, tiles = everyone.shape[0], everyone.shape[2]
    steps_here = parts.shape[0] - LAT
    at = lax.broadcasted_iota(jnp.int32, (LAT, tiles), 0)
    for kind, cov in ((0, time_cov), (1, lat_cov)):
        whole_cov = cov[...]
        upper = whole_cov.astype(jnp.bfloat16)
        lower = (whole_cov - upper.astype(jnp.float32)).astype(jnp.bfloat16)
        ones = []
        for d in range(devices):
            place = (everyone[d, 10:11, :] + 0.5).astype(jnp.int32)
            where = place // LAT + steps_here * d if kind == 0 else place % LAT
            one = (at == where).astype(jnp.float32)
            ones.append(one.astype(jnp.bfloat16))
            turned = one.T.astype(jnp.bfloat16)
            here = slice(d * tiles, (d + 1) * tiles)
            hot[kind, here, 0:LAT] = turned
            hot[kind, here, LAT : 2 * LAT] = turned
        picked = jnp.dot(
            jnp.concatenate([upper, lower], axis=0),
            jnp.concatenate(ones, axis=1),
            preferred_element_type=jnp.float32,
        )
        cols[kind] = picked.astype(jnp.bfloat16)
        both = picked[:LAT] + picked[LAT:]
        if kind == 0:
            times[...] = both
            mine = pl.ds(pl.multiple_of(me[0] * steps_here, steps_here), steps_here)
            parts[LAT:] = times[mine, :]
        else:
            parts[:LAT] = both

    later = hot_out.shape[1]
    rest = [
        pltpu.make_async_copy(hot.at[:, later:], hot_out, rest_sent.at[0]),
        pltpu.make_async_copy(cols, cols_out, rest_sent.at[1]),
        pltpu.make_async_copy(parts, parts_out, rest_sent.at[2]),
    ]
    for copy in rest:
        copy.start()
    pieces = sent.shape[0]
    rows = tile_prior.shape[0] // pieces

    def sending(piece):
        block = pl.ds(pl.multiple_of(piece * rows, rows), rows)
        return pltpu.make_async_copy(
            tile_prior.at[block], prior_out.at[block], sent.at[piece]
        )

    @pl.loop(0, pieces)
    def _(piece):
        block = pl.ds(pl.multiple_of(piece * rows, rows), rows)
        tile_prior[block, :] = prior_rows(hot, cols, block)
        sending(piece).start()

    for copy in rest:
        copy.wait()
    for piece in range(pieces):
        sending(piece).wait()


def column_product(columns, first, block):
    devices = block.shape[0] // columns.shape[2]
    lhs = jnp.concatenate([columns[first + d] for d in range(devices)], axis=1)
    return jnp.dot(lhs, block[...], preferred_element_type=jnp.float32)


def split_columns(mixed, total):
    devices, width, tiles = mixed.shape
    for d in range(devices):
        mixed[d] = total[:, d * tiles : (d + 1) * tiles].astype(jnp.bfloat16)


def build_mix_body(
    columns, hot_in, cols_in, prior_one,
    mixed, prior_two, total, hot, cols, held, built, hot_arrived, arrived, sent,
):
    cols_copies = fetch(cols_in, cols, hot_arrived.at[0:1])
    hot_copies = fetch(hot_in, hot, hot_arrived.at[1:2])
    copies = fetch(prior_one, held, arrived)
    half = columns.shape[0] // 2
    pieces = len(copies)
    rows = built.shape[0] // pieces
    for copy in cols_copies + hot_copies:
        copy.wait()
    sending = []
    for p in range(pieces):
        block = pl.ds(p * rows, rows)
        built[block, :] = prior_rows(hot, cols, block)
        copy = pltpu.make_async_copy(built.at[block], prior_two.at[block], sent.at[p])
        copy.start()
        sending.append(copy)
        first = half + p * half // pieces
        product = column_product(columns, first, built.at[block])
        total[...] = product if p == 0 else total[...] + product
    for p, copy in enumerate(copies):
        copy.wait()
        block = pl.ds(p * rows, rows)
        total[...] += column_product(columns, p * half // pieces, held.at[block])
    split_columns(mixed, total)
    for copy in sending:
        copy.wait()


def mix_body(columns, prior_one, prior_two, *rest):
    mixed, total, held_one, held_two, arrived_one, arrived_two = rest[-6:]
    one = fetch(prior_one, held_one, arrived_one)
    two = fetch(prior_two, held_two, arrived_two)
    half = columns.shape[0] // 2
    rows = held_one.shape[0] // len(one)
    for first, held, copies in ((0, held_one, one), (half, held_two, two)):
        for p, copy in enumerate(copies):
            copy.wait()
            at = first + p * half // len(copies)
            product = column_product(columns, at, held.at[pl.ds(p * rows, rows)])
            total[...] = product if at == 0 else total[...] + product
    split_columns(mixed, total)


def sum_body(terms, total, copies):
    value = jnp.sum(terms[...], axis=0)
    total[...] = value
    for d in range(copies.shape[0]):
        copies[d] = value


def collect_body(values, mask, footprint, sums, rows):
    chunks = values.shape[0] // SAMPLES
    owners, slots = footprint.shape[:2]
    is_second = mask[...] > 0.5
    for k in range(SAMPLES):
        turned = values[k * chunks : (k + 1) * chunks].reshape(LON, -1)
        turned = turned.astype(jnp.float32).T
        rows[:, 2 * k, :] = jnp.where(is_second, 0.0, turned)
        rows[:, 2 * k + 1, :] = jnp.where(is_second, turned, 0.0)
    for owner in range(owners):
        total = 0.0
        for c in range(slots):
            total = total + lax.dot_general(
                rows[owner * slots + c].astype(jnp.bfloat16),
                footprint[owner, c],
                (((1,), (1,)), ((), ())),
                preferred_element_type=jnp.float32,
            )
        sums[owner] = total


def dense_rows(parts, first):
    rows = []
    for t in range(first, first + 2):
        rows.append((parts[LAT + t : LAT + t + 1, :] * parts[:LAT]).astype(jnp.bfloat16))
    return jnp.concatenate(rows, axis=0)


def send_rows(ready, out, sent, step, value):
    at = pl.ds(step * LAT, 2 * LAT)
    ready[at] = value
    copy = pltpu.make_async_copy(ready.at[at], out.at[at], sent.at[step // 2])
    copy.start()
    return copy


def halved_product(dense, held, copies):
    half = held.shape[0] // 2
    total = 0.0
    for h in range(2):
        for copy in copies[h * PIECES // 2 : (h + 1) * PIECES // 2]:
            copy.wait()
        at = slice(h * half, (h + 1) * half)
        total = total + jnp.dot(dense[:, at], held[at], preferred_element_type=jnp.float32)
    return total


def mixed_samples(value, size):
    pieces = [value[:, k * LON : (k + 1) * LON] for k in range(SAMPLES)]
    mixed = []
    for j in range(SAMPLES):
        mixed.append(sum(pieces[k] * size[k][j] for k in range(SAMPLES)))
    return jnp.concatenate(mixed, axis=1)


def flux_product_body(
    rows, after, parts, gathered, out, token,
    ready, parts_held, held, parts_arrived, arrived, sent,
):
    del after
    (parts_copy,) = fetch(parts, parts_held, parts_arrived)
    copies = fetch(gathered, held, arrived)
    parts_copy.wait()
    sending = []
    for step in range(0, rows // LAT, 2):
        dense = dense_rows(parts_held, step)
        if step == 0:
            value = halved_product(dense, held, copies)
            token[...] = value[0:8, 0:128]
        else:
            value = jnp.dot(dense, held[...], preferred_element_type=jnp.float32)
        sending.append(send_rows(ready, out, sent, step, value))
    for copy in sending:
        copy.wait()


def flux_first_body(
    sizes, product, parts, gathered, out, token,
    ready, parts_held, held, parts_arrived, arrived, sent, product_held, product_arrived,
):
    done = product_held.shape[0] // LAT
    product_copies = fetch(product.at[: done * LAT], product_held, product_arrived)
    (parts_copy,) = fetch(parts, parts_held, parts_arrived)
    copies = fetch(gathered, held, arrived)
    size = entries(sizes)
    sending = []
    for copy in product_copies:
        copy.wait()
    for step in range(0, done, 2):
        value = product_held[step * LAT : (step + 2) * LAT]
        sending.append(send_rows(ready, out, sent, step, mixed_samples(value, size)))
    parts_copy.wait()
    for step in range(done, out.shape[0] // LAT, 2):
        dense = dense_rows(parts_held, step)
        if step == done:
            value = halved_product(dense, held, copies)
        else:
            value = jnp.dot(dense, held[...], preferred_element_type=jnp.float32)
        value = mixed_samples(value, size)
        sending.append(send_rows(ready, out, sent, step, value))
    token[...] = size[0][0] + jnp.zeros(token.shape, jnp.float32)
    for copy in sending:
        copy.wait()


def last_body(
    me, everyone, image_in, direction, sizes, norm, flux_one, flux_two,
    answer, flux, one, two, ready, one_arrived, two_arrived, sent,
):
    two_copies = fetch(flux_two, two, two_arrived)
    one_copies = fetch(flux_one, one, one_arrived)
    second = direction[...]
    image = with_variance(image_in[...], everyone, second)
    size_two = row_solve(row_gram(second, image), entries(norm))
    own = row_combine(everyone[me[0], 0:8, :], row_weights(entries(sizes)))
    own = own + row_combine(direction[me[0]], row_weights(size_two))
    for k in range(SAMPLES):
        for b in range(2):
            answer[b, k : k + 1, :] = own[2 * k + b : 2 * k + b + 1]

    steps = ready.shape[0]
    piece = steps // len(one_copies)
    sending = []
    for t in range(steps):
        if t % piece == 0:
            two_copies[t // piece].wait()
            one_copies[t // piece].wait()
        at = slice(t * LAT, (t + 1) * LAT)
        parts = [two[at, k * LON : (k + 1) * LON] for k in range(SAMPLES)]
        for j in range(SAMPLES):
            value = one[at, j * LON : (j + 1) * LON]
            for k in range(SAMPLES):
                value = value + parts[k] * size_two[k][j]
            ready[t, :, j, :] = value
        copy = pltpu.make_async_copy(ready.at[t], flux.at[t], sent.at[t])
        copy.start()
        sending.append(copy)
    for copy in sending:
        copy.wait()


MIB = 1024 * 1024


def shape_of(shape, dtype):
    return jax.ShapeDtypeStruct(shape, dtype)


def cost(flops, moved):
    return pl.CostEstimate(flops=flops, bytes_accessed=moved, transcendentals=0)


def by_columns(
    right_sides, obs_var, footprint, tile_block, tile_place, time_cov, lat_cov, lon_cov
):
    devices = lax.axis_size("tm")
    me = lax.axis_index("tm").reshape(1).astype(jnp.int32)
    steps_here = time_cov.shape[0] // devices
    tiles = tile_block.size
    every_tile = devices * tiles
    columns = SAMPLES * LON
    width = columns // devices
    rows_here = steps_here * LAT
    f32, bf16 = jnp.float32, jnp.bfloat16

    vmem = pl.BlockSpec(memory_space=pltpu.VMEM)
    smem = pl.BlockSpec(memory_space=pltpu.SMEM)
    hbm = pl.BlockSpec(memory_space=pltpu.HBM)
    vector_shape = shape_of((devices, 8, BLOCK_OBS), f32)
    column_shape = shape_of((devices, width, tiles), bf16)
    tile_shape = shape_of((tiles, columns), bf16)
    small_shape = shape_of((SAMPLES * SAMPLES, 128), f32)
    field_shape = shape_of((rows_here, columns), f32)
    parts_shape = shape_of((LAT + steps_here, every_tile), f32)
    token_shape = shape_of((8, 128), f32)
    prior_shape = shape_of((every_tile // 2, every_tile), bf16)
    flux_shape = shape_of((steps_here, LAT, SAMPLES, LON), f32)

    def flags(count):
        return pltpu.SemaphoreType.DMA((count,))

    products = pltpu.VMEM((tiles, 8, LON), f32)
    field = pltpu.VMEM(field_shape.shape, f32)
    gathered_held = pltpu.VMEM((every_tile, columns), bf16)
    prior_held = pltpu.VMEM(prior_shape.shape, bf16)
    spread_scratch = [products, pltpu.VMEM(footprint.shape, bf16), flags(4)]
    spread_scratch += [pltpu.VMEM((2, 128, 128), f32), pltpu.SemaphoreType.DMA]
    flux_scratch = [field, pltpu.VMEM(parts_shape.shape, f32), gathered_held]
    flux_scratch += [flags(1), flags(PIECES), flags(steps_here // 2)]
    tile_cost = cost(2 * 8 * footprint.size, footprint.size * 2)
    flux_cost = cost(2 * rows_here * every_tile * columns, every_tile * columns * 2)

    def call(body, in_specs, out_specs, out_shape, scratch, estimate, name, grant=53):
        return pl.pallas_call(
            body,
            in_specs=in_specs,
            out_specs=out_specs,
            out_shape=out_shape,
            scratch_shapes=scratch,
            compiler_params=pltpu.CompilerParams(vmem_limit_bytes=grant * MIB),
            cost_estimate=estimate,
            name=name,
        )

    def exchange(array):
        return lax.all_to_all(array, "tm", split_axis=0, concat_axis=0, tiled=True)

    pair_scratch = [pltpu.VMEM((2, 128, 128), f32), pltpu.SemaphoreType.DMA]
    packed, mask, shelf = call(
        pack_body,
        [vmem] * 5,
        [vmem, vmem, hbm],
        [
            shape_of((devices, 16, 128), f32),
            shape_of((128, 128), f32),
            shape_of((64, 128, 128), f32),
        ],
        pair_scratch,
        cost(0, 12 * MIB),
        "pack",
        59,
    )(right_sides, obs_var, tile_place.T, tile_block.T, lon_cov)
    everyone = exchange(packed)
    by_column, by_tile = call(
        first_body,
        [vmem, hbm, hbm],
        [vmem] * 2,
        [column_shape, tile_shape],
        spread_scratch,
        tile_cost,
        "spread_first",
    )(everyone, shelf, footprint)
    gathered_one = lax.all_gather(by_tile, "tm", axis=0, tiled=True)

    hot_shape = shape_of((2, every_tile // 2, 2 * LAT), bf16)
    cols_shape = shape_of((2, 2 * LAT, every_tile), bf16)
    prior_one, parts, hot, cols = call(
        build_body,
        [smem] + [vmem] * 3,
        [hbm] * 4,
        [prior_shape, parts_shape, hot_shape, cols_shape],
        [
            prior_held,
            pltpu.VMEM((2, every_tile, 2 * LAT), bf16),
            pltpu.VMEM(cols_shape.shape, bf16),
            pltpu.VMEM((LAT, every_tile), f32),
            pltpu.VMEM(parts_shape.shape, f32),
            flags(4),
            flags(3),
        ],
        cost(2 * every_tile * every_tile * 256, every_tile * every_tile * 2),
        "build_prior",
    )(me, everyone, time_cov, lat_cov)

    def flux_product(after, gathered, rows):
        return call(
            functools.partial(flux_product_body, rows),
            [hbm, hbm, hbm],
            [hbm, vmem],
            [field_shape, token_shape],
            flux_scratch,
            flux_cost,
            "flux_product",
        )(after, parts, gathered)

    mix_total = pltpu.VMEM((width, every_tile), f32)
    mix_cost = cost(2 * width * every_tile**2, every_tile**2 * 2)
    mixed, prior_two = call(
        build_mix_body,
        [vmem] + [hbm] * 3,
        [vmem, hbm],
        [column_shape, prior_shape],
        [
            mix_total,
            pltpu.VMEM(hot_shape.shape, bf16),
            pltpu.VMEM(cols_shape.shape, bf16),
            prior_held,
            prior_held,
            flags(2),
            flags(4),
            flags(4),
        ],
        mix_cost,
        "build_mix",
    )(exchange(by_column), hot, cols, prior_one)

    def mix(by_column, after):
        return call(
            mix_body,
            [vmem] + [hbm] * 3,
            vmem,
            column_shape,
            [mix_total, prior_held, prior_held, flags(4), flags(4)],
            mix_cost,
            "mix_columns",
        )(exchange(by_column), prior_one, prior_two, after)

    def collect(values):
        sums = call(
            collect_body, [vmem] * 3, vmem, vector_shape, [products], tile_cost, "collect", 48
        )(values, mask, footprint)
        own, copies = call(
            sum_body,
            [vmem],
            [vmem] * 2,
            [shape_of((8, BLOCK_OBS), f32), vector_shape],
            [],
            cost(0, 4 * MIB),
            "sum_terms",
        )(exchange(sums))
        return own, exchange(copies)

    own_image, image = collect(exchange(mixed))
    product_one, token = flux_product(own_image, gathered_one, rows_here // 2)
    by_column, by_tile, direction, sizes, norm = call(
        update_body,
        [vmem] * 2 + [hbm] * 3,
        [vmem] * 5,
        [column_shape, tile_shape, vector_shape, small_shape, small_shape],
        spread_scratch,
        tile_cost,
        "update_spread",
    )(everyone, image, shelf, footprint, token)
    gathered_two = lax.all_gather(by_tile, "tm", axis=0, tiled=True)
    flux_one, token = call(
        flux_first_body,
        [vmem, hbm, hbm, hbm],
        [hbm, vmem],
        [field_shape, token_shape],
        flux_scratch + [pltpu.VMEM((rows_here // 2, columns), f32), flags(2)],
        flux_cost,
        "flux_first",
    )(sizes, product_one, parts, gathered_one)

    own_image, image = collect(exchange(mix(by_column, token)))
    flux_two, _ = flux_product(own_image, gathered_two, rows_here)

    answer, flux = call(
        last_body,
        [smem] + [vmem] * 5 + [hbm] * 2,
        [vmem, hbm],
        [shape_of(right_sides.shape, f32), flux_shape],
        [field, field, pltpu.VMEM(flux_shape.shape, f32), flags(4), flags(4), flags(steps_here)],
        cost(1 << 20, 6 << 20),
        "last",
    )(me, everyone, image, direction, sizes, norm, flux_one, flux_two)
    return (answer, flux)


def local(right_sides, obs_var, footprint, tile_block, tile_place, *covariances):
    devices = lax.axis_size("tm")
    tiles = tile_block.size
    fits = devices * tiles <= 2048 and devices % 4 == 0 and tiles == 128
    fits = fits and right_sides.shape[0] == 2 and (SAMPLES * LON) % (32 * devices) == 0
    fits = fits and (covariances[0].shape[0] // devices) % 4 == 0
    plan = by_columns if fits else by_gather
    return plan(right_sides, obs_var, footprint, tile_block, tile_place, *covariances)


def solution(mesh):
    in_specs = (
        P(("grp", "tm"), None, None),
        P(("grp", "tm"), None),
        P(("grp", "tm"), None, None, None),
        P(("grp", "tm"), None),
        P(("grp", "tm"), None),
        P(),
        P(),
        P(),
    )
    out_specs = (P(("grp", "tm"), None, None), P(("grp", "tm"), None, None, None))
    return jax.shard_map(local, mesh=mesh, in_specs=in_specs, out_specs=out_specs, check_vma=False)
```

```python
import functools

import jax
import jax.numpy as jnp
from jax import lax
from jax.experimental import pallas as pl
from jax.experimental.pallas import tpu as pltpu
from jax.sharding import PartitionSpec as P

LAT = 128
LON = 128
BLOCK_OBS = 128
SAMPLES = 4
ITERS = 2


precise = lax.Precision.HIGHEST


def solve_spd(matrix, target):
    factor = jnp.linalg.cholesky(matrix)
    halfway = lax.linalg.triangular_solve(factor, target, left_side=True, lower=True)
    return lax.linalg.triangular_solve(
        factor, halfway, left_side=True, lower=True, transpose_a=True
    )


def combine(vectors, weights):
    return jnp.einsum("nks,kj->njs", vectors, weights, precision=precise)


def gram(left, right):
    return jnp.einsum("nks,njs->kj", left, right, precision=precise)


def to_all(array):
    devices = lax.axis_size("tm")
    copies = jnp.broadcast_to(array[None], (devices,) + array.shape)
    return lax.all_to_all(copies, "tm", split_axis=0, concat_axis=0, tiled=True)


def by_gather(
    right_sides, obs_var, footprint, tile_block, tile_place, time_cov, lat_cov, lon_cov
):
    devices = lax.axis_size("tm")
    me = lax.axis_index("tm")
    owned = right_sides.shape[0]
    blocks = devices * owned
    steps_here = time_cov.shape[0] // devices
    slots = tile_block.shape[1]
    tiles = devices * slots
    rows_here = steps_here * LAT
    owner_base = (jnp.arange(devices, dtype=jnp.int32) * owned)[:, None]
    requests = owner_base + tile_block

    packed = jnp.concatenate(
        [
            right_sides.reshape(-1, 128),
            obs_var.reshape(-1, 128),
            tile_place.astype(jnp.float32).reshape(-1, 128),
        ]
    )
    everyone = to_all(packed)
    at = owned * SAMPLES
    rhs = everyone[:, :at].reshape(blocks, SAMPLES, BLOCK_OBS)
    variance = everyone[:, at : at + owned].reshape(blocks, BLOCK_OBS)
    places = everyone[:, at + owned :].reshape(devices, tiles).astype(jnp.int32)
    times = (places // LAT + steps_here * jnp.arange(devices, dtype=jnp.int32)[:, None]).reshape(-1)
    rows = (places % LAT).reshape(-1)
    time_hot = (jnp.arange(time_cov.shape[0])[:, None] == times[None, :]).astype(jnp.float32)
    row_hot = (jnp.arange(LAT)[:, None] == rows[None, :]).astype(jnp.float32)
    my_times = lax.dynamic_slice_in_dim(time_cov, me * steps_here, steps_here, 0)
    time_part = jnp.dot(my_times, time_hot, precision=precise)
    row_part = jnp.dot(lat_cov, row_hot, precision=precise)
    dense = (time_part[:, None, :] * row_part[None, :, :]).astype(jnp.bfloat16)
    dense = dense.reshape(rows_here, devices * tiles)
    mine = jnp.take(dense, tile_place.reshape(-1), axis=0)

    def spread(vectors):
        chosen = jnp.take(vectors.astype(jnp.bfloat16), requests, axis=0)
        contrib = jnp.einsum(
            "ocks,ocsl->ockl", chosen, footprint, preferred_element_type=jnp.float32
        )
        contrib = contrib.astype(jnp.bfloat16).reshape(tiles, SAMPLES * LON)
        return lax.all_gather(contrib, "tm", axis=0, tiled=True)

    def collect(gathered):
        field = jnp.dot(mine, gathered, preferred_element_type=jnp.float32)
        field = jnp.dot(field.reshape(-1, LON), lon_cov, precision=precise)
        picked = field.astype(jnp.bfloat16).reshape(devices, slots, SAMPLES, LON)
        partial = jnp.einsum(
            "ockl,ocsl->ocks", picked, footprint, preferred_element_type=jnp.float32
        )
        block_range = jnp.arange(owned, dtype=jnp.int32)
        selector = (tile_block[:, :, None] == block_range).astype(jnp.float32)
        summed = jnp.einsum("ocb,ocks->obks", selector, partial, precision=precise)
        terms = lax.all_to_all(
            summed.reshape(devices, owned * SAMPLES, BLOCK_OBS), "tm", 0, 0, tiled=True
        )
        return to_all(terms.sum(0)).reshape(blocks, SAMPLES, BLOCK_OBS)

    solution = jnp.zeros_like(rhs)
    residual = rhs
    direction = rhs
    norm_now = gram(rhs, rhs)
    gathers, sizes = [], []
    for step in range(ITERS):
        gathered = spread(direction)
        image = collect(gathered) + variance[:, None, :] * direction
        step_size = solve_spd(gram(direction, image), norm_now)
        gathers.append(gathered)
        sizes.append(step_size)
        solution = solution + combine(direction, step_size)
        if step + 1 == ITERS:
            break
        residual = residual - combine(image, step_size)
        norm_next = gram(residual, residual)
        mix_ratio = solve_spd(norm_now, norm_next)
        direction = residual + combine(direction, mix_ratio)
        norm_now = norm_next

    def mix(gathered, size):
        whole = gathered.astype(jnp.float32).reshape(-1, SAMPLES, LON)
        return jnp.einsum("tkl,kj->tjl", whole, size, precision=precise)

    def apply_dense(gathered):
        return jnp.dot(dense, gathered, preferred_element_type=jnp.float32)

    if rows_here < devices * tiles // 4:
        flux = sum(mix(apply_dense(g), size) for g, size in zip(gathers, sizes))
    else:
        total = sum(mix(g, size) for g, size in zip(gathers, sizes))
        flux = apply_dense(total.astype(jnp.bfloat16).reshape(-1, SAMPLES * LON))
    flux = jnp.dot(flux.reshape(-1, LON), lon_cov, precision=precise)
    mine_now = lax.dynamic_slice_in_dim(solution, me * owned, owned, 0)
    return (mine_now, flux.reshape(steps_here, LAT, SAMPLES, LON))


def rolled(x, shift):
    return x if shift == 0 else pltpu.roll(x, 8 - 2 * shift, x.ndim - 2)


def row_gram(left, right):
    entry = [[None] * SAMPLES for _ in range(SAMPLES)]
    for shift in range(SAMPLES):
        product = jnp.sum(left * rolled(right, shift), axis=0)
        total = jnp.broadcast_to(jnp.sum(product, axis=1, keepdims=True), product.shape)
        for k in range(SAMPLES):
            pair = total[2 * k : 2 * k + 1] + total[2 * k + 1 : 2 * k + 2]
            entry[k][(k + shift) % SAMPLES] = pair
    return entry


def row_solve(matrix, target):
    size = range(SAMPLES)
    sym = [[0.5 * (matrix[i][j] + matrix[j][i]) for j in size] for i in size]
    low = [[None] * SAMPLES for _ in size]
    scaled = [[None] * SAMPLES for _ in size]
    inverse = []
    for j in size:
        pivot = sym[j][j]
        for p in range(j):
            pivot = pivot - low[j][p] * scaled[j][p]
        inverse.append(1.0 / pivot)
        for i in range(j + 1, SAMPLES):
            value = sym[i][j]
            for p in range(j):
                value = value - scaled[i][p] * low[j][p]
            scaled[i][j] = value
            low[i][j] = value * inverse[j]
    out = [[None] * SAMPLES for _ in size]
    for c in size:
        part = []
        for i in size:
            value = target[i][c]
            for p in range(i):
                value = value - low[i][p] * part[p]
            part.append(value)
        for i in reversed(size):
            value = part[i] * inverse[i]
            for p in range(i + 1, SAMPLES):
                value = value - low[p][i] * out[p][c]
            out[i][c] = value
    return out


def row_weights(weights):
    sample = lax.broadcasted_iota(jnp.int32, (8, 128), 0) // 2
    result = []
    for shift in range(SAMPLES):
        rows = jnp.broadcast_to(weights[shift][0], (8, 128))
        for j in range(1, SAMPLES):
            rows = jnp.where(sample == j, weights[(j + shift) % SAMPLES][j], rows)
        result.append(rows)
    return result


def row_combine(x, per_shift):
    total = 0.0
    for shift in range(SAMPLES):
        total = total + rolled(x, shift) * per_shift[shift]
    return total


PIECES = 8


def fetch(source, held, arrived, ahead=None):
    pieces = arrived.shape[0]
    size = source.shape[0] // pieces
    copies = []
    for p in range(pieces):
        at = pl.ds(p * size, size)
        copies.append(pltpu.make_async_copy(source.at[at], held.at[at], arrived.at[p]))
    for copy in copies[:ahead]:
        copy.start()
    return copies


def arrive(copies, p, ahead):
    copies[p].wait()
    if p + ahead < len(copies):
        copies[p + ahead].start()


def second_of(tile_block):
    slots, owners = tile_block.shape
    tiles = owners * slots
    tile = lax.broadcasted_iota(jnp.int32, (tiles, slots), 0)
    slot = lax.broadcasted_iota(jnp.int32, (tiles, slots), 1)
    rows = jnp.dot(
        (tile % slots == slot).astype(jnp.float32),
        tile_block[...].astype(jnp.float32),
        preferred_element_type=jnp.float32,
    )
    tile = lax.broadcasted_iota(jnp.int32, (tiles, owners), 0)
    owner = lax.broadcasted_iota(jnp.int32, (tiles, owners), 1)
    return jnp.sum(jnp.where(tile // slots == owner, rows, 0.0), axis=1, keepdims=True)


def pack_body(right_sides, obs_var, tile_place, tile_block, lon, copies, mask, shelf, pair, sent):
    slots, owners = tile_place.shape
    tiles = owners * slots
    owner = lax.broadcasted_iota(jnp.int32, (owners, tiles), 0)
    lane = lax.broadcasted_iota(jnp.int32, (owners, tiles), 1)
    spread_out = jnp.dot(
        tile_place[...].astype(jnp.float32),
        (lane // slots == owner).astype(jnp.float32),
        precision=precise,
        preferred_element_type=jnp.float32,
    )
    slot = lax.broadcasted_iota(jnp.int32, (slots, tiles), 0)
    lane = lax.broadcasted_iota(jnp.int32, (slots, tiles), 1)
    place = jnp.sum(jnp.where(lane % slots == slot, spread_out, 0.0), axis=0, keepdims=True)
    for k in range(SAMPLES):
        for b in range(2):
            copies[0, 2 * k + b : 2 * k + b + 1] = right_sides[b, k : k + 1]
    copies[0, 8:10] = obs_var[...]
    copies[0, 10:11] = place
    copies[0, 11:16] = jnp.zeros((5, tiles), jnp.float32)
    for d in range(1, copies.shape[0]):
        copies[d] = copies[0]
    second = jnp.broadcast_to(second_of(tile_block), lon.shape)
    mask[...] = second
    pair[0] = second
    pair[1] = lon[...]
    shelve = pltpu.make_async_copy(pair, shelf.at[0:2], sent)
    shelve.start()
    shelve.wait()


def spread_tiles(vectors, held, copies, products, split):
    owners, slots = held.shape[:2]
    piece = owners // len(copies)
    for owner in range(owners):
        if owner % piece == 0:
            arrive(copies, owner // piece, 2)
        rows = vectors[owner, 0:8]
        lhs = rows.astype(jnp.bfloat16)
        if split:
            upper = lhs.astype(jnp.float32)
            lhs = jnp.concatenate([upper, rows - upper], axis=0).astype(jnp.bfloat16)
        for c in range(slots):
            r = jnp.dot(lhs, held[owner, c], preferred_element_type=jnp.float32)
            products[owner * slots + c] = r[:8] + r[8:] if split else r


def spread_end(products, mask_lon, by_column, by_tile):
    second = mask_lon[0] > 0.5
    width = by_column.shape[1]
    chunks = LON // width
    for k in range(SAMPLES):
        chosen = jnp.where(second, products[:, 2 * k + 1, :], products[:, 2 * k, :])
        mixed = jnp.dot(
            chosen, mask_lon[1], precision=precise, preferred_element_type=jnp.float32
        )
        by_tile[:, k * LON : (k + 1) * LON] = mixed.astype(jnp.bfloat16)
        turned = mixed.T.astype(jnp.bfloat16)
        by_column[k * chunks : (k + 1) * chunks] = turned.reshape(chunks, width, LON)


def first_body(
    everyone, shelf, footprint,
    by_column, by_tile, products, held, arrived, mask_lon, shelf_arrived,
):
    shelf_copy = pltpu.make_async_copy(shelf.at[0:2], mask_lon, shelf_arrived)
    shelf_copy.start()
    copies = fetch(footprint, held, arrived, 2)
    spread_tiles(everyone, held, copies, products, False)
    shelf_copy.wait()
    spread_end(products, mask_lon, by_column, by_tile)


def with_variance(image, everyone, vectors):
    block = lax.broadcasted_iota(jnp.int32, vectors.shape, 1) % 2
    variance = jnp.where(block == 0, everyone[:, 8:9, :], everyone[:, 9:10, :])
    return image + variance * vectors


def entries(ref):
    grid = range(SAMPLES)
    return [[ref[SAMPLES * k + j : SAMPLES * k + j + 1] for j in grid] for k in grid]


def keep(ref, matrix):
    for k in range(SAMPLES):
        for j in range(SAMPLES):
            ref[SAMPLES * k + j : SAMPLES * k + j + 1] = matrix[k][j]


def update_body(
    everyone, image_in, shelf, footprint, after,
    by_column, by_tile, direction, sizes, norm,
    products, held, arrived, mask_lon, shelf_arrived,
):
    del after
    shelf_copy = pltpu.make_async_copy(shelf.at[0:2], mask_lon, shelf_arrived)
    shelf_copy.start()
    copies = fetch(footprint, held, arrived, 2)
    first = everyone[:, 0:8, :]
    image = with_variance(image_in[...], everyone, first)
    norm_now = row_gram(first, first)
    step_size = row_solve(row_gram(first, image), norm_now)
    residual = first - row_combine(image, row_weights(step_size))
    norm_next = row_gram(residual, residual)
    ratio = row_solve(norm_now, norm_next)
    direction[...] = residual + row_combine(first, row_weights(ratio))
    keep(sizes, step_size)
    keep(norm, norm_next)
    spread_tiles(direction, held, copies, products, True)
    shelf_copy.wait()
    spread_end(products, mask_lon, by_column, by_tile)


def build_body(
    me, everyone, time_cov, lat_cov,
    prior_out, parts_out, tile_prior, hot, cols, times, parts, sent, parts_sent,
):
    devices, tiles = everyone.shape[0], everyone.shape[2]
    steps_here = parts.shape[0] - LAT
    at = lax.broadcasted_iota(jnp.int32, (LAT, tiles), 0)
    for kind, cov in ((0, time_cov), (1, lat_cov)):
        whole_cov = cov[...]
        upper = whole_cov.astype(jnp.bfloat16)
        lower = (whole_cov - upper.astype(jnp.float32)).astype(jnp.bfloat16)
        ones = []
        for d in range(devices):
            place = (everyone[d, 10:11, :] + 0.5).astype(jnp.int32)
            where = place // LAT + steps_here * d if kind == 0 else place % LAT
            one = (at == where).astype(jnp.float32)
            ones.append(one.astype(jnp.bfloat16))
            turned = one.T.astype(jnp.bfloat16)
            here = slice(d * tiles, (d + 1) * tiles)
            hot[kind, here, 0:LAT] = turned
            hot[kind, here, LAT : 2 * LAT] = turned
        picked = jnp.dot(
            jnp.concatenate([upper, lower], axis=0),
            jnp.concatenate(ones, axis=1),
            preferred_element_type=jnp.float32,
        )
        cols[kind] = picked.astype(jnp.bfloat16)
        both = picked[:LAT] + picked[LAT:]
        if kind == 0:
            times[...] = both
            mine = pl.ds(pl.multiple_of(me[0] * steps_here, steps_here), steps_here)
            parts[LAT:] = times[mine, :]
        else:
            parts[:LAT] = both

    parts_copy = pltpu.make_async_copy(parts, parts_out, parts_sent)
    parts_copy.start()
    rows = tile_prior.shape[0] // PIECES

    def sending(piece):
        block = pl.ds(pl.multiple_of(piece * rows, rows), rows)
        return pltpu.make_async_copy(
            tile_prior.at[block], prior_out.at[block], sent.at[piece]
        )

    @pl.loop(0, PIECES)
    def _(piece):
        block = pl.ds(pl.multiple_of(piece * rows, rows), rows)
        by_time = jnp.dot(hot[0, block, :], cols[0], preferred_element_type=jnp.float32)
        by_row = jnp.dot(hot[1, block, :], cols[1], preferred_element_type=jnp.float32)
        tile_prior[block, :] = (by_time * by_row).astype(jnp.bfloat16)
        sending(piece).start()

    parts_copy.wait()
    for piece in range(PIECES):
        sending(piece).wait()


def mix_body(columns, tile_prior, *rest):
    mixed, total, held, arrived = rest[-4:]
    copies = fetch(tile_prior, held, arrived, 3)
    devices, width, tiles = columns.shape
    part = devices // len(copies)
    for p in range(len(copies)):
        at = range(p * part, (p + 1) * part)
        lhs = jnp.concatenate([columns[d] for d in at], axis=1)
        arrive(copies, p, 3)
        product = jnp.dot(
            lhs,
            held[p * part * tiles : (p + 1) * part * tiles],
            preferred_element_type=jnp.float32,
        )
        total[...] = product if p == 0 else total[...] + product
    for d in range(devices):
        mixed[d] = total[:, d * tiles : (d + 1) * tiles].astype(jnp.bfloat16)


def sum_body(terms, total, copies):
    value = jnp.sum(terms[...], axis=0)
    total[...] = value
    for d in range(copies.shape[0]):
        copies[d] = value


def collect_body(values, mask, footprint, sums, rows):
    chunks = values.shape[0] // SAMPLES
    owners, slots = footprint.shape[:2]
    is_second = mask[...] > 0.5
    for k in range(SAMPLES):
        turned = values[k * chunks : (k + 1) * chunks].reshape(LON, -1)
        turned = turned.astype(jnp.float32).T
        rows[:, 2 * k, :] = jnp.where(is_second, 0.0, turned)
        rows[:, 2 * k + 1, :] = jnp.where(is_second, turned, 0.0)
    for owner in range(owners):
        total = 0.0
        for c in range(slots):
            total = total + lax.dot_general(
                rows[owner * slots + c].astype(jnp.bfloat16),
                footprint[owner, c],
                (((1,), (1,)), ((), ())),
                preferred_element_type=jnp.float32,
            )
        sums[owner] = total


def dense_rows(parts, first):
    rows = []
    for t in range(first, first + 2):
        rows.append((parts[LAT + t : LAT + t + 1, :] * parts[:LAT]).astype(jnp.bfloat16))
    return jnp.concatenate(rows, axis=0)


def send_rows(ready, out, sent, step, value):
    at = pl.ds(step * LAT, 2 * LAT)
    ready[at] = value
    copy = pltpu.make_async_copy(ready.at[at], out.at[at], sent.at[step // 2])
    copy.start()
    return copy


def halved_product(dense, held, copies):
    half = held.shape[0] // 2
    total = 0.0
    for h in range(2):
        for copy in copies[h * PIECES // 2 : (h + 1) * PIECES // 2]:
            copy.wait()
        at = slice(h * half, (h + 1) * half)
        total = total + jnp.dot(dense[:, at], held[at], preferred_element_type=jnp.float32)
    return total


def mixed_samples(value, size):
    pieces = [value[:, k * LON : (k + 1) * LON] for k in range(SAMPLES)]
    mixed = []
    for j in range(SAMPLES):
        mixed.append(sum(pieces[k] * size[k][j] for k in range(SAMPLES)))
    return jnp.concatenate(mixed, axis=1)


def flux_product_body(
    rows, after, parts, gathered, out, token,
    ready, parts_held, held, parts_arrived, arrived, sent,
):
    del after
    (parts_copy,) = fetch(parts, parts_held, parts_arrived)
    copies = fetch(gathered, held, arrived)
    parts_copy.wait()
    sending = []
    for step in range(0, rows // LAT, 2):
        dense = dense_rows(parts_held, step)
        if step == 0:
            value = halved_product(dense, held, copies)
            token[...] = value[0:8, 0:128]
        else:
            value = jnp.dot(dense, held[...], preferred_element_type=jnp.float32)
        sending.append(send_rows(ready, out, sent, step, value))
    for copy in sending:
        copy.wait()


def flux_first_body(
    sizes, product, parts, gathered, out, token,
    ready, parts_held, held, parts_arrived, arrived, sent, product_held, product_arrived,
):
    done = product_held.shape[0] // LAT
    product_copies = fetch(product.at[: done * LAT], product_held, product_arrived)
    (parts_copy,) = fetch(parts, parts_held, parts_arrived)
    copies = fetch(gathered, held, arrived)
    size = entries(sizes)
    sending = []
    for copy in product_copies:
        copy.wait()
    for step in range(0, done, 2):
        value = product_held[step * LAT : (step + 2) * LAT]
        sending.append(send_rows(ready, out, sent, step, mixed_samples(value, size)))
    parts_copy.wait()
    for step in range(done, out.shape[0] // LAT, 2):
        dense = dense_rows(parts_held, step)
        if step == done:
            value = halved_product(dense, held, copies)
        else:
            value = jnp.dot(dense, held[...], preferred_element_type=jnp.float32)
        value = mixed_samples(value, size)
        sending.append(send_rows(ready, out, sent, step, value))
    token[...] = size[0][0] + jnp.zeros(token.shape, jnp.float32)
    for copy in sending:
        copy.wait()


def last_body(
    me, everyone, image_in, direction, sizes, norm, flux_one, flux_two,
    answer, flux, one, two, ready, one_arrived, two_arrived, sent,
):
    two_copies = fetch(flux_two, two, two_arrived)
    one_copies = fetch(flux_one, one, one_arrived)
    second = direction[...]
    image = with_variance(image_in[...], everyone, second)
    size_two = row_solve(row_gram(second, image), entries(norm))
    own = row_combine(everyone[me[0], 0:8, :], row_weights(entries(sizes)))
    own = own + row_combine(direction[me[0]], row_weights(size_two))
    for k in range(SAMPLES):
        for b in range(2):
            answer[b, k : k + 1, :] = own[2 * k + b : 2 * k + b + 1]

    steps = ready.shape[0]
    piece = steps // len(one_copies)
    sending = []
    for t in range(steps):
        if t % piece == 0:
            two_copies[t // piece].wait()
            one_copies[t // piece].wait()
        at = slice(t * LAT, (t + 1) * LAT)
        parts = [two[at, k * LON : (k + 1) * LON] for k in range(SAMPLES)]
        for j in range(SAMPLES):
            value = one[at, j * LON : (j + 1) * LON]
            for k in range(SAMPLES):
                value = value + parts[k] * size_two[k][j]
            ready[t, :, j, :] = value
        copy = pltpu.make_async_copy(ready.at[t], flux.at[t], sent.at[t])
        copy.start()
        sending.append(copy)
    for copy in sending:
        copy.wait()


MIB = 1024 * 1024


def shape_of(shape, dtype):
    return jax.ShapeDtypeStruct(shape, dtype)


def cost(flops, moved):
    return pl.CostEstimate(flops=flops, bytes_accessed=moved, transcendentals=0)


def by_columns(
    right_sides, obs_var, footprint, tile_block, tile_place, time_cov, lat_cov, lon_cov
):
    devices = lax.axis_size("tm")
    me = lax.axis_index("tm").reshape(1).astype(jnp.int32)
    steps_here = time_cov.shape[0] // devices
    tiles = tile_block.size
    every_tile = devices * tiles
    columns = SAMPLES * LON
    width = columns // devices
    rows_here = steps_here * LAT
    f32, bf16 = jnp.float32, jnp.bfloat16

    vmem = pl.BlockSpec(memory_space=pltpu.VMEM)
    smem = pl.BlockSpec(memory_space=pltpu.SMEM)
    hbm = pl.BlockSpec(memory_space=pltpu.HBM)
    vector_shape = shape_of((devices, 8, BLOCK_OBS), f32)
    column_shape = shape_of((devices, width, tiles), bf16)
    tile_shape = shape_of((tiles, columns), bf16)
    small_shape = shape_of((SAMPLES * SAMPLES, 128), f32)
    field_shape = shape_of((rows_here, columns), f32)
    parts_shape = shape_of((LAT + steps_here, every_tile), f32)
    token_shape = shape_of((8, 128), f32)
    prior_shape = shape_of((every_tile, every_tile), bf16)
    flux_shape = shape_of((steps_here, LAT, SAMPLES, LON), f32)

    def flags(count):
        return pltpu.SemaphoreType.DMA((count,))

    products = pltpu.VMEM((tiles, 8, LON), f32)
    field = pltpu.VMEM(field_shape.shape, f32)
    gathered_held = pltpu.VMEM((every_tile, columns), bf16)
    prior_held = pltpu.VMEM(prior_shape.shape, bf16)
    spread_scratch = [products, pltpu.VMEM(footprint.shape, bf16), flags(PIECES)]
    spread_scratch += [pltpu.VMEM((2, 128, 128), f32), pltpu.SemaphoreType.DMA]
    flux_scratch = [field, pltpu.VMEM(parts_shape.shape, f32), gathered_held]
    flux_scratch += [flags(1), flags(PIECES), flags(steps_here // 2)]
    tile_cost = cost(2 * 8 * footprint.size, footprint.size * 2)
    flux_cost = cost(2 * rows_here * every_tile * columns, every_tile * columns * 2)

    def call(body, in_specs, out_specs, out_shape, scratch, estimate, name, grant=53):
        return pl.pallas_call(
            body,
            in_specs=in_specs,
            out_specs=out_specs,
            out_shape=out_shape,
            scratch_shapes=scratch,
            compiler_params=pltpu.CompilerParams(vmem_limit_bytes=grant * MIB),
            cost_estimate=estimate,
            name=name,
        )

    def exchange(array):
        return lax.all_to_all(array, "tm", split_axis=0, concat_axis=0, tiled=True)

    pair_scratch = [pltpu.VMEM((2, 128, 128), f32), pltpu.SemaphoreType.DMA]
    packed, mask, shelf = call(
        pack_body,
        [vmem] * 5,
        [vmem, vmem, hbm],
        [
            shape_of((devices, 16, 128), f32),
            shape_of((128, 128), f32),
            shape_of((64, 128, 128), f32),
        ],
        pair_scratch,
        cost(0, 12 * MIB),
        "pack",
        59,
    )(right_sides, obs_var, tile_place.T, tile_block.T, lon_cov)
    everyone = exchange(packed)
    by_column, by_tile = call(
        first_body,
        [vmem, hbm, hbm],
        [vmem] * 2,
        [column_shape, tile_shape],
        spread_scratch,
        tile_cost,
        "spread_first",
    )(everyone, shelf, footprint)
    gathered_one = lax.all_gather(by_tile, "tm", axis=0, tiled=True)

    tile_prior, parts = call(
        build_body,
        [smem] + [vmem] * 3,
        [hbm, hbm],
        [prior_shape, parts_shape],
        [
            prior_held,
            pltpu.VMEM((2, every_tile, 2 * LAT), bf16),
            pltpu.VMEM((2, 2 * LAT, every_tile), bf16),
            pltpu.VMEM((LAT, every_tile), f32),
            pltpu.VMEM(parts_shape.shape, f32),
            flags(PIECES),
            pltpu.SemaphoreType.DMA,
        ],
        cost(4 * every_tile * every_tile * 256, every_tile * every_tile * 2),
        "build_prior",
    )(me, everyone, time_cov, lat_cov)

    def flux_product(after, gathered, rows):
        return call(
            functools.partial(flux_product_body, rows),
            [hbm, hbm, hbm],
            [hbm, vmem],
            [field_shape, token_shape],
            flux_scratch,
            flux_cost,
            "flux_product",
        )(after, parts, gathered)

    def prior(by_column, *after):
        mixed = call(
            mix_body,
            [vmem, hbm] + [hbm] * len(after),
            vmem,
            column_shape,
            [pltpu.VMEM((width, every_tile), f32), prior_held, flags(PIECES)],
            cost(2 * width * every_tile**2, every_tile**2 * 2),
            "mix_columns",
        )(exchange(by_column), tile_prior, *after)
        return exchange(mixed)

    def collect(values):
        sums = call(
            collect_body, [vmem] * 3, vmem, vector_shape, [products], tile_cost, "collect", 48
        )(values, mask, footprint)
        own, copies = call(
            sum_body,
            [vmem],
            [vmem] * 2,
            [shape_of((8, BLOCK_OBS), f32), vector_shape],
            [],
            cost(0, 4 * MIB),
            "sum_terms",
        )(exchange(sums))
        return own, exchange(copies)

    own_image, image = collect(prior(by_column))
    product_one, token = flux_product(own_image, gathered_one, rows_here // 2)
    by_column, by_tile, direction, sizes, norm = call(
        update_body,
        [vmem] * 2 + [hbm] * 3,
        [vmem] * 5,
        [column_shape, tile_shape, vector_shape, small_shape, small_shape],
        spread_scratch,
        tile_cost,
        "update_spread",
    )(everyone, image, shelf, footprint, token)
    gathered_two = lax.all_gather(by_tile, "tm", axis=0, tiled=True)
    flux_one, token = call(
        flux_first_body,
        [vmem, hbm, hbm, hbm],
        [hbm, vmem],
        [field_shape, token_shape],
        flux_scratch + [pltpu.VMEM((rows_here // 2, columns), f32), flags(2)],
        flux_cost,
        "flux_first",
    )(sizes, product_one, parts, gathered_one)

    own_image, image = collect(prior(by_column, token))
    flux_two, _ = flux_product(own_image, gathered_two, rows_here)

    answer, flux = call(
        last_body,
        [smem] + [vmem] * 5 + [hbm] * 2,
        [vmem, hbm],
        [shape_of(right_sides.shape, f32), flux_shape],
        [field, field, pltpu.VMEM(flux_shape.shape, f32), flags(4), flags(4), flags(steps_here)],
        cost(1 << 20, 6 << 20),
        "last",
    )(me, everyone, image, direction, sizes, norm, flux_one, flux_two)
    return (answer, flux)


def local(right_sides, obs_var, footprint, tile_block, tile_place, *covariances):
    devices = lax.axis_size("tm")
    tiles = tile_block.size
    fits = devices * tiles <= 2048 and devices % 4 == 0 and tiles == 128
    fits = fits and right_sides.shape[0] == 2 and (SAMPLES * LON) % (32 * devices) == 0
    fits = fits and (covariances[0].shape[0] // devices) % 4 == 0
    plan = by_columns if fits else by_gather
    return plan(right_sides, obs_var, footprint, tile_block, tile_place, *covariances)


def solution(mesh):
    in_specs = (
        P(("grp", "tm"), None, None),
        P(("grp", "tm"), None),
        P(("grp", "tm"), None, None, None),
        P(("grp", "tm"), None),
        P(("grp", "tm"), None),
        P(),
        P(),
        P(),
    )
    out_specs = (P(("grp", "tm"), None, None), P(("grp", "tm"), None, None, None))
    return jax.shard_map(local, mesh=mesh, in_specs=in_specs, out_specs=out_specs, check_vma=False)
```

```python
import functools

import jax
import jax.numpy as jnp
from jax import lax
from jax.experimental import pallas as pl
from jax.experimental.pallas import tpu as pltpu
from jax.sharding import PartitionSpec as P

LAT = 128
LON = 128
BLOCK_OBS = 128
SAMPLES = 4
ITERS = 2


precise = lax.Precision.HIGHEST


def solve_spd(matrix, target):
    factor = jnp.linalg.cholesky(matrix)
    halfway = lax.linalg.triangular_solve(factor, target, left_side=True, lower=True)
    return lax.linalg.triangular_solve(
        factor, halfway, left_side=True, lower=True, transpose_a=True
    )


def combine(vectors, weights):
    return jnp.einsum("nks,kj->njs", vectors, weights, precision=precise)


def gram(left, right):
    return jnp.einsum("nks,njs->kj", left, right, precision=precise)


def to_all(array):
    devices = lax.axis_size("tm")
    copies = jnp.broadcast_to(array[None], (devices,) + array.shape)
    return lax.all_to_all(copies, "tm", split_axis=0, concat_axis=0, tiled=True)


def by_gather(
    right_sides, obs_var, footprint, tile_block, tile_place, time_cov, lat_cov, lon_cov
):
    devices = lax.axis_size("tm")
    me = lax.axis_index("tm")
    owned = right_sides.shape[0]
    blocks = devices * owned
    steps_here = time_cov.shape[0] // devices
    slots = tile_block.shape[1]
    tiles = devices * slots
    rows_here = steps_here * LAT
    owner_base = (jnp.arange(devices, dtype=jnp.int32) * owned)[:, None]
    requests = owner_base + tile_block

    packed = jnp.concatenate(
        [
            right_sides.reshape(-1, 128),
            obs_var.reshape(-1, 128),
            tile_place.astype(jnp.float32).reshape(-1, 128),
        ]
    )
    everyone = to_all(packed)
    at = owned * SAMPLES
    rhs = everyone[:, :at].reshape(blocks, SAMPLES, BLOCK_OBS)
    variance = everyone[:, at : at + owned].reshape(blocks, BLOCK_OBS)
    places = everyone[:, at + owned :].reshape(devices, tiles).astype(jnp.int32)
    times = (places // LAT + steps_here * jnp.arange(devices, dtype=jnp.int32)[:, None]).reshape(-1)
    rows = (places % LAT).reshape(-1)
    time_hot = (jnp.arange(time_cov.shape[0])[:, None] == times[None, :]).astype(jnp.float32)
    row_hot = (jnp.arange(LAT)[:, None] == rows[None, :]).astype(jnp.float32)
    my_times = lax.dynamic_slice_in_dim(time_cov, me * steps_here, steps_here, 0)
    time_part = jnp.dot(my_times, time_hot, precision=precise)
    row_part = jnp.dot(lat_cov, row_hot, precision=precise)
    dense = (time_part[:, None, :] * row_part[None, :, :]).astype(jnp.bfloat16)
    dense = dense.reshape(rows_here, devices * tiles)
    mine = jnp.take(dense, tile_place.reshape(-1), axis=0)

    def spread(vectors):
        chosen = jnp.take(vectors.astype(jnp.bfloat16), requests, axis=0)
        contrib = jnp.einsum(
            "ocks,ocsl->ockl", chosen, footprint, preferred_element_type=jnp.float32
        )
        contrib = contrib.astype(jnp.bfloat16).reshape(tiles, SAMPLES * LON)
        return lax.all_gather(contrib, "tm", axis=0, tiled=True)

    def collect(gathered):
        field = jnp.dot(mine, gathered, preferred_element_type=jnp.float32)
        field = jnp.dot(field.reshape(-1, LON), lon_cov, precision=precise)
        picked = field.astype(jnp.bfloat16).reshape(devices, slots, SAMPLES, LON)
        partial = jnp.einsum(
            "ockl,ocsl->ocks", picked, footprint, preferred_element_type=jnp.float32
        )
        block_range = jnp.arange(owned, dtype=jnp.int32)
        selector = (tile_block[:, :, None] == block_range).astype(jnp.float32)
        summed = jnp.einsum("ocb,ocks->obks", selector, partial, precision=precise)
        terms = lax.all_to_all(
            summed.reshape(devices, owned * SAMPLES, BLOCK_OBS), "tm", 0, 0, tiled=True
        )
        return to_all(terms.sum(0)).reshape(blocks, SAMPLES, BLOCK_OBS)

    solution = jnp.zeros_like(rhs)
    residual = rhs
    direction = rhs
    norm_now = gram(rhs, rhs)
    gathers, sizes = [], []
    for step in range(ITERS):
        gathered = spread(direction)
        image = collect(gathered) + variance[:, None, :] * direction
        step_size = solve_spd(gram(direction, image), norm_now)
        gathers.append(gathered)
        sizes.append(step_size)
        solution = solution + combine(direction, step_size)
        if step + 1 == ITERS:
            break
        residual = residual - combine(image, step_size)
        norm_next = gram(residual, residual)
        mix_ratio = solve_spd(norm_now, norm_next)
        direction = residual + combine(direction, mix_ratio)
        norm_now = norm_next

    def mix(gathered, size):
        whole = gathered.astype(jnp.float32).reshape(-1, SAMPLES, LON)
        return jnp.einsum("tkl,kj->tjl", whole, size, precision=precise)

    def apply_dense(gathered):
        return jnp.dot(dense, gathered, preferred_element_type=jnp.float32)

    if rows_here < devices * tiles // 4:
        flux = sum(mix(apply_dense(g), size) for g, size in zip(gathers, sizes))
    else:
        total = sum(mix(g, size) for g, size in zip(gathers, sizes))
        flux = apply_dense(total.astype(jnp.bfloat16).reshape(-1, SAMPLES * LON))
    flux = jnp.dot(flux.reshape(-1, LON), lon_cov, precision=precise)
    mine_now = lax.dynamic_slice_in_dim(solution, me * owned, owned, 0)
    return (mine_now, flux.reshape(steps_here, LAT, SAMPLES, LON))


def rolled(x, shift):
    return x if shift == 0 else pltpu.roll(x, 8 - 2 * shift, x.ndim - 2)


def row_gram(left, right):
    entry = [[None] * SAMPLES for _ in range(SAMPLES)]
    for shift in range(SAMPLES):
        product = jnp.sum(left * rolled(right, shift), axis=0)
        total = jnp.broadcast_to(jnp.sum(product, axis=1, keepdims=True), product.shape)
        for k in range(SAMPLES):
            pair = total[2 * k : 2 * k + 1] + total[2 * k + 1 : 2 * k + 2]
            entry[k][(k + shift) % SAMPLES] = pair
    return entry


def row_solve(matrix, target):
    size = range(SAMPLES)
    sym = [[0.5 * (matrix[i][j] + matrix[j][i]) for j in size] for i in size]
    low = [[None] * SAMPLES for _ in size]
    scaled = [[None] * SAMPLES for _ in size]
    inverse = []
    for j in size:
        pivot = sym[j][j]
        for p in range(j):
            pivot = pivot - low[j][p] * scaled[j][p]
        inverse.append(1.0 / pivot)
        for i in range(j + 1, SAMPLES):
            value = sym[i][j]
            for p in range(j):
                value = value - scaled[i][p] * low[j][p]
            scaled[i][j] = value
            low[i][j] = value * inverse[j]
    out = [[None] * SAMPLES for _ in size]
    for c in size:
        part = []
        for i in size:
            value = target[i][c]
            for p in range(i):
                value = value - low[i][p] * part[p]
            part.append(value)
        for i in reversed(size):
            value = part[i] * inverse[i]
            for p in range(i + 1, SAMPLES):
                value = value - low[p][i] * out[p][c]
            out[i][c] = value
    return out


def row_weights(weights):
    sample = lax.broadcasted_iota(jnp.int32, (8, 128), 0) // 2
    result = []
    for shift in range(SAMPLES):
        rows = jnp.broadcast_to(weights[shift][0], (8, 128))
        for j in range(1, SAMPLES):
            rows = jnp.where(sample == j, weights[(j + shift) % SAMPLES][j], rows)
        result.append(rows)
    return result


def row_combine(x, per_shift):
    total = 0.0
    for shift in range(SAMPLES):
        total = total + rolled(x, shift) * per_shift[shift]
    return total


PIECES = 8


def fetch(source, held, arrived):
    pieces = arrived.shape[0]
    size = source.shape[0] // pieces
    copies = []
    for p in range(pieces):
        at = pl.ds(p * size, size)
        copies.append(pltpu.make_async_copy(source.at[at], held.at[at], arrived.at[p]))
    for copy in copies:
        copy.start()
    return copies


def second_of(tile_block):
    slots, owners = tile_block.shape
    tiles = owners * slots
    tile = lax.broadcasted_iota(jnp.int32, (tiles, slots), 0)
    slot = lax.broadcasted_iota(jnp.int32, (tiles, slots), 1)
    rows = jnp.dot(
        (tile % slots == slot).astype(jnp.float32),
        tile_block[...].astype(jnp.float32),
        preferred_element_type=jnp.float32,
    )
    tile = lax.broadcasted_iota(jnp.int32, (tiles, owners), 0)
    owner = lax.broadcasted_iota(jnp.int32, (tiles, owners), 1)
    return jnp.sum(jnp.where(tile // slots == owner, rows, 0.0), axis=1, keepdims=True)


def pack_body(right_sides, obs_var, tile_place, tile_block, lon, copies, mask, shelf, pair, sent):
    slots, owners = tile_place.shape
    tiles = owners * slots
    owner = lax.broadcasted_iota(jnp.int32, (owners, tiles), 0)
    lane = lax.broadcasted_iota(jnp.int32, (owners, tiles), 1)
    spread_out = jnp.dot(
        tile_place[...].astype(jnp.float32),
        (lane // slots == owner).astype(jnp.float32),
        precision=precise,
        preferred_element_type=jnp.float32,
    )
    slot = lax.broadcasted_iota(jnp.int32, (slots, tiles), 0)
    lane = lax.broadcasted_iota(jnp.int32, (slots, tiles), 1)
    place = jnp.sum(jnp.where(lane % slots == slot, spread_out, 0.0), axis=0, keepdims=True)
    for k in range(SAMPLES):
        for b in range(2):
            copies[0, 2 * k + b : 2 * k + b + 1] = right_sides[b, k : k + 1]
    copies[0, 8:10] = obs_var[...]
    copies[0, 10:11] = place
    copies[0, 11:16] = jnp.zeros((5, tiles), jnp.float32)
    for d in range(1, copies.shape[0]):
        copies[d] = copies[0]
    second = jnp.broadcast_to(second_of(tile_block), lon.shape)
    mask[...] = second
    pair[0] = second
    pair[1] = lon[...]
    shelve = pltpu.make_async_copy(pair, shelf.at[0:2], sent)
    shelve.start()
    shelve.wait()


def spread_tiles(vectors, held, copies, products, split):
    owners, slots = held.shape[:2]
    piece = owners // len(copies)
    for owner in range(owners):
        if owner % piece == 0:
            copies[owner // piece].wait()
        rows = vectors[owner, 0:8]
        lhs = rows.astype(jnp.bfloat16)
        if split:
            upper = lhs.astype(jnp.float32)
            lhs = jnp.concatenate([upper, rows - upper], axis=0).astype(jnp.bfloat16)
        for c in range(slots):
            r = jnp.dot(lhs, held[owner, c], preferred_element_type=jnp.float32)
            products[owner * slots + c] = r[:8] + r[8:] if split else r


def spread_end(products, mask_lon, by_column, by_tile):
    second = mask_lon[0] > 0.5
    width = by_column.shape[1]
    chunks = LON // width
    for k in range(SAMPLES):
        chosen = jnp.where(second, products[:, 2 * k + 1, :], products[:, 2 * k, :])
        mixed = jnp.dot(
            chosen, mask_lon[1], precision=precise, preferred_element_type=jnp.float32
        )
        by_tile[:, k * LON : (k + 1) * LON] = mixed.astype(jnp.bfloat16)
        turned = mixed.T.astype(jnp.bfloat16)
        by_column[k * chunks : (k + 1) * chunks] = turned.reshape(chunks, width, LON)


def first_body(
    everyone, shelf, footprint,
    by_column, by_tile, products, held, arrived, mask_lon, shelf_arrived,
):
    shelf_copy = pltpu.make_async_copy(shelf.at[0:2], mask_lon, shelf_arrived)
    shelf_copy.start()
    copies = fetch(footprint, held, arrived)
    spread_tiles(everyone, held, copies, products, False)
    shelf_copy.wait()
    spread_end(products, mask_lon, by_column, by_tile)


def with_variance(image, everyone, vectors):
    block = lax.broadcasted_iota(jnp.int32, vectors.shape, 1) % 2
    variance = jnp.where(block == 0, everyone[:, 8:9, :], everyone[:, 9:10, :])
    return image + variance * vectors


def entries(ref):
    grid = range(SAMPLES)
    return [[ref[SAMPLES * k + j : SAMPLES * k + j + 1] for j in grid] for k in grid]


def keep(ref, matrix):
    for k in range(SAMPLES):
        for j in range(SAMPLES):
            ref[SAMPLES * k + j : SAMPLES * k + j + 1] = matrix[k][j]


def update_body(
    everyone, image_in, shelf, footprint, after,
    by_column, by_tile, direction, sizes, norm,
    products, held, arrived, mask_lon, shelf_arrived,
):
    del after
    shelf_copy = pltpu.make_async_copy(shelf.at[0:2], mask_lon, shelf_arrived)
    shelf_copy.start()
    copies = fetch(footprint, held, arrived)
    first = everyone[:, 0:8, :]
    image = with_variance(image_in[...], everyone, first)
    norm_now = row_gram(first, first)
    step_size = row_solve(row_gram(first, image), norm_now)
    residual = first - row_combine(image, row_weights(step_size))
    norm_next = row_gram(residual, residual)
    ratio = row_solve(norm_now, norm_next)
    direction[...] = residual + row_combine(first, row_weights(ratio))
    keep(sizes, step_size)
    keep(norm, norm_next)
    spread_tiles(direction, held, copies, products, True)
    shelf_copy.wait()
    spread_end(products, mask_lon, by_column, by_tile)


def build_body(
    me, everyone, time_cov, lat_cov,
    prior_out, parts_out, tile_prior, hot, cols, times, parts, sent, parts_sent,
):
    devices, tiles = everyone.shape[0], everyone.shape[2]
    steps_here = parts.shape[0] - LAT
    at = lax.broadcasted_iota(jnp.int32, (LAT, tiles), 0)
    for kind, cov in ((0, time_cov), (1, lat_cov)):
        whole_cov = cov[...]
        upper = whole_cov.astype(jnp.bfloat16)
        lower = (whole_cov - upper.astype(jnp.float32)).astype(jnp.bfloat16)
        ones = []
        for d in range(devices):
            place = (everyone[d, 10:11, :] + 0.5).astype(jnp.int32)
            where = place // LAT + steps_here * d if kind == 0 else place % LAT
            one = (at == where).astype(jnp.float32)
            ones.append(one.astype(jnp.bfloat16))
            turned = one.T.astype(jnp.bfloat16)
            here = slice(d * tiles, (d + 1) * tiles)
            hot[kind, here, 0:LAT] = turned
            hot[kind, here, LAT : 2 * LAT] = turned
        picked = jnp.dot(
            jnp.concatenate([upper, lower], axis=0),
            jnp.concatenate(ones, axis=1),
            preferred_element_type=jnp.float32,
        )
        cols[kind] = picked.astype(jnp.bfloat16)
        both = picked[:LAT] + picked[LAT:]
        if kind == 0:
            times[...] = both
            mine = pl.ds(pl.multiple_of(me[0] * steps_here, steps_here), steps_here)
            parts[LAT:] = times[mine, :]
        else:
            parts[:LAT] = both

    parts_copy = pltpu.make_async_copy(parts, parts_out, parts_sent)
    parts_copy.start()
    rows = tile_prior.shape[0] // PIECES

    def sending(piece):
        block = pl.ds(pl.multiple_of(piece * rows, rows), rows)
        return pltpu.make_async_copy(
            tile_prior.at[block], prior_out.at[block], sent.at[piece]
        )

    @pl.loop(0, PIECES)
    def _(piece):
        block = pl.ds(pl.multiple_of(piece * rows, rows), rows)
        by_time = jnp.dot(hot[0, block, :], cols[0], preferred_element_type=jnp.float32)
        by_row = jnp.dot(hot[1, block, :], cols[1], preferred_element_type=jnp.float32)
        tile_prior[block, :] = (by_time * by_row).astype(jnp.bfloat16)
        sending(piece).start()

    parts_copy.wait()
    for piece in range(PIECES):
        sending(piece).wait()


def mix_body(columns, tile_prior, *rest):
    mixed, total, held, arrived = rest[-4:]
    copies = fetch(tile_prior, held, arrived)
    devices, width, tiles = columns.shape
    part = devices // len(copies)
    for p, copy in enumerate(copies):
        at = range(p * part, (p + 1) * part)
        lhs = jnp.concatenate([columns[d] for d in at], axis=1)
        copy.wait()
        product = jnp.dot(
            lhs,
            held[p * part * tiles : (p + 1) * part * tiles],
            preferred_element_type=jnp.float32,
        )
        total[...] = product if p == 0 else total[...] + product
    for d in range(devices):
        mixed[d] = total[:, d * tiles : (d + 1) * tiles].astype(jnp.bfloat16)


def sum_body(terms, total, copies):
    value = jnp.sum(terms[...], axis=0)
    total[...] = value
    for d in range(copies.shape[0]):
        copies[d] = value


def collect_body(values, mask, footprint, sums, rows):
    chunks = values.shape[0] // SAMPLES
    owners, slots = footprint.shape[:2]
    is_second = mask[...] > 0.5
    for k in range(SAMPLES):
        turned = values[k * chunks : (k + 1) * chunks].reshape(LON, -1)
        turned = turned.astype(jnp.float32).T
        rows[:, 2 * k, :] = jnp.where(is_second, 0.0, turned)
        rows[:, 2 * k + 1, :] = jnp.where(is_second, turned, 0.0)
    for owner in range(owners):
        total = 0.0
        for c in range(slots):
            total = total + lax.dot_general(
                rows[owner * slots + c].astype(jnp.bfloat16),
                footprint[owner, c],
                (((1,), (1,)), ((), ())),
                preferred_element_type=jnp.float32,
            )
        sums[owner] = total


def dense_rows(parts, first):
    rows = []
    for t in range(first, first + 2):
        rows.append((parts[LAT + t : LAT + t + 1, :] * parts[:LAT]).astype(jnp.bfloat16))
    return jnp.concatenate(rows, axis=0)


def send_rows(ready, out, sent, step, value):
    at = pl.ds(step * LAT, 2 * LAT)
    ready[at] = value
    copy = pltpu.make_async_copy(ready.at[at], out.at[at], sent.at[step // 2])
    copy.start()
    return copy


def halved_product(dense, held, copies):
    half = held.shape[0] // 2
    total = 0.0
    for h in range(2):
        for copy in copies[h * PIECES // 2 : (h + 1) * PIECES // 2]:
            copy.wait()
        at = slice(h * half, (h + 1) * half)
        total = total + jnp.dot(dense[:, at], held[at], preferred_element_type=jnp.float32)
    return total


def mixed_samples(value, size):
    pieces = [value[:, k * LON : (k + 1) * LON] for k in range(SAMPLES)]
    mixed = []
    for j in range(SAMPLES):
        mixed.append(sum(pieces[k] * size[k][j] for k in range(SAMPLES)))
    return jnp.concatenate(mixed, axis=1)


def flux_product_body(
    rows, after, parts, gathered, out, token,
    ready, parts_held, held, parts_arrived, arrived, sent,
):
    del after
    (parts_copy,) = fetch(parts, parts_held, parts_arrived)
    copies = fetch(gathered, held, arrived)
    parts_copy.wait()
    sending = []
    for step in range(0, rows // LAT, 2):
        dense = dense_rows(parts_held, step)
        if step == 0:
            value = halved_product(dense, held, copies)
            token[...] = value[0:8, 0:128]
        else:
            value = jnp.dot(dense, held[...], preferred_element_type=jnp.float32)
        sending.append(send_rows(ready, out, sent, step, value))
    for copy in sending:
        copy.wait()


def flux_first_body(
    sizes, product, parts, gathered, out, token,
    ready, parts_held, held, parts_arrived, arrived, sent, product_held, product_arrived,
):
    done = product_held.shape[0] // LAT
    product_copies = fetch(product.at[: done * LAT], product_held, product_arrived)
    (parts_copy,) = fetch(parts, parts_held, parts_arrived)
    copies = fetch(gathered, held, arrived)
    size = entries(sizes)
    sending = []
    for copy in product_copies:
        copy.wait()
    for step in range(0, done, 2):
        value = product_held[step * LAT : (step + 2) * LAT]
        sending.append(send_rows(ready, out, sent, step, mixed_samples(value, size)))
    parts_copy.wait()
    for step in range(done, out.shape[0] // LAT, 2):
        dense = dense_rows(parts_held, step)
        if step == done:
            value = halved_product(dense, held, copies)
        else:
            value = jnp.dot(dense, held[...], preferred_element_type=jnp.float32)
        value = mixed_samples(value, size)
        sending.append(send_rows(ready, out, sent, step, value))
    token[...] = size[0][0] + jnp.zeros(token.shape, jnp.float32)
    for copy in sending:
        copy.wait()


def last_body(
    me, everyone, image_in, direction, sizes, norm, flux_one, flux_two,
    answer, flux, one, two, ready, one_arrived, two_arrived, sent,
):
    two_copies = fetch(flux_two, two, two_arrived)
    one_copies = fetch(flux_one, one, one_arrived)
    second = direction[...]
    image = with_variance(image_in[...], everyone, second)
    size_two = row_solve(row_gram(second, image), entries(norm))
    own = row_combine(everyone[me[0], 0:8, :], row_weights(entries(sizes)))
    own = own + row_combine(direction[me[0]], row_weights(size_two))
    for k in range(SAMPLES):
        for b in range(2):
            answer[b, k : k + 1, :] = own[2 * k + b : 2 * k + b + 1]

    steps = ready.shape[0]
    piece = steps // len(one_copies)
    sending = []
    for t in range(steps):
        if t % piece == 0:
            two_copies[t // piece].wait()
            one_copies[t // piece].wait()
        at = slice(t * LAT, (t + 1) * LAT)
        parts = [two[at, k * LON : (k + 1) * LON] for k in range(SAMPLES)]
        for j in range(SAMPLES):
            value = one[at, j * LON : (j + 1) * LON]
            for k in range(SAMPLES):
                value = value + parts[k] * size_two[k][j]
            ready[t, :, j, :] = value
        copy = pltpu.make_async_copy(ready.at[t], flux.at[t], sent.at[t])
        copy.start()
        sending.append(copy)
    for copy in sending:
        copy.wait()


MIB = 1024 * 1024


def shape_of(shape, dtype):
    return jax.ShapeDtypeStruct(shape, dtype)


def cost(flops, moved):
    return pl.CostEstimate(flops=flops, bytes_accessed=moved, transcendentals=0)


def by_columns(
    right_sides, obs_var, footprint, tile_block, tile_place, time_cov, lat_cov, lon_cov
):
    devices = lax.axis_size("tm")
    me = lax.axis_index("tm").reshape(1).astype(jnp.int32)
    steps_here = time_cov.shape[0] // devices
    tiles = tile_block.size
    every_tile = devices * tiles
    columns = SAMPLES * LON
    width = columns // devices
    rows_here = steps_here * LAT
    f32, bf16 = jnp.float32, jnp.bfloat16

    vmem = pl.BlockSpec(memory_space=pltpu.VMEM)
    smem = pl.BlockSpec(memory_space=pltpu.SMEM)
    hbm = pl.BlockSpec(memory_space=pltpu.HBM)
    vector_shape = shape_of((devices, 8, BLOCK_OBS), f32)
    column_shape = shape_of((devices, width, tiles), bf16)
    tile_shape = shape_of((tiles, columns), bf16)
    small_shape = shape_of((SAMPLES * SAMPLES, 128), f32)
    field_shape = shape_of((rows_here, columns), f32)
    parts_shape = shape_of((LAT + steps_here, every_tile), f32)
    token_shape = shape_of((8, 128), f32)
    prior_shape = shape_of((every_tile, every_tile), bf16)
    flux_shape = shape_of((steps_here, LAT, SAMPLES, LON), f32)

    def flags(count):
        return pltpu.SemaphoreType.DMA((count,))

    products = pltpu.VMEM((tiles, 8, LON), f32)
    field = pltpu.VMEM(field_shape.shape, f32)
    gathered_held = pltpu.VMEM((every_tile, columns), bf16)
    prior_held = pltpu.VMEM(prior_shape.shape, bf16)
    spread_scratch = [products, pltpu.VMEM(footprint.shape, bf16), flags(4)]
    spread_scratch += [pltpu.VMEM((2, 128, 128), f32), pltpu.SemaphoreType.DMA]
    flux_scratch = [field, pltpu.VMEM(parts_shape.shape, f32), gathered_held]
    flux_scratch += [flags(1), flags(PIECES), flags(steps_here // 2)]
    tile_cost = cost(2 * 8 * footprint.size, footprint.size * 2)
    flux_cost = cost(2 * rows_here * every_tile * columns, every_tile * columns * 2)

    def call(body, in_specs, out_specs, out_shape, scratch, estimate, name, grant=53):
        return pl.pallas_call(
            body,
            in_specs=in_specs,
            out_specs=out_specs,
            out_shape=out_shape,
            scratch_shapes=scratch,
            compiler_params=pltpu.CompilerParams(vmem_limit_bytes=grant * MIB),
            cost_estimate=estimate,
            name=name,
        )

    def exchange(array):
        return lax.all_to_all(array, "tm", split_axis=0, concat_axis=0, tiled=True)

    pair_scratch = [pltpu.VMEM((2, 128, 128), f32), pltpu.SemaphoreType.DMA]
    packed, mask, shelf = call(
        pack_body,
        [vmem] * 5,
        [vmem, vmem, hbm],
        [
            shape_of((devices, 16, 128), f32),
            shape_of((128, 128), f32),
            shape_of((64, 128, 128), f32),
        ],
        pair_scratch,
        cost(0, 12 * MIB),
        "pack",
        59,
    )(right_sides, obs_var, tile_place.T, tile_block.T, lon_cov)
    everyone = exchange(packed)
    by_column, by_tile = call(
        first_body,
        [vmem, hbm, hbm],
        [vmem] * 2,
        [column_shape, tile_shape],
        spread_scratch,
        tile_cost,
        "spread_first",
    )(everyone, shelf, footprint)
    gathered_one = lax.all_gather(by_tile, "tm", axis=0, tiled=True)

    tile_prior, parts = call(
        build_body,
        [smem] + [vmem] * 3,
        [hbm, hbm],
        [prior_shape, parts_shape],
        [
            prior_held,
            pltpu.VMEM((2, every_tile, 2 * LAT), bf16),
            pltpu.VMEM((2, 2 * LAT, every_tile), bf16),
            pltpu.VMEM((LAT, every_tile), f32),
            pltpu.VMEM(parts_shape.shape, f32),
            flags(PIECES),
            pltpu.SemaphoreType.DMA,
        ],
        cost(4 * every_tile * every_tile * 256, every_tile * every_tile * 2),
        "build_prior",
    )(me, everyone, time_cov, lat_cov)

    def flux_product(after, gathered, rows):
        return call(
            functools.partial(flux_product_body, rows),
            [hbm, hbm, hbm],
            [hbm, vmem],
            [field_shape, token_shape],
            flux_scratch,
            flux_cost,
            "flux_product",
        )(after, parts, gathered)

    def prior(by_column, *after):
        mixed = call(
            mix_body,
            [vmem, hbm] + [hbm] * len(after),
            vmem,
            column_shape,
            [pltpu.VMEM((width, every_tile), f32), prior_held, flags(PIECES)],
            cost(2 * width * every_tile**2, every_tile**2 * 2),
            "mix_columns",
        )(exchange(by_column), tile_prior, *after)
        return exchange(mixed)

    def collect(values):
        sums = call(
            collect_body, [vmem] * 3, vmem, vector_shape, [products], tile_cost, "collect", 48
        )(values, mask, footprint)
        own, copies = call(
            sum_body,
            [vmem],
            [vmem] * 2,
            [shape_of((8, BLOCK_OBS), f32), vector_shape],
            [],
            cost(0, 4 * MIB),
            "sum_terms",
        )(exchange(sums))
        return own, exchange(copies)

    own_image, image = collect(prior(by_column))
    product_one, token = flux_product(own_image, gathered_one, rows_here // 2)
    by_column, by_tile, direction, sizes, norm = call(
        update_body,
        [vmem] * 2 + [hbm] * 3,
        [vmem] * 5,
        [column_shape, tile_shape, vector_shape, small_shape, small_shape],
        spread_scratch,
        tile_cost,
        "update_spread",
    )(everyone, image, shelf, footprint, token)
    gathered_two = lax.all_gather(by_tile, "tm", axis=0, tiled=True)
    flux_one, token = call(
        flux_first_body,
        [vmem, hbm, hbm, hbm],
        [hbm, vmem],
        [field_shape, token_shape],
        flux_scratch + [pltpu.VMEM((rows_here // 2, columns), f32), flags(2)],
        flux_cost,
        "flux_first",
    )(sizes, product_one, parts, gathered_one)

    own_image, image = collect(prior(by_column, token))
    flux_two, _ = flux_product(own_image, gathered_two, rows_here)

    answer, flux = call(
        last_body,
        [smem] + [vmem] * 5 + [hbm] * 2,
        [vmem, hbm],
        [shape_of(right_sides.shape, f32), flux_shape],
        [field, field, pltpu.VMEM(flux_shape.shape, f32), flags(4), flags(4), flags(steps_here)],
        cost(1 << 20, 6 << 20),
        "last",
    )(me, everyone, image, direction, sizes, norm, flux_one, flux_two)
    return (answer, flux)


def local(right_sides, obs_var, footprint, tile_block, tile_place, *covariances):
    devices = lax.axis_size("tm")
    tiles = tile_block.size
    fits = devices * tiles <= 2048 and devices % 4 == 0 and tiles == 128
    fits = fits and right_sides.shape[0] == 2 and (SAMPLES * LON) % (32 * devices) == 0
    fits = fits and (covariances[0].shape[0] // devices) % 4 == 0
    plan = by_columns if fits else by_gather
    return plan(right_sides, obs_var, footprint, tile_block, tile_place, *covariances)


def solution(mesh):
    in_specs = (
        P(("grp", "tm"), None, None),
        P(("grp", "tm"), None),
        P(("grp", "tm"), None, None, None),
        P(("grp", "tm"), None),
        P(("grp", "tm"), None),
        P(),
        P(),
        P(),
    )
    out_specs = (P(("grp", "tm"), None, None), P(("grp", "tm"), None, None, None))
    return jax.shard_map(local, mesh=mesh, in_specs=in_specs, out_specs=out_specs, check_vma=False)
```

```python
import functools

import jax
import jax.numpy as jnp
from jax import lax
from jax.experimental import pallas as pl
from jax.experimental.pallas import tpu as pltpu
from jax.sharding import PartitionSpec as P

LAT = 128
LON = 128
BLOCK_OBS = 128
SAMPLES = 4
ITERS = 2


precise = lax.Precision.HIGHEST


def solve_spd(matrix, target):
    factor = jnp.linalg.cholesky(matrix)
    halfway = lax.linalg.triangular_solve(factor, target, left_side=True, lower=True)
    return lax.linalg.triangular_solve(
        factor, halfway, left_side=True, lower=True, transpose_a=True
    )


def combine(vectors, weights):
    return jnp.einsum("nks,kj->njs", vectors, weights, precision=precise)


def gram(left, right):
    return jnp.einsum("nks,njs->kj", left, right, precision=precise)


def to_all(array):
    devices = lax.axis_size("tm")
    copies = jnp.broadcast_to(array[None], (devices,) + array.shape)
    return lax.all_to_all(copies, "tm", split_axis=0, concat_axis=0, tiled=True)


def by_gather(
    right_sides, obs_var, footprint, tile_block, tile_place, time_cov, lat_cov, lon_cov
):
    devices = lax.axis_size("tm")
    me = lax.axis_index("tm")
    owned = right_sides.shape[0]
    blocks = devices * owned
    steps_here = time_cov.shape[0] // devices
    slots = tile_block.shape[1]
    tiles = devices * slots
    rows_here = steps_here * LAT
    owner_base = (jnp.arange(devices, dtype=jnp.int32) * owned)[:, None]
    requests = owner_base + tile_block

    packed = jnp.concatenate(
        [
            right_sides.reshape(-1, 128),
            obs_var.reshape(-1, 128),
            tile_place.astype(jnp.float32).reshape(-1, 128),
        ]
    )
    everyone = to_all(packed)
    at = owned * SAMPLES
    rhs = everyone[:, :at].reshape(blocks, SAMPLES, BLOCK_OBS)
    variance = everyone[:, at : at + owned].reshape(blocks, BLOCK_OBS)
    places = everyone[:, at + owned :].reshape(devices, tiles).astype(jnp.int32)
    times = (places // LAT + steps_here * jnp.arange(devices, dtype=jnp.int32)[:, None]).reshape(-1)
    rows = (places % LAT).reshape(-1)
    time_hot = (jnp.arange(time_cov.shape[0])[:, None] == times[None, :]).astype(jnp.float32)
    row_hot = (jnp.arange(LAT)[:, None] == rows[None, :]).astype(jnp.float32)
    my_times = lax.dynamic_slice_in_dim(time_cov, me * steps_here, steps_here, 0)
    time_part = jnp.dot(my_times, time_hot, precision=precise)
    row_part = jnp.dot(lat_cov, row_hot, precision=precise)
    dense = (time_part[:, None, :] * row_part[None, :, :]).astype(jnp.bfloat16)
    dense = dense.reshape(rows_here, devices * tiles)
    mine = jnp.take(dense, tile_place.reshape(-1), axis=0)

    def spread(vectors):
        chosen = jnp.take(vectors.astype(jnp.bfloat16), requests, axis=0)
        contrib = jnp.einsum(
            "ocks,ocsl->ockl", chosen, footprint, preferred_element_type=jnp.float32
        )
        contrib = contrib.astype(jnp.bfloat16).reshape(tiles, SAMPLES * LON)
        return lax.all_gather(contrib, "tm", axis=0, tiled=True)

    def collect(gathered):
        field = jnp.dot(mine, gathered, preferred_element_type=jnp.float32)
        field = jnp.dot(field.reshape(-1, LON), lon_cov, precision=precise)
        picked = field.astype(jnp.bfloat16).reshape(devices, slots, SAMPLES, LON)
        partial = jnp.einsum(
            "ockl,ocsl->ocks", picked, footprint, preferred_element_type=jnp.float32
        )
        block_range = jnp.arange(owned, dtype=jnp.int32)
        selector = (tile_block[:, :, None] == block_range).astype(jnp.float32)
        summed = jnp.einsum("ocb,ocks->obks", selector, partial, precision=precise)
        terms = lax.all_to_all(
            summed.reshape(devices, owned * SAMPLES, BLOCK_OBS), "tm", 0, 0, tiled=True
        )
        return to_all(terms.sum(0)).reshape(blocks, SAMPLES, BLOCK_OBS)

    solution = jnp.zeros_like(rhs)
    residual = rhs
    direction = rhs
    norm_now = gram(rhs, rhs)
    gathers, sizes = [], []
    for step in range(ITERS):
        gathered = spread(direction)
        image = collect(gathered) + variance[:, None, :] * direction
        step_size = solve_spd(gram(direction, image), norm_now)
        gathers.append(gathered)
        sizes.append(step_size)
        solution = solution + combine(direction, step_size)
        if step + 1 == ITERS:
            break
        residual = residual - combine(image, step_size)
        norm_next = gram(residual, residual)
        mix_ratio = solve_spd(norm_now, norm_next)
        direction = residual + combine(direction, mix_ratio)
        norm_now = norm_next

    def mix(gathered, size):
        whole = gathered.astype(jnp.float32).reshape(-1, SAMPLES, LON)
        return jnp.einsum("tkl,kj->tjl", whole, size, precision=precise)

    def apply_dense(gathered):
        return jnp.dot(dense, gathered, preferred_element_type=jnp.float32)

    if rows_here < devices * tiles // 4:
        flux = sum(mix(apply_dense(g), size) for g, size in zip(gathers, sizes))
    else:
        total = sum(mix(g, size) for g, size in zip(gathers, sizes))
        flux = apply_dense(total.astype(jnp.bfloat16).reshape(-1, SAMPLES * LON))
    flux = jnp.dot(flux.reshape(-1, LON), lon_cov, precision=precise)
    mine_now = lax.dynamic_slice_in_dim(solution, me * owned, owned, 0)
    return (mine_now, flux.reshape(steps_here, LAT, SAMPLES, LON))


def rolled(x, shift):
    return x if shift == 0 else pltpu.roll(x, 8 - 2 * shift, x.ndim - 2)


def row_gram(left, right):
    entry = [[None] * SAMPLES for _ in range(SAMPLES)]
    for shift in range(SAMPLES):
        product = jnp.sum(left * rolled(right, shift), axis=0)
        total = jnp.broadcast_to(jnp.sum(product, axis=1, keepdims=True), product.shape)
        for k in range(SAMPLES):
            pair = total[2 * k : 2 * k + 1] + total[2 * k + 1 : 2 * k + 2]
            entry[k][(k + shift) % SAMPLES] = pair
    return entry


def row_solve(matrix, target):
    size = range(SAMPLES)
    sym = [[0.5 * (matrix[i][j] + matrix[j][i]) for j in size] for i in size]
    low = [[None] * SAMPLES for _ in size]
    scaled = [[None] * SAMPLES for _ in size]
    inverse = []
    for j in size:
        pivot = sym[j][j]
        for p in range(j):
            pivot = pivot - low[j][p] * scaled[j][p]
        inverse.append(1.0 / pivot)
        for i in range(j + 1, SAMPLES):
            value = sym[i][j]
            for p in range(j):
                value = value - scaled[i][p] * low[j][p]
            scaled[i][j] = value
            low[i][j] = value * inverse[j]
    out = [[None] * SAMPLES for _ in size]
    for c in size:
        part = []
        for i in size:
            value = target[i][c]
            for p in range(i):
                value = value - low[i][p] * part[p]
            part.append(value)
        for i in reversed(size):
            value = part[i] * inverse[i]
            for p in range(i + 1, SAMPLES):
                value = value - low[p][i] * out[p][c]
            out[i][c] = value
    return out


def row_weights(weights):
    sample = lax.broadcasted_iota(jnp.int32, (8, 128), 0) // 2
    result = []
    for shift in range(SAMPLES):
        rows = jnp.broadcast_to(weights[shift][0], (8, 128))
        for j in range(1, SAMPLES):
            rows = jnp.where(sample == j, weights[(j + shift) % SAMPLES][j], rows)
        result.append(rows)
    return result


def row_combine(x, per_shift):
    total = 0.0
    for shift in range(SAMPLES):
        total = total + rolled(x, shift) * per_shift[shift]
    return total


PIECES = 8


def fetch(source, held, arrived):
    pieces = arrived.shape[0]
    size = source.shape[0] // pieces
    copies = []
    for p in range(pieces):
        at = pl.ds(p * size, size)
        copies.append(pltpu.make_async_copy(source.at[at], held.at[at], arrived.at[p]))
    for copy in copies:
        copy.start()
    return copies


def second_of(tile_block):
    slots, owners = tile_block.shape
    tiles = owners * slots
    tile = lax.broadcasted_iota(jnp.int32, (tiles, slots), 0)
    slot = lax.broadcasted_iota(jnp.int32, (tiles, slots), 1)
    rows = jnp.dot(
        (tile % slots == slot).astype(jnp.float32),
        tile_block[...].astype(jnp.float32),
        preferred_element_type=jnp.float32,
    )
    tile = lax.broadcasted_iota(jnp.int32, (tiles, owners), 0)
    owner = lax.broadcasted_iota(jnp.int32, (tiles, owners), 1)
    return jnp.sum(jnp.where(tile // slots == owner, rows, 0.0), axis=1, keepdims=True)


def pack_body(right_sides, obs_var, tile_place, tile_block, lon, copies, mask, shelf, pair, sent):
    slots, owners = tile_place.shape
    tiles = owners * slots
    owner = lax.broadcasted_iota(jnp.int32, (owners, tiles), 0)
    lane = lax.broadcasted_iota(jnp.int32, (owners, tiles), 1)
    spread_out = jnp.dot(
        tile_place[...].astype(jnp.float32),
        (lane // slots == owner).astype(jnp.float32),
        precision=precise,
        preferred_element_type=jnp.float32,
    )
    slot = lax.broadcasted_iota(jnp.int32, (slots, tiles), 0)
    lane = lax.broadcasted_iota(jnp.int32, (slots, tiles), 1)
    place = jnp.sum(jnp.where(lane % slots == slot, spread_out, 0.0), axis=0, keepdims=True)
    for k in range(SAMPLES):
        for b in range(2):
            copies[0, 2 * k + b : 2 * k + b + 1] = right_sides[b, k : k + 1]
    copies[0, 8:10] = obs_var[...]
    copies[0, 10:11] = place
    copies[0, 11:16] = jnp.zeros((5, tiles), jnp.float32)
    for d in range(1, copies.shape[0]):
        copies[d] = copies[0]
    second = jnp.broadcast_to(second_of(tile_block), lon.shape)
    mask[...] = second
    pair[0] = second
    pair[1] = lon[...]
    shelve = pltpu.make_async_copy(pair, shelf.at[0:2], sent)
    shelve.start()
    shelve.wait()


def spread_tiles(vectors, held, copies, products, split):
    owners, slots = held.shape[:2]
    piece = owners // len(copies)
    for owner in range(owners):
        if owner % piece == 0:
            copies[owner // piece].wait()
        rows = vectors[owner, 0:8]
        lhs = rows.astype(jnp.bfloat16)
        if split:
            upper = lhs.astype(jnp.float32)
            lhs = jnp.concatenate([upper, rows - upper], axis=0).astype(jnp.bfloat16)
        for c in range(slots):
            r = jnp.dot(lhs, held[owner, c], preferred_element_type=jnp.float32)
            products[owner * slots + c] = r[:8] + r[8:] if split else r


def halves(x):
    upper = x.astype(jnp.bfloat16)
    return upper, (x - upper.astype(jnp.float32)).astype(jnp.bfloat16)


def spread_end(products, mask_lon, by_column, by_tile):
    second = mask_lon[0] > 0.5
    upper, lower = halves(mask_lon[1])
    lon = jnp.concatenate([upper, upper, lower], axis=0)
    width = by_column.shape[1]
    chunks = LON // width
    for k in range(SAMPLES):
        chosen = jnp.where(second, products[:, 2 * k + 1, :], products[:, 2 * k, :])
        upper, lower = halves(chosen)
        mixed = jnp.dot(
            jnp.concatenate([upper, lower, upper], axis=1),
            lon,
            preferred_element_type=jnp.float32,
        )
        by_tile[:, k * LON : (k + 1) * LON] = mixed.astype(jnp.bfloat16)
        turned = mixed.T.astype(jnp.bfloat16)
        by_column[k * chunks : (k + 1) * chunks] = turned.reshape(chunks, width, LON)


def first_body(
    everyone, shelf, footprint,
    by_column, by_tile, products, held, arrived, mask_lon, shelf_arrived,
):
    shelf_copy = pltpu.make_async_copy(shelf.at[0:2], mask_lon, shelf_arrived)
    shelf_copy.start()
    copies = fetch(footprint, held, arrived)
    spread_tiles(everyone, held, copies, products, False)
    shelf_copy.wait()
    spread_end(products, mask_lon, by_column, by_tile)


def with_variance(image, everyone, vectors):
    block = lax.broadcasted_iota(jnp.int32, vectors.shape, 1) % 2
    variance = jnp.where(block == 0, everyone[:, 8:9, :], everyone[:, 9:10, :])
    return image + variance * vectors


def entries(ref):
    grid = range(SAMPLES)
    return [[ref[SAMPLES * k + j : SAMPLES * k + j + 1] for j in grid] for k in grid]


def keep(ref, matrix):
    for k in range(SAMPLES):
        for j in range(SAMPLES):
            ref[SAMPLES * k + j : SAMPLES * k + j + 1] = matrix[k][j]


def update_body(
    everyone, image_in, shelf, footprint, after,
    by_column, by_tile, direction, sizes, norm,
    products, held, arrived, mask_lon, shelf_arrived,
):
    del after
    shelf_copy = pltpu.make_async_copy(shelf.at[0:2], mask_lon, shelf_arrived)
    shelf_copy.start()
    copies = fetch(footprint, held, arrived)
    first = everyone[:, 0:8, :]
    image = with_variance(image_in[...], everyone, first)
    norm_now = row_gram(first, first)
    step_size = row_solve(row_gram(first, image), norm_now)
    residual = first - row_combine(image, row_weights(step_size))
    norm_next = row_gram(residual, residual)
    ratio = row_solve(norm_now, norm_next)
    direction[...] = residual + row_combine(first, row_weights(ratio))
    keep(sizes, step_size)
    keep(norm, norm_next)
    spread_tiles(direction, held, copies, products, True)
    shelf_copy.wait()
    spread_end(products, mask_lon, by_column, by_tile)


def build_body(
    me, everyone, time_cov, lat_cov,
    prior_out, parts_out, tile_prior, hot, cols, times, parts, sent, parts_sent,
):
    devices, tiles = everyone.shape[0], everyone.shape[2]
    steps_here = parts.shape[0] - LAT
    at = lax.broadcasted_iota(jnp.int32, (LAT, tiles), 0)
    for kind, cov in ((0, time_cov), (1, lat_cov)):
        whole_cov = cov[...]
        upper = whole_cov.astype(jnp.bfloat16)
        lower = (whole_cov - upper.astype(jnp.float32)).astype(jnp.bfloat16)
        ones = []
        for d in range(devices):
            place = (everyone[d, 10:11, :] + 0.5).astype(jnp.int32)
            where = place // LAT + steps_here * d if kind == 0 else place % LAT
            one = (at == where).astype(jnp.float32)
            ones.append(one.astype(jnp.bfloat16))
            turned = one.T.astype(jnp.bfloat16)
            here = slice(d * tiles, (d + 1) * tiles)
            hot[kind, here, 0:LAT] = turned
            hot[kind, here, LAT : 2 * LAT] = turned
        picked = jnp.dot(
            jnp.concatenate([upper, lower], axis=0),
            jnp.concatenate(ones, axis=1),
            preferred_element_type=jnp.float32,
        )
        cols[kind] = picked.astype(jnp.bfloat16)
        both = picked[:LAT] + picked[LAT:]
        if kind == 0:
            times[...] = both
            mine = pl.ds(pl.multiple_of(me[0] * steps_here, steps_here), steps_here)
            parts[LAT:] = times[mine, :]
        else:
            parts[:LAT] = both

    parts_copy = pltpu.make_async_copy(parts, parts_out, parts_sent)
    parts_copy.start()
    rows = tile_prior.shape[0] // PIECES

    def sending(piece):
        block = pl.ds(pl.multiple_of(piece * rows, rows), rows)
        return pltpu.make_async_copy(
            tile_prior.at[block], prior_out.at[block], sent.at[piece]
        )

    @pl.loop(0, PIECES)
    def _(piece):
        block = pl.ds(pl.multiple_of(piece * rows, rows), rows)
        by_time = jnp.dot(hot[0, block, :], cols[0], preferred_element_type=jnp.float32)
        by_row = jnp.dot(hot[1, block, :], cols[1], preferred_element_type=jnp.float32)
        tile_prior[block, :] = (by_time * by_row).astype(jnp.bfloat16)
        sending(piece).start()

    parts_copy.wait()
    for piece in range(PIECES):
        sending(piece).wait()


def mix_body(columns, tile_prior, *rest):
    mixed, total, held, arrived = rest[-4:]
    copies = fetch(tile_prior, held, arrived)
    devices, width, tiles = columns.shape
    part = devices // len(copies)
    for p, copy in enumerate(copies):
        at = range(p * part, (p + 1) * part)
        lhs = jnp.concatenate([columns[d] for d in at], axis=1)
        copy.wait()
        product = jnp.dot(
            lhs,
            held[p * part * tiles : (p + 1) * part * tiles],
            preferred_element_type=jnp.float32,
        )
        total[...] = product if p == 0 else total[...] + product
    for d in range(devices):
        mixed[d] = total[:, d * tiles : (d + 1) * tiles].astype(jnp.bfloat16)


def sum_body(terms, total, copies):
    value = jnp.sum(terms[...], axis=0)
    total[...] = value
    for d in range(copies.shape[0]):
        copies[d] = value


def collect_body(values, mask, footprint, sums, rows):
    chunks = values.shape[0] // SAMPLES
    owners, slots = footprint.shape[:2]
    is_second = mask[...] > 0.5
    for k in range(SAMPLES):
        turned = values[k * chunks : (k + 1) * chunks].reshape(LON, -1)
        turned = turned.astype(jnp.float32).T
        rows[:, 2 * k, :] = jnp.where(is_second, 0.0, turned)
        rows[:, 2 * k + 1, :] = jnp.where(is_second, turned, 0.0)
    for owner in range(owners):
        total = 0.0
        for c in range(slots):
            total = total + lax.dot_general(
                rows[owner * slots + c].astype(jnp.bfloat16),
                footprint[owner, c],
                (((1,), (1,)), ((), ())),
                preferred_element_type=jnp.float32,
            )
        sums[owner] = total


def dense_rows(parts, first):
    rows = []
    for t in range(first, first + 2):
        rows.append((parts[LAT + t : LAT + t + 1, :] * parts[:LAT]).astype(jnp.bfloat16))
    return jnp.concatenate(rows, axis=0)


def send_rows(ready, out, sent, step, value):
    at = pl.ds(step * LAT, 2 * LAT)
    ready[at] = value
    copy = pltpu.make_async_copy(ready.at[at], out.at[at], sent.at[step // 2])
    copy.start()
    return copy


def halved_product(dense, held, copies):
    half = held.shape[0] // 2
    total = 0.0
    for h in range(2):
        for copy in copies[h * PIECES // 2 : (h + 1) * PIECES // 2]:
            copy.wait()
        at = slice(h * half, (h + 1) * half)
        total = total + jnp.dot(dense[:, at], held[at], preferred_element_type=jnp.float32)
    return total


def mixed_samples(value, size):
    pieces = [value[:, k * LON : (k + 1) * LON] for k in range(SAMPLES)]
    mixed = []
    for j in range(SAMPLES):
        mixed.append(sum(pieces[k] * size[k][j] for k in range(SAMPLES)))
    return jnp.concatenate(mixed, axis=1)


def flux_product_body(
    rows, after, parts, gathered, out, token,
    ready, parts_held, held, parts_arrived, arrived, sent,
):
    del after
    (parts_copy,) = fetch(parts, parts_held, parts_arrived)
    copies = fetch(gathered, held, arrived)
    parts_copy.wait()
    sending = []
    for step in range(0, rows // LAT, 2):
        dense = dense_rows(parts_held, step)
        if step == 0:
            value = halved_product(dense, held, copies)
            token[...] = value[0:8, 0:128]
        else:
            value = jnp.dot(dense, held[...], preferred_element_type=jnp.float32)
        sending.append(send_rows(ready, out, sent, step, value))
    for copy in sending:
        copy.wait()


def flux_first_body(
    sizes, product, parts, gathered, out, token,
    ready, parts_held, held, parts_arrived, arrived, sent, product_held, product_arrived,
):
    done = product_held.shape[0] // LAT
    product_copies = fetch(product.at[: done * LAT], product_held, product_arrived)
    (parts_copy,) = fetch(parts, parts_held, parts_arrived)
    copies = fetch(gathered, held, arrived)
    size = entries(sizes)
    sending = []
    for copy in product_copies:
        copy.wait()
    for step in range(0, done, 2):
        value = product_held[step * LAT : (step + 2) * LAT]
        sending.append(send_rows(ready, out, sent, step, mixed_samples(value, size)))
    parts_copy.wait()
    for step in range(done, out.shape[0] // LAT, 2):
        dense = dense_rows(parts_held, step)
        if step == done:
            value = halved_product(dense, held, copies)
        else:
            value = jnp.dot(dense, held[...], preferred_element_type=jnp.float32)
        value = mixed_samples(value, size)
        sending.append(send_rows(ready, out, sent, step, value))
    token[...] = size[0][0] + jnp.zeros(token.shape, jnp.float32)
    for copy in sending:
        copy.wait()


def last_body(
    me, everyone, image_in, direction, sizes, norm, flux_one, flux_two,
    answer, flux, one, two, ready, one_arrived, two_arrived, sent,
):
    two_copies = fetch(flux_two, two, two_arrived)
    one_copies = fetch(flux_one, one, one_arrived)
    second = direction[...]
    image = with_variance(image_in[...], everyone, second)
    size_two = row_solve(row_gram(second, image), entries(norm))
    own = row_combine(everyone[me[0], 0:8, :], row_weights(entries(sizes)))
    own = own + row_combine(direction[me[0]], row_weights(size_two))
    for k in range(SAMPLES):
        for b in range(2):
            answer[b, k : k + 1, :] = own[2 * k + b : 2 * k + b + 1]

    steps = ready.shape[0]
    piece = steps // len(one_copies)
    sending = []
    for t in range(steps):
        if t % piece == 0:
            two_copies[t // piece].wait()
            one_copies[t // piece].wait()
        at = slice(t * LAT, (t + 1) * LAT)
        parts = [two[at, k * LON : (k + 1) * LON] for k in range(SAMPLES)]
        for j in range(SAMPLES):
            value = one[at, j * LON : (j + 1) * LON]
            for k in range(SAMPLES):
                value = value + parts[k] * size_two[k][j]
            ready[t, :, j, :] = value
        copy = pltpu.make_async_copy(ready.at[t], flux.at[t], sent.at[t])
        copy.start()
        sending.append(copy)
    for copy in sending:
        copy.wait()


MIB = 1024 * 1024


def shape_of(shape, dtype):
    return jax.ShapeDtypeStruct(shape, dtype)


def cost(flops, moved):
    return pl.CostEstimate(flops=flops, bytes_accessed=moved, transcendentals=0)


def by_columns(
    right_sides, obs_var, footprint, tile_block, tile_place, time_cov, lat_cov, lon_cov
):
    devices = lax.axis_size("tm")
    me = lax.axis_index("tm").reshape(1).astype(jnp.int32)
    steps_here = time_cov.shape[0] // devices
    tiles = tile_block.size
    every_tile = devices * tiles
    columns = SAMPLES * LON
    width = columns // devices
    rows_here = steps_here * LAT
    f32, bf16 = jnp.float32, jnp.bfloat16

    vmem = pl.BlockSpec(memory_space=pltpu.VMEM)
    smem = pl.BlockSpec(memory_space=pltpu.SMEM)
    hbm = pl.BlockSpec(memory_space=pltpu.HBM)
    vector_shape = shape_of((devices, 8, BLOCK_OBS), f32)
    column_shape = shape_of((devices, width, tiles), bf16)
    tile_shape = shape_of((tiles, columns), bf16)
    small_shape = shape_of((SAMPLES * SAMPLES, 128), f32)
    field_shape = shape_of((rows_here, columns), f32)
    parts_shape = shape_of((LAT + steps_here, every_tile), f32)
    token_shape = shape_of((8, 128), f32)
    prior_shape = shape_of((every_tile, every_tile), bf16)
    flux_shape = shape_of((steps_here, LAT, SAMPLES, LON), f32)

    def flags(count):
        return pltpu.SemaphoreType.DMA((count,))

    products = pltpu.VMEM((tiles, 8, LON), f32)
    field = pltpu.VMEM(field_shape.shape, f32)
    gathered_held = pltpu.VMEM((every_tile, columns), bf16)
    prior_held = pltpu.VMEM(prior_shape.shape, bf16)
    spread_scratch = [products, pltpu.VMEM(footprint.shape, bf16), flags(4)]
    spread_scratch += [pltpu.VMEM((2, 128, 128), f32), pltpu.SemaphoreType.DMA]
    flux_scratch = [field, pltpu.VMEM(parts_shape.shape, f32), gathered_held]
    flux_scratch += [flags(1), flags(PIECES), flags(steps_here // 2)]
    tile_cost = cost(2 * 8 * footprint.size, footprint.size * 2)
    flux_cost = cost(2 * rows_here * every_tile * columns, every_tile * columns * 2)

    def call(body, in_specs, out_specs, out_shape, scratch, estimate, name, grant=53):
        return pl.pallas_call(
            body,
            in_specs=in_specs,
            out_specs=out_specs,
            out_shape=out_shape,
            scratch_shapes=scratch,
            compiler_params=pltpu.CompilerParams(vmem_limit_bytes=grant * MIB),
            cost_estimate=estimate,
            name=name,
        )

    def exchange(array):
        return lax.all_to_all(array, "tm", split_axis=0, concat_axis=0, tiled=True)

    pair_scratch = [pltpu.VMEM((2, 128, 128), f32), pltpu.SemaphoreType.DMA]
    packed, mask, shelf = call(
        pack_body,
        [vmem] * 5,
        [vmem, vmem, hbm],
        [
            shape_of((devices, 16, 128), f32),
            shape_of((128, 128), f32),
            shape_of((64, 128, 128), f32),
        ],
        pair_scratch,
        cost(0, 12 * MIB),
        "pack",
        59,
    )(right_sides, obs_var, tile_place.T, tile_block.T, lon_cov)
    everyone = exchange(packed)
    by_column, by_tile = call(
        first_body,
        [vmem, hbm, hbm],
        [vmem] * 2,
        [column_shape, tile_shape],
        spread_scratch,
        tile_cost,
        "spread_first",
    )(everyone, shelf, footprint)
    gathered_one = lax.all_gather(by_tile, "tm", axis=0, tiled=True)

    tile_prior, parts = call(
        build_body,
        [smem] + [vmem] * 3,
        [hbm, hbm],
        [prior_shape, parts_shape],
        [
            prior_held,
            pltpu.VMEM((2, every_tile, 2 * LAT), bf16),
            pltpu.VMEM((2, 2 * LAT, every_tile), bf16),
            pltpu.VMEM((LAT, every_tile), f32),
            pltpu.VMEM(parts_shape.shape, f32),
            flags(PIECES),
            pltpu.SemaphoreType.DMA,
        ],
        cost(4 * every_tile * every_tile * 256, every_tile * every_tile * 2),
        "build_prior",
    )(me, everyone, time_cov, lat_cov)

    def flux_product(after, gathered, rows):
        return call(
            functools.partial(flux_product_body, rows),
            [hbm, hbm, hbm],
            [hbm, vmem],
            [field_shape, token_shape],
            flux_scratch,
            flux_cost,
            "flux_product",
        )(after, parts, gathered)

    def prior(by_column, *after):
        mixed = call(
            mix_body,
            [vmem, hbm] + [hbm] * len(after),
            vmem,
            column_shape,
            [pltpu.VMEM((width, every_tile), f32), prior_held, flags(PIECES)],
            cost(2 * width * every_tile**2, every_tile**2 * 2),
            "mix_columns",
        )(exchange(by_column), tile_prior, *after)
        return exchange(mixed)

    def collect(values):
        sums = call(
            collect_body, [vmem] * 3, vmem, vector_shape, [products], tile_cost, "collect", 48
        )(values, mask, footprint)
        own, copies = call(
            sum_body,
            [vmem],
            [vmem] * 2,
            [shape_of((8, BLOCK_OBS), f32), vector_shape],
            [],
            cost(0, 4 * MIB),
            "sum_terms",
        )(exchange(sums))
        return own, exchange(copies)

    own_image, image = collect(prior(by_column))
    product_one, token = flux_product(own_image, gathered_one, rows_here // 2)
    by_column, by_tile, direction, sizes, norm = call(
        update_body,
        [vmem] * 2 + [hbm] * 3,
        [vmem] * 5,
        [column_shape, tile_shape, vector_shape, small_shape, small_shape],
        spread_scratch,
        tile_cost,
        "update_spread",
    )(everyone, image, shelf, footprint, token)
    gathered_two = lax.all_gather(by_tile, "tm", axis=0, tiled=True)
    flux_one, token = call(
        flux_first_body,
        [vmem, hbm, hbm, hbm],
        [hbm, vmem],
        [field_shape, token_shape],
        flux_scratch + [pltpu.VMEM((rows_here // 2, columns), f32), flags(2)],
        flux_cost,
        "flux_first",
    )(sizes, product_one, parts, gathered_one)

    own_image, image = collect(prior(by_column, token))
    flux_two, _ = flux_product(own_image, gathered_two, rows_here)

    answer, flux = call(
        last_body,
        [smem] + [vmem] * 5 + [hbm] * 2,
        [vmem, hbm],
        [shape_of(right_sides.shape, f32), flux_shape],
        [field, field, pltpu.VMEM(flux_shape.shape, f32), flags(4), flags(4), flags(steps_here)],
        cost(1 << 20, 6 << 20),
        "last",
    )(me, everyone, image, direction, sizes, norm, flux_one, flux_two)
    return (answer, flux)


def local(right_sides, obs_var, footprint, tile_block, tile_place, *covariances):
    devices = lax.axis_size("tm")
    tiles = tile_block.size
    fits = devices * tiles <= 2048 and devices % 4 == 0 and tiles == 128
    fits = fits and right_sides.shape[0] == 2 and (SAMPLES * LON) % (32 * devices) == 0
    fits = fits and (covariances[0].shape[0] // devices) % 4 == 0
    plan = by_columns if fits else by_gather
    return plan(right_sides, obs_var, footprint, tile_block, tile_place, *covariances)


def solution(mesh):
    in_specs = (
        P(("grp", "tm"), None, None),
        P(("grp", "tm"), None),
        P(("grp", "tm"), None, None, None),
        P(("grp", "tm"), None),
        P(("grp", "tm"), None),
        P(),
        P(),
        P(),
    )
    out_specs = (P(("grp", "tm"), None, None), P(("grp", "tm"), None, None, None))
    return jax.shard_map(local, mesh=mesh, in_specs=in_specs, out_specs=out_specs, check_vma=False)
```
